32 devices in a mesh: groups: 2 (over y), ctx: 4 (over z), head: 2 (over x), rep: 2 (over core).
Axes of the slice: x: 2, y: 2, z: 4, core: 2. Of those that a mesh axis runs over, the one named last changes fastest.
Arguments:
- queries: bfloat16 [8192, 16, 2, 128], P(('groups', 'ctx'), 'head', 'rep'), parts along dimension 0, may hold values from -10 to 10
- keys_values: bfloat16 [2, 8192, 16, 128], P('rep', ('groups', 'ctx'), 'head'), parts along dimension 1, may hold values from -6 to 6
- far_list: int32 [64, 16], P('groups'), parts along dimension 0, may hold values from 0 to 31, as said below
- far_count: int32 [64], P('groups'), parts along dimension 0, may hold values from 0 to 8
Outputs:
- attended: bfloat16 [8192, 16, 2, 128], P(('groups', 'ctx'), 'head', 'rep'), parts along dimension 0
The draws below stay inside these ranges and needn't reach their ends.
There are 2 independent parts, one for each index of `groups`. The reference program is written for one: setup_inputs(seed, part) draws one part's arguments, and reference() takes and returns one part's arrays. A program takes and returns all parts, laid end to end along the dimension named above; each array names one. Nothing has to cross between parts.
Inputs may be any that keep to these rules, and one draw needn't show every extreme that they name: `far_list`: for query block c, the entries j < far_count[c] are distinct block numbers no later than c - 4; entries from far_count[c] on are arbitrary and not read. Taken over all query blocks of one span of 1024 tokens, the counted entries name at most 2 distinct blocks of any one span, and some span's query blocks name exactly 2 of some span in every draw.
All inputs are finite; a program needn't handle non-finite values.
Results may differ from the reference program's by a relative error of at most 0.003.
Values may be sent and summed in bfloat16 or wider, within the bound.
No kernel may reach another device: no remote copies, remote signals or barrier semaphores. Data moves between devices by JAX's collectives and lax.ppermute only.
A program may use at most 128 MiB of HBM per device.

```python
import jax
import jax.numpy as jnp
from jax import lax

DH = 128
KVH = 16
GQA = 2
BLK = 128
WB = 4
FSEL = 16
CAP = 2
L_DEV = 1024
SEQ = 4096


def draw_queries(key, part):
    own_key = jax.random.fold_in(key, 23)
    drawn = jnp.clip(2.5 * jax.random.normal(own_key, (SEQ, KVH, GQA, DH), jnp.float32), -10.0, 10.0)
    return drawn.astype(jnp.bfloat16)


def draw_keys_values(key, part):
    own_key = jax.random.fold_in(key, 29)
    drawn = jnp.clip(jax.random.normal(own_key, (2, SEQ, KVH, DH), jnp.float32), -6.0, 6.0)
    return drawn.astype(jnp.bfloat16)


def far_tables(key):
    base_key = jax.random.fold_in(key, 5)
    pool_key, order_key, jitter_key, filler_key = jax.random.split(base_key, 4)
    span_blocks = L_DEV // BLK
    span_total = SEQ // L_DEV
    all_blocks = span_blocks * span_total
    local_ids = jnp.arange(span_blocks, dtype=jnp.int32)
    span_ids = jnp.arange(span_total, dtype=jnp.int32)
    raw_scores = jax.random.randint(pool_key, (span_total, span_total, span_blocks), 0, 1 << 20, dtype=jnp.int32)
    too_late = (span_ids[None, :, None] == span_ids[:, None, None]) & (local_ids[None, None, :] >= span_blocks - WB)
    pool_score = raw_scores * span_blocks + local_ids[None, None, :] + too_late.astype(jnp.int32) * (1 << 26)
    pool_order = jnp.argsort(pool_score, axis=-1)[:, :, :CAP].astype(jnp.int32)
    pool_blocks = pool_order + span_ids[None, :, None] * span_blocks
    pool_ok = jnp.broadcast_to(span_ids[None, :, None] <= span_ids[:, None, None], pool_blocks.shape)
    block_ids = jnp.arange(all_blocks, dtype=jnp.int32)
    span_of = block_ids // span_blocks
    pool_width = span_total * CAP
    candidates = pool_blocks[span_of].reshape(all_blocks, pool_width)
    eligible = pool_ok[span_of].reshape(all_blocks, pool_width) & (candidates <= block_ids[:, None] - WB)
    owner_draw = jax.random.randint(order_key, (all_blocks, span_total), 0, 1 << 20, dtype=jnp.int32) * span_total + span_ids[None, :]
    owner_rank = jnp.argsort(jnp.argsort(owner_draw, axis=1), axis=1).astype(jnp.int32)
    slot_key = (owner_rank[:, :, None] * CAP + jnp.arange(CAP, dtype=jnp.int32)[None, None, :]).reshape(all_blocks, pool_width)
    sort_key = jnp.where(eligible, slot_key, slot_key + pool_width)
    picked = jnp.argsort(sort_key, axis=1)
    listed = jnp.take_along_axis(candidates, picked, axis=1).astype(jnp.int32)
    available = jnp.sum(eligible.astype(jnp.int32), axis=1)
    jitter = jax.random.randint(jitter_key, (all_blocks,), 0, 2, dtype=jnp.int32)
    jitter = jnp.where(block_ids == all_blocks - 1, 0, jitter)
    target = FSEL * (span_of + 1) // span_total - jitter
    counts = jnp.clip(jnp.minimum(target, available), 0, FSEL).astype(jnp.int32)
    if pool_width >= FSEL:
        listed = listed[:, :FSEL]
    else:
        listed = jnp.concatenate([listed, jnp.zeros((all_blocks, FSEL - pool_width), jnp.int32)], axis=1)
    filler = jax.random.randint(filler_key, (all_blocks, FSEL), 0, all_blocks, dtype=jnp.int32)
    listed = jnp.where(jnp.arange(FSEL, dtype=jnp.int32)[None, :] < counts[:, None], listed, filler)
    return (listed, counts)


def draw_far_list(key, part):
    return far_tables(key)[0]


def draw_far_count(key, part):
    return far_tables(key)[1]


def setup_inputs(seed: int = 0, part: int = 0) -> dict:
    streams_of = jax.random.split(jax.random.key(seed), 5)
    part_splits = jax.random.split(jax.random.fold_in(streams_of[4], part), 5)
    return {
        "queries": draw_queries(jax.random.fold_in(jax.random.fold_in(streams_of[4], part), 71), part),
        "keys_values": draw_keys_values(jax.random.fold_in(jax.random.fold_in(streams_of[4], part), 71), part),
        "far_list": draw_far_list(jax.random.fold_in(jax.random.fold_in(streams_of[4], part), 71), part),
        "far_count": draw_far_count(jax.random.fold_in(jax.random.fold_in(streams_of[4], part), 71), part),
    }


floor_score = -1.0e30
score_scale = 1.0 / 12.0


def group_weights(scores, usable):
    masked = jnp.where(usable, scores, floor_score)
    summit = jnp.max(masked, axis=-1, keepdims=True)
    weights = jnp.where(usable, jnp.exp(masked - summit), 0.0)
    return summit, weights, jnp.sum(weights, axis=-1, keepdims=True)


def attend(query_tile, keys_tile, values_tile, usable):
    scores = jnp.einsum("qhgd,khd->hgqk", query_tile.astype(jnp.float32), keys_tile.astype(jnp.float32), precision=lax.Precision.HIGHEST) * score_scale
    summit, weights, weight_sum = group_weights(scores, usable)
    light_weights = lax.optimization_barrier(weights.astype(jnp.bfloat16)).astype(jnp.float32)
    mixed_out = jnp.einsum("hgqk,khd->hgqd", light_weights, values_tile.astype(jnp.float32), precision=lax.Precision.HIGHEST)
    return summit, mixed_out, weight_sum


def reference(queries, keys_values, far_list, far_count):
    all_blocks = SEQ // BLK
    query_blocks = queries.reshape(all_blocks, BLK, KVH, GQA, DH)
    key_blocks = keys_values[0].reshape(all_blocks, BLK, KVH, DH)
    value_blocks = keys_values[1].reshape(all_blocks, BLK, KVH, DH)
    inside = jnp.arange(BLK, dtype=jnp.int32)
    window_pos = (jnp.arange(WB, dtype=jnp.int32)[:, None] * BLK + inside[None, :]).reshape(-1)
    slot_range = jnp.arange(FSEL, dtype=jnp.int32)

    def one_block(block_id):
        query_tile = query_blocks[block_id]
        window_ids = block_id - WB + 1 + jnp.arange(WB, dtype=jnp.int32)
        window_ok = jnp.repeat(window_ids >= 0, BLK)
        clipped = jnp.maximum(window_ids, 0).astype(jnp.int32)
        near_keys = key_blocks[clipped].reshape(WB * BLK, KVH, DH)
        near_values = value_blocks[clipped].reshape(WB * BLK, KVH, DH)
        query_pos = (WB - 1) * BLK + inside
        near_usable = (window_pos[None, :] <= query_pos[:, None]) & window_ok[None, :]
        near_top, near_out, near_sum = attend(query_tile, near_keys, near_values, near_usable)
        picked = far_list[block_id].astype(jnp.int32)
        far_keys = key_blocks[picked].reshape(FSEL * BLK, KVH, DH)
        far_values = value_blocks[picked].reshape(FSEL * BLK, KVH, DH)
        far_usable = jnp.repeat(slot_range < far_count[block_id], BLK)[None, :]
        far_top, far_out, far_sum = attend(query_tile, far_keys, far_values, far_usable)
        summit = jnp.maximum(near_top, far_top)
        near_scale = jnp.exp(near_top - summit)
        far_scale = jnp.exp(far_top - summit)
        result = (near_scale * near_out + far_scale * far_out) / (near_scale * near_sum + far_scale * far_sum)
        return jnp.transpose(result, (2, 0, 1, 3)).astype(jnp.bfloat16)

    outputs = lax.map(one_block, jnp.arange(all_blocks, dtype=jnp.int32))
    return outputs.reshape(SEQ, KVH, GQA, DH)
```

```python
import functools
import math

import jax
import jax.numpy as jnp
from jax import lax
from jax.experimental import pallas as pl
from jax.experimental.pallas import tpu as pltpu
from jax.sharding import PartitionSpec as P

BLK = 128
WB = 4
CAP = 2
RIM = (WB - 1) * BLK
TILE = 256

FLOOR = -1.0e30
SCALE = math.log2(math.e) / 12.0
NONE = 1.0e6
VMEM_BYTES = 48 * 1024 * 1024
SMALL = pl.CostEstimate(flops=1024, bytes_accessed=1024, transcendentals=0)


def contract_last(a, b):
    return lax.dot_general(a, b, (((1,), (1,)), ((), ())), preferred_element_type=jnp.float32)


def mix(weights, values):
    return jnp.dot(weights, values, preferred_element_type=jnp.float32)


def split_order(heads):
    step = TILE // heads
    row = lax.broadcasted_iota(jnp.int32, (TILE, TILE), 0)
    col = lax.broadcasted_iota(jnp.int32, (TILE, TILE), 1)
    return (col == (row % step) * heads + row // step).astype(jnp.float32).astype(jnp.bfloat16)


def join_order(heads):
    step = TILE // heads
    row = lax.broadcasted_iota(jnp.int32, (TILE, TILE), 0)
    col = lax.broadcasted_iota(jnp.int32, (TILE, TILE), 1)
    return (col == (row % heads) * step + row // heads).astype(jnp.float32).astype(jnp.bfloat16)


def to_heads(src, tokens, order, dst, base):
    heads = dst.shape[0]
    step = TILE // heads
    for i in range(tokens // step):
        turned = mix(order, src[i * TILE : (i + 1) * TILE, :]).astype(jnp.bfloat16)
        dst[:, pl.ds(base + i * step, step), :] = turned.reshape(heads, step, turned.shape[-1])


def from_heads(src, tokens, order, dst):
    heads = src.shape[0]
    step = TILE // heads
    for i in range(tokens // step):
        rows = src[:, i * step : (i + 1) * step, :].reshape(TILE, src.shape[-1])
        dst[i * TILE : (i + 1) * TILE, :] = mix(order, rows).astype(jnp.bfloat16)


def route_kernel(me_ref, list_ref, count_ref, kv_ref, table_ref, *rest):
    spans = table_ref.shape[0] // (2 * CAP)
    pools, sem = rest[:-1], rest[-1]
    me = me_ref[0]
    listed = list_ref[...]
    entries, total = listed.shape
    own = total // spans
    slot = lax.broadcasted_iota(jnp.int32, (entries, total), 0)
    lane = lax.broadcasted_iota(jnp.int32, (entries, total), 1)
    counted = slot < count_ref[...]
    named = jnp.where(counted, listed.astype(jnp.float32), 2.0 * NONE)

    def pick(user, source):
        low = (source * own).astype(jnp.float32)
        mine = (lane >= user * own) & (lane < (user + 1) * own)
        left = jnp.where(mine & (named >= low) & (named < low + own), named, NONE)
        picked = []
        for _ in range(CAP):
            least = jnp.min(left)
            picked.append(least)
            left = jnp.where(left == least, NONE, left)
        return picked

    row_len = kv_ref.shape[0] // own
    copies = []
    for by in range(1, spans):
        for j, block in enumerate(pick(me + by, me)):
            local = jnp.clip(block - (me * own).astype(jnp.float32), 0.0, NONE)
            local = jnp.where(local < own, local, 0.0).astype(jnp.int32)
            start = pl.multiple_of(local * row_len, row_len)
            copy = pltpu.make_async_copy(
                kv_ref.at[pl.ds(start, row_len), :],
                pools[by - 1].at[pl.ds(j * row_len, row_len), :],
                sem.at[(by - 1) * CAP + j],
            )
            copy.start()
            copies.append(copy)
    for by in range(spans):
        source = me - by
        for j, block in enumerate(pick(me, source)):
            used = jnp.max((named == block).astype(jnp.float32), axis=0, keepdims=True)
            local = block - (source * own).astype(jnp.float32)
            local = jnp.where(local < own, local, 0.0)
            row = by * CAP + j
            table_ref[row : row + 1, :] = used.astype(jnp.int32)
            ids = jnp.zeros((1, total), jnp.float32) + local
            table_ref[spans * CAP + row : spans * CAP + row + 1, :] = ids.astype(jnp.int32)
    for copy in copies:
        copy.wait()


def route(me, far_list, far_count, kv, spans):
    total = far_list.shape[0]
    rows = kv.shape[0] // (total // spans) * CAP
    pool = jax.ShapeDtypeStruct((rows, kv.shape[1]), kv.dtype)
    grid_spec = pltpu.PrefetchScalarGridSpec(
        num_scalar_prefetch=1,
        grid=(1,),
        in_specs=[
            pl.BlockSpec(far_list.shape[::-1], lambda i, *_: (0, 0)),
            pl.BlockSpec((1, total), lambda i, *_: (0, 0)),
            pl.BlockSpec(memory_space=pltpu.HBM),
        ],
        out_specs=[pl.BlockSpec((2 * CAP * spans, total), lambda i, *_: (0, 0))]
        + [pl.BlockSpec(memory_space=pltpu.HBM)] * (spans - 1),
        scratch_shapes=[pltpu.SemaphoreType.DMA(((spans - 1) * CAP,))],
    )
    return pl.pallas_call(
        route_kernel,
        grid_spec=grid_spec,
        out_shape=[jax.ShapeDtypeStruct((2 * CAP * spans, total), jnp.int32)] + [pool] * (spans - 1),
        cost_estimate=SMALL,
        name="route",
    )(me, far_list.T, far_count[None, :], kv)


def first_kernel(
    spans, me_ref, table_ref, q_ref, mine_ref, other_ref, qt_ref, acc_ref, stat_ref, both_t, order, diag
):
    heads = qt_ref.shape[0]
    own = pl.num_programs(0)
    c = pl.program_id(0)

    @pl.when(c == 0)
    def _():
        order[...] = split_order(heads)
        row = lax.broadcasted_iota(jnp.int32, (BLK, BLK), 0)
        col = lax.broadcasted_iota(jnp.int32, (BLK, BLK), 1)
        diag[...] = jnp.where(col <= row, 0.0, FLOOR)

    base = pl.multiple_of(c * BLK, BLK)
    turn = order[...]
    to_heads(q_ref, BLK, turn, qt_ref, 0)
    to_heads(mine_ref, BLK, turn, both_t.at[me_ref[1]], base)
    to_heads(other_ref, BLK, turn, both_t.at[1 - me_ref[1]], base)
    kt, vt = both_t.at[0], both_t.at[1]

    @pl.when(c < WB - 1)
    def _():
        acc_ref[...] = jnp.zeros_like(acc_ref)
        lane = lax.broadcasted_iota(jnp.int32, stat_ref.shape, 1)
        stat_ref[...] = jnp.where((lane >= heads) & (lane < 2 * heads), 0.0, FLOOR)

    @pl.when(c >= WB - 1)
    def _():
        start = pl.multiple_of((c - (WB - 1)) * BLK, BLK)
        here = me_ref[0] * own + c
        shut = [jnp.where(table_ref[j, here] > 0, 0.0, FLOOR) for j in range(CAP)]
        far_at = [pl.multiple_of(table_ref[spans * CAP + j, here] * BLK, BLK) for j in range(CAP)]
        causal = diag[...]
        for h in range(heads):
            q = qt_ref[h]
            near = contract_last(q, kt[h, pl.ds(start, WB * BLK), :]) * SCALE
            near = jnp.concatenate([near[:, : RIM], near[:, RIM:] + causal], axis=1)
            top = jnp.max(near, axis=1, keepdims=True)
            w = jnp.exp2(near - top)
            total = jnp.sum(w, axis=1, keepdims=True)
            part = mix(w.astype(jnp.bfloat16), vt[h, pl.ds(start, WB * BLK), :])
            far = jnp.concatenate(
                [contract_last(q, kt[h, pl.ds(far_at[j], BLK), :]) * SCALE + shut[j] for j in range(CAP)],
                axis=1,
            )
            far_v = jnp.concatenate([vt[h, pl.ds(far_at[j], BLK), :] for j in range(CAP)], axis=0)
            far_top = jnp.max(far, axis=1, keepdims=True)
            far_w = jnp.exp2(far - far_top)
            far_total = jnp.sum(far_w, axis=1, keepdims=True)
            far_part = mix(far_w.astype(jnp.bfloat16), far_v)
            both = jnp.maximum(top, far_top)
            a = jnp.exp2(top - both)
            b = jnp.exp2(far_top - both)
            acc_ref[h] = part * a + far_part * b
            stat_ref[:, h : h + 1] = both
            stat_ref[:, heads + h : heads + h + 1] = total * a + far_total * b
            stat_ref[:, 2 * heads + h : 2 * heads + h + 1] = far_top


def first(me, table, q, mine, other, heads, spans):
    tokens = q.shape[0] // heads
    width = q.shape[1]
    own = tokens // BLK
    raw = pl.BlockSpec((BLK * heads, width), lambda c, *_: (c, 0))
    grid_spec = pltpu.PrefetchScalarGridSpec(
        num_scalar_prefetch=2,
        grid=(own,),
        in_specs=[raw, raw, raw],
        out_specs=[
            pl.BlockSpec((heads, BLK, width), lambda c, *_: (0, c, 0)),
            pl.BlockSpec((heads, BLK, width), lambda c, *_: (0, c, 0)),
            pl.BlockSpec((BLK, 128), lambda c, *_: (c, 0)),
        ],
        scratch_shapes=[
            pltpu.VMEM((2, heads, tokens, width), jnp.bfloat16),
            pltpu.VMEM((TILE, TILE), jnp.bfloat16),
            pltpu.VMEM((BLK, BLK), jnp.float32),
        ],
    )
    return pl.pallas_call(
        functools.partial(first_kernel, spans),
        grid_spec=grid_spec,
        out_shape=[
            jax.ShapeDtypeStruct((heads, tokens, width), jnp.bfloat16),
            jax.ShapeDtypeStruct((heads, tokens, width), jnp.float32),
            jax.ShapeDtypeStruct((tokens, 128), jnp.float32),
        ],
        compiler_params=pltpu.CompilerParams(vmem_limit_bytes=VMEM_BYTES),
        cost_estimate=SMALL,
        name="first",
    )(me, table, q, mine, other)


def far_kernel(by, own, last, me_ref, table_ref, q_ref, mine_ref, other_ref, acc_in, stat_in, *rest):
    if last:
        acc_ref, stat_ref, out_ref, both_t, order, bias, done = rest
    else:
        acc_ref, stat_ref, both_t, order, bias = rest
    heads = q_ref.shape[0]
    rows = q_ref.shape[1]
    i = pl.program_id(0)

    @pl.when(i == 0)
    def _():
        turn = split_order(heads)
        to_heads(mine_ref, CAP * BLK, turn, both_t.at[me_ref[1]], 0)
        to_heads(other_ref, CAP * BLK, turn, both_t.at[1 - me_ref[1]], 0)
        if last:
            order[...] = join_order(heads)

    kt, vt = both_t.at[0], both_t.at[1]
    here = me_ref[0] * own + i * (rows // BLK)
    for a in range(rows // BLK):
        for j in range(CAP):
            shut = jnp.where(table_ref[by * CAP + j, here + a] > 0, 0.0, FLOOR)
            bias[a * BLK : (a + 1) * BLK, j * BLK : (j + 1) * BLK] = jnp.zeros((BLK, BLK), jnp.float32) + shut
    for h in range(heads):
        far = contract_last(q_ref[h], kt[h]) * SCALE + bias[...]
        top = stat_in[:, h : h + 1]
        total = stat_in[:, heads + h : heads + h + 1]
        far_top = stat_in[:, 2 * heads + h : 2 * heads + h + 1]
        far_top = jnp.maximum(far_top, jnp.max(far, axis=1, keepdims=True))
        both = jnp.maximum(top, far_top)
        w = jnp.exp2(far - far_top)
        a = jnp.exp2(top - both)
        b = jnp.exp2(far_top - both)
        total = total * a + jnp.sum(w, axis=1, keepdims=True) * b
        part = acc_in[h] * a + mix(w.astype(jnp.bfloat16), vt[h]) * b
        acc_ref[h] = part
        stat_ref[:, h : h + 1] = both
        stat_ref[:, heads + h : heads + h + 1] = total
        stat_ref[:, 2 * heads + h : 2 * heads + h + 1] = far_top
        if last:
            done[h] = (part / total).astype(jnp.bfloat16)
    if last:
        from_heads(done, rows, order[...], out_ref)


def far(by, me, table, qt, mine, other, acc, stat, last):
    heads, tokens, width = qt.shape
    rows = min(TILE, tokens)
    split = pl.BlockSpec((heads, rows, width), lambda i, *_: (0, i, 0))
    stats = pl.BlockSpec((rows, 128), lambda i, *_: (i, 0))
    whole = pl.BlockSpec(mine.shape, lambda i, *_: (0, 0))
    out_specs = [split, stats]
    out_shape = [
        jax.ShapeDtypeStruct(acc.shape, acc.dtype),
        jax.ShapeDtypeStruct(stat.shape, stat.dtype),
    ]
    scratch = [
        pltpu.VMEM((2, heads, CAP * BLK, width), jnp.bfloat16),
        pltpu.VMEM((TILE, TILE), jnp.bfloat16),
        pltpu.VMEM((rows, CAP * BLK), jnp.float32),
    ]
    if last:
        out_specs.append(pl.BlockSpec((rows * heads, width), lambda i, *_: (i, 0)))
        out_shape.append(jax.ShapeDtypeStruct((tokens * heads, width), jnp.bfloat16))
        scratch.append(pltpu.VMEM((heads, rows, width), jnp.bfloat16))
    grid_spec = pltpu.PrefetchScalarGridSpec(
        num_scalar_prefetch=2,
        grid=(tokens // rows,),
        in_specs=[split, whole, whole, split, stats],
        out_specs=out_specs,
        scratch_shapes=scratch,
    )
    return pl.pallas_call(
        functools.partial(far_kernel, by, tokens // BLK, last),
        grid_spec=grid_spec,
        out_shape=out_shape,
        input_output_aliases={5: 0, 6: 1},
        compiler_params=pltpu.CompilerParams(vmem_limit_bytes=VMEM_BYTES),
        cost_estimate=SMALL,
        name=f"far{by}",
    )(me, table, qt, mine, other, acc, stat)


def rim_kernel(
    me_ref, q_ref, rim_mine, rim_other, mine_ref, other_ref, acc_in, stat_in, out_in, out_ref, both_t, order, diag, done
):
    heads = q_ref.shape[0]
    c = pl.program_id(0)

    @pl.when(c == 0)
    def _():
        turn = split_order(heads)
        mine_t, other_t = both_t.at[me_ref[1]], both_t.at[1 - me_ref[1]]
        to_heads(rim_mine, RIM, turn, mine_t, 0)
        to_heads(rim_other, RIM, turn, other_t, 0)
        to_heads(mine_ref, RIM, turn, mine_t, RIM)
        to_heads(other_ref, RIM, turn, other_t, RIM)
        order[...] = join_order(heads)
        row = lax.broadcasted_iota(jnp.int32, (BLK, BLK), 0)
        col = lax.broadcasted_iota(jnp.int32, (BLK, BLK), 1)
        diag[...] = jnp.where(col <= row, 0.0, FLOOR)

    kt, vt = both_t.at[0], both_t.at[1]
    start = pl.multiple_of(c * BLK, BLK)
    col = lax.broadcasted_iota(jnp.int32, (1, RIM), 1)
    shut = jnp.where((col + c * BLK >= RIM) | (me_ref[0] > 0), 0.0, FLOOR)
    causal = diag[...]
    for h in range(heads):
        near = contract_last(q_ref[h], kt[h, pl.ds(start, WB * BLK), :]) * SCALE
        near = jnp.concatenate([near[:, :RIM] + shut, near[:, RIM:] + causal], axis=1)
        near_top = jnp.max(near, axis=1, keepdims=True)
        top = stat_in[:, h : h + 1]
        total = stat_in[:, heads + h : heads + h + 1]
        both = jnp.maximum(top, near_top)
        w = jnp.exp2(near - near_top)
        a = jnp.exp2(top - both)
        b = jnp.exp2(near_top - both)
        total = total * a + jnp.sum(w, axis=1, keepdims=True) * b
        part = acc_in[h] * a + mix(w.astype(jnp.bfloat16), vt[h, pl.ds(start, WB * BLK), :]) * b
        done[h] = (part / total).astype(jnp.bfloat16)
    from_heads(done, BLK, order[...], out_ref)


def rim(me, qt, rim_mine, rim_other, mine, other, acc, stat, out):
    heads, tokens, width = qt.shape
    split = pl.BlockSpec((heads, BLK, width), lambda i, *_: (0, i, 0))
    stats = pl.BlockSpec((BLK, 128), lambda i, *_: (i, 0))
    edge = pl.BlockSpec((RIM * heads, width), lambda i, *_: (0, 0))
    grid_spec = pltpu.PrefetchScalarGridSpec(
        num_scalar_prefetch=1,
        grid=(WB - 1,),
        in_specs=[split, edge, edge, edge, edge, split, stats, pl.BlockSpec(memory_space=pl.ANY)],
        out_specs=pl.BlockSpec((BLK * heads, width), lambda i, *_: (i, 0)),
        scratch_shapes=[
            pltpu.VMEM((2, heads, 2 * RIM, width), jnp.bfloat16),
            pltpu.VMEM((TILE, TILE), jnp.bfloat16),
            pltpu.VMEM((BLK, BLK), jnp.float32),
            pltpu.VMEM((heads, BLK, width), jnp.bfloat16),
        ],
    )
    return pl.pallas_call(
        rim_kernel,
        grid_spec=grid_spec,
        out_shape=jax.ShapeDtypeStruct(out.shape, out.dtype),
        input_output_aliases={8: 0},
        compiler_params=pltpu.CompilerParams(vmem_limit_bytes=VMEM_BYTES),
        cost_estimate=SMALL,
        name="rim",
    )(me, qt, rim_mine, rim_other, mine, other, acc, stat, out)


def other_core(x):
    return lax.ppermute(x, "rep", [(0, 1), (1, 0)])


def ahead(x, by):
    count = lax.axis_size("ctx")
    return lax.ppermute(x, "ctx", [(i, i + by) for i in range(count - by)])


def local(queries, keys_values, far_list, far_count):
    tokens, heads, _, width = queries.shape
    spans = lax.axis_size("ctx")
    me = jnp.stack([lax.axis_index("ctx"), lax.axis_index("rep")]).astype(jnp.int32)
    q = queries.reshape(tokens * heads, width)
    kv = keys_values.reshape(tokens * heads, width)
    rim_mine = ahead(kv[(tokens - RIM) * heads :], 1)
    other = other_core(kv)
    table, *pools = route(me, far_list, far_count, kv, spans)
    arrived = [ahead(pool, by) for by, pool in enumerate(pools, 1)]
    qt, acc, stat = first(me, table, q, kv, other, heads, spans)
    rim_mine, stat = lax.optimization_barrier((rim_mine, stat))
    rim_other = other_core(rim_mine)
    for by in range(spans - 1, 0, -1):
        piece, stat = lax.optimization_barrier((arrived[by - 1], stat))
        acc, stat, *out = far(by, me, table, qt, piece, other_core(piece), acc, stat, by == 1)
    done = rim(me, qt, rim_mine, rim_other, kv, other, acc, stat, out[0])
    return done.reshape(queries.shape)


def solution(mesh):
    in_specs = (
        P(("groups", "ctx"), "head", "rep", None),
        P("rep", ("groups", "ctx"), "head", None),
        P("groups", None),
        P("groups"),
    )
    out_specs = P(("groups", "ctx"), "head", "rep", None)
    return jax.shard_map(local, mesh=mesh, in_specs=in_specs, out_specs=out_specs, check_vma=False)
```

```python
import functools
import math

import jax
import jax.numpy as jnp
from jax import lax
from jax.experimental import pallas as pl
from jax.experimental.pallas import tpu as pltpu
from jax.sharding import PartitionSpec as P

BLK = 128
WB = 4
CAP = 2
RIM = (WB - 1) * BLK
TILE = 256

FLOOR = -1.0e30
SCALE = math.log2(math.e) / 12.0
NONE = 1.0e6
VMEM_BYTES = 48 * 1024 * 1024
SMALL = pl.CostEstimate(flops=1024, bytes_accessed=1024, transcendentals=0)


def contract_last(a, b):
    return lax.dot_general(a, b, (((1,), (1,)), ((), ())), preferred_element_type=jnp.float32)


def mix(a, b):
    return jnp.dot(a, b, preferred_element_type=jnp.float32)


def unit(n):
    row = lax.broadcasted_iota(jnp.int32, (n, n), 0)
    col = lax.broadcasted_iota(jnp.int32, (n, n), 1)
    return (row == col).astype(jnp.float32).astype(jnp.bfloat16)


def causal_bias():
    key = lax.broadcasted_iota(jnp.int32, (BLK, BLK), 0)
    query = lax.broadcasted_iota(jnp.int32, (BLK, BLK), 1)
    return jnp.where(key <= query, 0.0, FLOOR)


def softmax_blocks(scores, shut, top=None):
    for block, closed in zip(scores, shut):
        block_top = jnp.max(block, axis=0, keepdims=True) * SCALE
        block_top = block_top if closed is None else block_top + closed
        top = block_top if top is None else jnp.maximum(top, block_top)
    weights, total = [], 0.0
    for block, closed in zip(scores, shut):
        base = top if closed is None else jnp.where(closed < 0.0, -FLOOR, top)
        w = jnp.exp2(block * SCALE - base)
        total = total + jnp.sum(w, axis=0, keepdims=True)
        weights.append(w.astype(jnp.bfloat16))
    return top, jnp.concatenate(weights, axis=0), total


def near_scores(keys, query, causal):
    scores = contract_last(keys, query)
    blocks = [scores[b * BLK : (b + 1) * BLK, :] for b in range(WB)]
    return blocks[:-1] + [blocks[-1] + causal]


def split_order(heads):
    step = TILE // heads
    row = lax.broadcasted_iota(jnp.int32, (TILE, TILE), 0)
    col = lax.broadcasted_iota(jnp.int32, (TILE, TILE), 1)
    return (col == (row % step) * heads + row // step).astype(jnp.float32).astype(jnp.bfloat16)


def join_order(heads):
    step = TILE // heads
    row = lax.broadcasted_iota(jnp.int32, (TILE, TILE), 0)
    col = lax.broadcasted_iota(jnp.int32, (TILE, TILE), 1)
    return (col == (row % heads) * step + row // heads).astype(jnp.float32).astype(jnp.bfloat16)


def to_heads(src, tokens, order, dst, base):
    heads = dst.shape[0]
    step = TILE // heads
    for i in range(tokens // step):
        turned = mix(order, src[i * TILE : (i + 1) * TILE, :]).astype(jnp.bfloat16)
        dst[:, pl.ds(base + i * step, step), :] = turned.reshape(heads, step, turned.shape[-1])


def from_heads(src, tokens, order, dst):
    heads = src.shape[0]
    step = TILE // heads
    for i in range(tokens // step):
        rows = src[:, i * step : (i + 1) * step, :].reshape(TILE, src.shape[-1])
        dst[i * TILE : (i + 1) * TILE, :] = mix(order, rows).astype(jnp.bfloat16)


def route_kernel(me_ref, list_ref, count_ref, kv_ref, table_ref, *rest):
    spans = table_ref.shape[0] // (2 * CAP)
    pools, sem = rest[:-1], rest[-1]
    me = me_ref[0]
    listed = list_ref[...]
    entries, total = listed.shape
    own = total // spans
    slot = lax.broadcasted_iota(jnp.int32, (entries, total), 0)
    lane = lax.broadcasted_iota(jnp.int32, (entries, total), 1)
    counted = slot < count_ref[...]
    named = jnp.where(counted, listed.astype(jnp.float32), 2.0 * NONE)

    def pick(user, source):
        low = (source * own).astype(jnp.float32)
        mine = (lane >= user * own) & (lane < (user + 1) * own)
        left = jnp.where(mine & (named >= low) & (named < low + own), named, NONE)
        picked = []
        for _ in range(CAP):
            least = jnp.min(left)
            picked.append(least)
            left = jnp.where(left == least, NONE, left)
        return picked

    row_len = kv_ref.shape[0] // own
    copies = []
    for by in range(1, spans):
        for j, block in enumerate(pick(me + by, me)):
            local = jnp.clip(block - (me * own).astype(jnp.float32), 0.0, NONE)
            local = jnp.where(local < own, local, 0.0).astype(jnp.int32)
            start = pl.multiple_of(local * row_len, row_len)
            copy = pltpu.make_async_copy(
                kv_ref.at[pl.ds(start, row_len), :],
                pools[by - 1].at[pl.ds(j * row_len, row_len), :],
                sem.at[(by - 1) * CAP + j],
            )
            copy.start()
            copies.append(copy)
    for by in range(spans):
        source = me - by
        for j, block in enumerate(pick(me, source)):
            used = jnp.max((named == block).astype(jnp.float32), axis=0, keepdims=True)
            local = block - (source * own).astype(jnp.float32)
            local = jnp.where(local < own, local, 0.0)
            row = by * CAP + j
            table_ref[row : row + 1, :] = used.astype(jnp.int32)
            ids = jnp.zeros((1, total), jnp.float32) + local
            table_ref[spans * CAP + row : spans * CAP + row + 1, :] = ids.astype(jnp.int32)
    for copy in copies:
        copy.wait()


def route(me, far_list, far_count, kv, spans):
    total = far_list.shape[0]
    rows = kv.shape[0] // (total // spans) * CAP
    pool = jax.ShapeDtypeStruct((rows, kv.shape[1]), kv.dtype)
    grid_spec = pltpu.PrefetchScalarGridSpec(
        num_scalar_prefetch=1,
        grid=(1,),
        in_specs=[
            pl.BlockSpec(far_list.shape[::-1], lambda i, *_: (0, 0)),
            pl.BlockSpec((1, total), lambda i, *_: (0, 0)),
            pl.BlockSpec(memory_space=pltpu.HBM),
        ],
        out_specs=[pl.BlockSpec((2 * CAP * spans, total), lambda i, *_: (0, 0))]
        + [pl.BlockSpec((rows, kv.shape[1]), lambda i, *_: (0, 0))] * (spans - 1),
        scratch_shapes=[pltpu.SemaphoreType.DMA(((spans - 1) * CAP,))],
    )
    return pl.pallas_call(
        route_kernel,
        grid_spec=grid_spec,
        out_shape=[jax.ShapeDtypeStruct((2 * CAP * spans, total), jnp.int32)] + [pool] * (spans - 1),
        cost_estimate=SMALL,
        name="route",
    )(me, far_list.T, far_count[None, :], kv)


def first_kernel(
    spans, me_ref, table_ref, q_ref, mine_ref, other_ref, qt_ref, acc_ref, stat_ref, kx_ref, vx_ref, both_t, vt, order, eye, diag
):
    heads = qt_ref.shape[0]
    own = pl.num_programs(0)
    c = pl.program_id(0)

    @pl.when(c == 0)
    def _():
        order[...] = split_order(heads)
        eye[...] = unit(eye.shape[0])
        diag[...] = causal_bias()

    base = pl.multiple_of(c * BLK, BLK)
    turn = order[...]
    to_heads(q_ref, BLK, turn, qt_ref, 0)
    to_heads(mine_ref, BLK, turn, both_t.at[me_ref[1]], base)
    to_heads(other_ref, BLK, turn, both_t.at[1 - me_ref[1]], base)
    kt = both_t.at[0]
    for h in range(heads):
        vt[h, :, pl.ds(base, BLK)] = contract_last(eye[...], both_t[1, h, pl.ds(base, BLK), :]).astype(jnp.bfloat16)

    @pl.when(c < WB - 1)
    def _():
        kx_ref[:, pl.ds(base, BLK), :] = kt[:, pl.ds(base, BLK), :]
        vx_ref[:, :, pl.ds(base, BLK)] = vt[:, :, pl.ds(base, BLK)]
        acc_ref[...] = jnp.zeros_like(acc_ref)
        floor = jnp.full(stat_ref.shape[1:], FLOOR, jnp.float32)
        stat_ref[0] = floor
        stat_ref[1] = jnp.zeros_like(floor)
        stat_ref[2] = floor

    @pl.when(c >= WB - 1)
    def _():
        start = pl.multiple_of((c - (WB - 1)) * BLK, BLK)
        here = me_ref[0] * own + c
        shut = [jnp.where(table_ref[j, here] > 0, 0.0, FLOOR) for j in range(CAP)]
        far_at = [pl.multiple_of(table_ref[spans * CAP + j, here] * BLK, BLK) for j in range(CAP)]
        causal = diag[...]
        for h in range(heads):
            q = qt_ref[h]
            near = near_scores(kt[h, pl.ds(start, WB * BLK), :], q, causal)
            top, w, total = softmax_blocks(near, [None] * WB)
            part = mix(vt[h, :, pl.ds(start, WB * BLK)], w)
            far = [contract_last(kt[h, pl.ds(at, BLK), :], q) for at in far_at]
            far_top, far_w, far_total = softmax_blocks(far, shut)
            far_v = jnp.concatenate([vt[h, :, pl.ds(at, BLK)] for at in far_at], axis=1)
            far_part = mix(far_v, far_w)
            both = jnp.maximum(top, far_top)
            a = jnp.exp2(top - both)
            b = jnp.exp2(far_top - both)
            acc_ref[h] = part * a + far_part * b
            stat_ref[0, h : h + 1, :] = both
            stat_ref[1, h : h + 1, :] = total * a + far_total * b
            stat_ref[2, h : h + 1, :] = far_top


def first(me, table, q, mine, other, heads, spans):
    tokens = q.shape[0] // heads
    width = q.shape[1]
    own = tokens // BLK
    raw = pl.BlockSpec((BLK * heads, width), lambda c, *_: (c, 0))
    grid_spec = pltpu.PrefetchScalarGridSpec(
        num_scalar_prefetch=2,
        grid=(own,),
        in_specs=[raw, raw, raw],
        out_specs=[
            pl.BlockSpec((heads, BLK, width), lambda c, *_: (0, c, 0)),
            pl.BlockSpec((heads, width, BLK), lambda c, *_: (0, 0, c)),
            pl.BlockSpec((3, heads, BLK), lambda c, *_: (0, 0, c)),
            pl.BlockSpec((heads, RIM, width), lambda c, *_: (0, 0, 0)),
            pl.BlockSpec((heads, width, RIM), lambda c, *_: (0, 0, 0)),
        ],
        scratch_shapes=[
            pltpu.VMEM((2, heads, tokens, width), jnp.bfloat16),
            pltpu.VMEM((heads, width, tokens), jnp.bfloat16),
            pltpu.VMEM((TILE, TILE), jnp.bfloat16),
            pltpu.VMEM((width, width), jnp.bfloat16),
            pltpu.VMEM((BLK, BLK), jnp.float32),
        ],
    )
    return pl.pallas_call(
        functools.partial(first_kernel, spans),
        grid_spec=grid_spec,
        out_shape=[
            jax.ShapeDtypeStruct((heads, tokens, width), jnp.bfloat16),
            jax.ShapeDtypeStruct((heads, width, tokens), jnp.float32),
            jax.ShapeDtypeStruct((3, heads, tokens), jnp.float32),
            jax.ShapeDtypeStruct((heads, RIM, width), jnp.bfloat16),
            jax.ShapeDtypeStruct((heads, width, RIM), jnp.bfloat16),
        ],
        compiler_params=pltpu.CompilerParams(vmem_limit_bytes=VMEM_BYTES),
        cost_estimate=SMALL,
        name="first",
    )(me, table, q, mine, other)


def take_halves(me_ref, mine_ref, other_ref, tokens, both_t, vt):
    heads, width = vt.shape[:2]
    turn = split_order(heads)
    to_heads(mine_ref, tokens, turn, both_t.at[me_ref[1]], 0)
    to_heads(other_ref, tokens, turn, both_t.at[1 - me_ref[1]], 0)
    eye = unit(width)
    for h in range(heads):
        vt[h, :, :tokens] = contract_last(eye, both_t[1, h, :tokens, :]).astype(jnp.bfloat16)


def finish(done, done_t, rows, order, out_ref):
    eye = unit(rows)
    for h in range(done.shape[0]):
        done[h] = contract_last(eye, done_t[h]).astype(jnp.bfloat16)
    from_heads(done, rows, order, out_ref)


def far_kernel(by, own, last, me_ref, table_ref, q_ref, mine_ref, other_ref, acc_in, stat_in, *rest):
    if last:
        acc_ref, stat_ref, out_ref, both_t, vt, order, done_t, done = rest
    else:
        acc_ref, stat_ref, both_t, vt = rest
    heads, rows, _ = q_ref.shape
    i = pl.program_id(0)

    @pl.when(i == 0)
    def _():
        take_halves(me_ref, mine_ref, other_ref, CAP * BLK, both_t, vt)
        if last:
            order[...] = join_order(heads)

    here = me_ref[0] * own + i * (rows // BLK)
    shut = []
    for j in range(CAP):
        row = [jnp.where(table_ref[by * CAP + j, here + a] > 0, 0.0, FLOOR) for a in range(rows // BLK)]
        shut.append(jnp.concatenate([jnp.full((1, BLK), closed, jnp.float32) for closed in row], axis=1))
    for h in range(heads):
        scores = contract_last(both_t[0, h], q_ref[h])
        blocks = [scores[j * BLK : (j + 1) * BLK, :] for j in range(CAP)]
        far_top, w, far_total = softmax_blocks(blocks, shut, stat_in[2, h : h + 1, :])
        top = stat_in[0, h : h + 1, :]
        both = jnp.maximum(top, far_top)
        a = jnp.exp2(top - both)
        b = jnp.exp2(far_top - both)
        total = stat_in[1, h : h + 1, :] * a + far_total * b
        part = acc_in[h] * a + mix(vt[h], w) * b
        acc_ref[h] = part
        stat_ref[0, h : h + 1, :] = both
        stat_ref[1, h : h + 1, :] = total
        stat_ref[2, h : h + 1, :] = far_top
        if last:
            done_t[h] = (part * (1.0 / jnp.where(total > 0.0, total, 1.0))).astype(jnp.bfloat16)
    if last:
        finish(done, done_t, rows, order[...], out_ref)


def far(by, me, table, qt, mine, other, acc, stat, last):
    heads, tokens, width = qt.shape
    rows = min(TILE, tokens)
    split = pl.BlockSpec((heads, rows, width), lambda i, *_: (0, i, 0))
    parts = pl.BlockSpec((heads, width, rows), lambda i, *_: (0, 0, i))
    stats = pl.BlockSpec((3, heads, rows), lambda i, *_: (0, 0, i))
    whole = pl.BlockSpec(mine.shape, lambda i, *_: (0, 0))
    out_specs = [parts, stats]
    out_shape = [
        jax.ShapeDtypeStruct(acc.shape, acc.dtype),
        jax.ShapeDtypeStruct(stat.shape, stat.dtype),
    ]
    scratch = [
        pltpu.VMEM((2, heads, CAP * BLK, width), jnp.bfloat16),
        pltpu.VMEM((heads, width, CAP * BLK), jnp.bfloat16),
    ]
    if last:
        out_specs.append(pl.BlockSpec((rows * heads, width), lambda i, *_: (i, 0)))
        out_shape.append(jax.ShapeDtypeStruct((tokens * heads, width), jnp.bfloat16))
        scratch.append(pltpu.VMEM((TILE, TILE), jnp.bfloat16))
        scratch.append(pltpu.VMEM((heads, width, rows), jnp.bfloat16))
        scratch.append(pltpu.VMEM((heads, rows, width), jnp.bfloat16))
    grid_spec = pltpu.PrefetchScalarGridSpec(
        num_scalar_prefetch=2,
        grid=(tokens // rows,),
        in_specs=[split, whole, whole, parts, stats],
        out_specs=out_specs,
        scratch_shapes=scratch,
    )
    return pl.pallas_call(
        functools.partial(far_kernel, by, tokens // BLK, last),
        grid_spec=grid_spec,
        out_shape=out_shape,
        input_output_aliases={5: 0, 6: 1},
        compiler_params=pltpu.CompilerParams(vmem_limit_bytes=VMEM_BYTES),
        cost_estimate=SMALL,
        name=f"far{by}",
    )(me, table, qt, mine, other, acc, stat)


def rim_kernel(
    me_ref, q_ref, mine_ref, other_ref, kx_ref, vx_ref, acc_in, stat_in, out_in, out_ref, both_t, vt, order, diag, done_t, done
):
    heads = q_ref.shape[0]
    c = pl.program_id(0)

    @pl.when(c == 0)
    def _():
        take_halves(me_ref, mine_ref, other_ref, RIM, both_t, vt)
        both_t[0, :, RIM:, :] = kx_ref[...]
        vt[:, :, RIM:] = vx_ref[...]
        order[...] = join_order(heads)
        diag[...] = causal_bias()

    start = pl.multiple_of(c * BLK, BLK)
    causal = diag[...]
    shut = [jnp.where((c + b >= WB - 1) | (me_ref[0] > 0), 0.0, FLOOR) for b in range(WB - 1)] + [None]
    for h in range(heads):
        near = near_scores(both_t[0, h, pl.ds(start, WB * BLK), :], q_ref[h], causal)
        near_top, w, near_total = softmax_blocks(near, shut)
        top = stat_in[0, h : h + 1, :]
        both = jnp.maximum(top, near_top)
        a = jnp.exp2(top - both)
        b = jnp.exp2(near_top - both)
        total = stat_in[1, h : h + 1, :] * a + near_total * b
        part = acc_in[h] * a + mix(vt[h, :, pl.ds(start, WB * BLK)], w) * b
        done_t[h] = (part * (1.0 / total)).astype(jnp.bfloat16)
    finish(done, done_t, BLK, order[...], out_ref)


def rim(me, qt, mine, other, kx, vx, acc, stat, out):
    heads, tokens, width = qt.shape
    grid_spec = pltpu.PrefetchScalarGridSpec(
        num_scalar_prefetch=1,
        grid=(WB - 1,),
        in_specs=[
            pl.BlockSpec((heads, BLK, width), lambda i, *_: (0, i, 0)),
            pl.BlockSpec(mine.shape, lambda i, *_: (0, 0)),
            pl.BlockSpec(mine.shape, lambda i, *_: (0, 0)),
            pl.BlockSpec(kx.shape, lambda i, *_: (0, 0, 0)),
            pl.BlockSpec(vx.shape, lambda i, *_: (0, 0, 0)),
            pl.BlockSpec((heads, width, BLK), lambda i, *_: (0, 0, i)),
            pl.BlockSpec((3, heads, BLK), lambda i, *_: (0, 0, i)),
            pl.BlockSpec(memory_space=pl.ANY),
        ],
        out_specs=pl.BlockSpec((BLK * heads, width), lambda i, *_: (i, 0)),
        scratch_shapes=[
            pltpu.VMEM((2, heads, 2 * RIM, width), jnp.bfloat16),
            pltpu.VMEM((heads, width, 2 * RIM), jnp.bfloat16),
            pltpu.VMEM((TILE, TILE), jnp.bfloat16),
            pltpu.VMEM((BLK, BLK), jnp.float32),
            pltpu.VMEM((heads, width, BLK), jnp.bfloat16),
            pltpu.VMEM((heads, BLK, width), jnp.bfloat16),
        ],
    )
    return pl.pallas_call(
        rim_kernel,
        grid_spec=grid_spec,
        out_shape=jax.ShapeDtypeStruct(out.shape, out.dtype),
        input_output_aliases={8: 0},
        compiler_params=pltpu.CompilerParams(vmem_limit_bytes=VMEM_BYTES),
        cost_estimate=SMALL,
        name="rim",
    )(me, qt, mine, other, kx, vx, acc, stat, out)


def other_core(x):
    return lax.ppermute(x, "rep", [(0, 1), (1, 0)])


def ahead(x, by):
    count = lax.axis_size("ctx")
    return lax.ppermute(x, "ctx", [(i, i + by) for i in range(count - by)])


def local(queries, keys_values, far_list, far_count):
    tokens, heads, _, width = queries.shape
    spans = lax.axis_size("ctx")
    me = jnp.stack([lax.axis_index("ctx"), lax.axis_index("rep")]).astype(jnp.int32)
    q = queries.reshape(tokens * heads, width)
    kv = keys_values.reshape(tokens * heads, width)
    rim_mine = ahead(kv[(tokens - RIM) * heads :], 1)
    other = other_core(kv)
    table, *pools = route(me, far_list, far_count, kv, spans)
    arrived = [ahead(pool, by) for by, pool in enumerate(pools, 1)]
    qt, acc, stat, kx, vx = first(me, table, q, kv, other, heads, spans)
    rim_mine, stat = lax.optimization_barrier((rim_mine, stat))
    rim_other = other_core(rim_mine)
    for by in range(spans - 1, 0, -1):
        piece, stat = lax.optimization_barrier((arrived[by - 1], stat))
        acc, stat, *out = far(by, me, table, qt, piece, other_core(piece), acc, stat, by == 1)
    done = rim(me, qt, rim_mine, rim_other, kx, vx, acc, stat, out[0])
    return done.reshape(queries.shape)


def solution(mesh):
    in_specs = (
        P(("groups", "ctx"), "head", "rep", None),
        P("rep", ("groups", "ctx"), "head", None),
        P("groups", None),
        P("groups"),
    )
    out_specs = P(("groups", "ctx"), "head", "rep", None)
    return jax.shard_map(local, mesh=mesh, in_specs=in_specs, out_specs=out_specs, check_vma=False)
```

```python
import functools
import math

import jax
import jax.numpy as jnp
from jax import lax
from jax.experimental import pallas as pl
from jax.experimental.pallas import tpu as pltpu
from jax.sharding import PartitionSpec as P

BLK = 128
WB = 4
CAP = 2
RIM = (WB - 1) * BLK
TILE = 256
GROUP = 3

FLOOR = -1.0e30
SCALE = math.log2(math.e) / 12.0
NONE = 1.0e6
VMEM_BYTES = 48 * 1024 * 1024
SMALL = pl.CostEstimate(flops=1024, bytes_accessed=1024, transcendentals=0)


def contract_last(a, b):
    return lax.dot_general(a, b, (((1,), (1,)), ((), ())), preferred_element_type=jnp.float32)


def mix(a, b):
    return jnp.dot(a, b, preferred_element_type=jnp.float32)


def unit(n):
    row = lax.broadcasted_iota(jnp.int32, (n, n), 0)
    col = lax.broadcasted_iota(jnp.int32, (n, n), 1)
    return (row == col).astype(jnp.float32).astype(jnp.bfloat16)


def causal_bias():
    key = lax.broadcasted_iota(jnp.int32, (BLK, BLK), 0)
    query = lax.broadcasted_iota(jnp.int32, (BLK, BLK), 1)
    return jnp.where(key <= query, 0.0, FLOOR)


def softmax_blocks(scores, shut, top=None):
    for block, closed in zip(scores, shut):
        block_top = jnp.max(block, axis=0, keepdims=True) * SCALE
        block_top = block_top if closed is None else block_top + closed
        top = block_top if top is None else jnp.maximum(top, block_top)
    weights, total = [], 0.0
    for block, closed in zip(scores, shut):
        base = top if closed is None else jnp.where(closed < 0.0, -FLOOR, top)
        w = jnp.exp2(block * SCALE - base)
        total = total + jnp.sum(w, axis=0, keepdims=True)
        weights.append(w.astype(jnp.bfloat16))
    return top, jnp.concatenate(weights, axis=0), total


def near_scores(scores, causal):
    blocks = [scores[b * BLK : (b + 1) * BLK, :] for b in range(WB)]
    return blocks[:-1] + [blocks[-1] + causal]


def split_order(heads):
    step = TILE // heads
    row = lax.broadcasted_iota(jnp.int32, (TILE, TILE), 0)
    col = lax.broadcasted_iota(jnp.int32, (TILE, TILE), 1)
    return (col == (row % step) * heads + row // step).astype(jnp.float32).astype(jnp.bfloat16)


def join_order(heads):
    step = TILE // heads
    row = lax.broadcasted_iota(jnp.int32, (TILE, TILE), 0)
    col = lax.broadcasted_iota(jnp.int32, (TILE, TILE), 1)
    return (col == (row % heads) * step + row // heads).astype(jnp.float32).astype(jnp.bfloat16)


def to_heads(src, tokens, order, dst, base):
    heads = dst.shape[0]
    step = TILE // heads
    for i in range(tokens // step):
        turned = mix(order, src[i * TILE : (i + 1) * TILE, :]).astype(jnp.bfloat16)
        dst[:, pl.ds(base + i * step, step), :] = turned.reshape(heads, step, turned.shape[-1])


def from_heads(src, tokens, order, dst):
    heads = src.shape[0]
    step = TILE // heads
    for i in range(tokens // step):
        rows = src[:, i * step : (i + 1) * step, :].reshape(TILE, src.shape[-1])
        dst[i * TILE : (i + 1) * TILE, :] = mix(order, rows).astype(jnp.bfloat16)


def route_kernel(me_ref, list_ref, count_ref, kv_ref, table_ref, *rest):
    spans = table_ref.shape[0] // (2 * CAP)
    pools, sem = rest[:-1], rest[-1]
    me = me_ref[0]
    listed = list_ref[...]
    entries, total = listed.shape
    own = total // spans
    slot = lax.broadcasted_iota(jnp.int32, (entries, total), 0)
    lane = lax.broadcasted_iota(jnp.int32, (entries, total), 1)
    counted = slot < count_ref[...]
    named = jnp.where(counted, listed.astype(jnp.float32), 2.0 * NONE)

    def pick(user, source):
        low = (source * own).astype(jnp.float32)
        mine = (lane >= user * own) & (lane < (user + 1) * own)
        left = jnp.where(mine & (named >= low) & (named < low + own), named, NONE)
        picked = []
        for _ in range(CAP):
            least = jnp.min(left)
            picked.append(least)
            left = jnp.where(left == least, NONE, left)
        return picked

    row_len = kv_ref.shape[0] // own
    copies = []
    for by in range(1, spans):
        for j, block in enumerate(pick(me + by, me)):
            local = jnp.clip(block - (me * own).astype(jnp.float32), 0.0, NONE)
            local = jnp.where(local < own, local, 0.0).astype(jnp.int32)
            start = pl.multiple_of(local * row_len, row_len)
            copy = pltpu.make_async_copy(
                kv_ref.at[pl.ds(start, row_len), :],
                pools[by - 1].at[pl.ds(j * row_len, row_len), :],
                sem.at[(by - 1) * CAP + j],
            )
            copy.start()
            copies.append(copy)
    for by in range(spans):
        source = me - by
        for j, block in enumerate(pick(me, source)):
            used = jnp.max((named == block).astype(jnp.float32), axis=0, keepdims=True)
            local = block - (source * own).astype(jnp.float32)
            local = jnp.where(local < own, local, 0.0)
            row = by * CAP + j
            table_ref[row : row + 1, :] = used.astype(jnp.int32)
            ids = jnp.zeros((1, total), jnp.float32) + local
            table_ref[spans * CAP + row : spans * CAP + row + 1, :] = ids.astype(jnp.int32)
    for copy in copies:
        copy.wait()


def route(me, far_list, far_count, kv, spans):
    total = far_list.shape[0]
    rows = kv.shape[0] // (total // spans) * CAP
    pool = jax.ShapeDtypeStruct((rows, kv.shape[1]), kv.dtype)
    grid_spec = pltpu.PrefetchScalarGridSpec(
        num_scalar_prefetch=1,
        grid=(1,),
        in_specs=[
            pl.BlockSpec(far_list.shape[::-1], lambda i, *_: (0, 0)),
            pl.BlockSpec((1, total), lambda i, *_: (0, 0)),
            pl.BlockSpec(memory_space=pltpu.HBM),
        ],
        out_specs=[pl.BlockSpec((2 * CAP * spans, total), lambda i, *_: (0, 0))]
        + [pl.BlockSpec((rows, kv.shape[1]), lambda i, *_: (0, 0))] * (spans - 1),
        scratch_shapes=[pltpu.SemaphoreType.DMA(((spans - 1) * CAP,))],
    )
    return pl.pallas_call(
        route_kernel,
        grid_spec=grid_spec,
        out_shape=[jax.ShapeDtypeStruct((2 * CAP * spans, total), jnp.int32)] + [pool] * (spans - 1),
        cost_estimate=SMALL,
        name="route",
    )(me, far_list.T, far_count[None, :], kv)


def first_kernel(
    spans, me_ref, table_ref, q_ref, mine_ref, other_ref, qt_ref, acc_ref, stat_ref, kx_ref, vx_ref, both_t, vt, qs, order, eye, diag
):
    heads = qt_ref.shape[0]
    own = pl.num_programs(0)
    c = pl.program_id(0)

    @pl.when(c == 0)
    def _():
        order[...] = split_order(heads)
        eye[...] = unit(eye.shape[0])
        diag[...] = causal_bias()

    base = pl.multiple_of(c * BLK, BLK)
    turn = order[...]
    to_heads(q_ref, BLK, turn, qs, 0)
    to_heads(mine_ref, BLK, turn, both_t.at[me_ref[1]], base)
    to_heads(other_ref, BLK, turn, both_t.at[1 - me_ref[1]], base)
    kt = both_t.at[0]
    for h in range(heads):
        qt_ref[h] = qs[h]
        vt[h, :, pl.ds(base, BLK)] = contract_last(eye[...], both_t[1, h, pl.ds(base, BLK), :]).astype(jnp.bfloat16)

    @pl.when(c < WB - 1)
    def _():
        kx_ref[:, pl.ds(base, BLK), :] = kt[:, pl.ds(base, BLK), :]
        vx_ref[:, :, pl.ds(base, BLK)] = vt[:, :, pl.ds(base, BLK)]
        acc_ref[...] = jnp.zeros_like(acc_ref)
        floor = jnp.full(stat_ref.shape[1:], FLOOR, jnp.float32)
        stat_ref[0] = floor
        stat_ref[1] = jnp.zeros_like(floor)
        stat_ref[2] = floor

    @pl.when(c >= WB - 1)
    def _():
        start = pl.multiple_of((c - (WB - 1)) * BLK, BLK)
        here = me_ref[0] * own + c
        shut = [jnp.where(table_ref[j, here] > 0, 0.0, FLOOR) for j in range(CAP)]
        far_at = [pl.multiple_of(table_ref[spans * CAP + j, here] * BLK, BLK) for j in range(CAP)]
        causal = diag[...]
        for h in range(heads):
            q = qs[h]
            near = near_scores(contract_last(kt[h, pl.ds(start, WB * BLK), :], q), causal)
            top, w, total = softmax_blocks(near, [None] * WB)
            part = mix(vt[h, :, pl.ds(start, WB * BLK)], w)
            far = [contract_last(kt[h, pl.ds(at, BLK), :], q) for at in far_at]
            far_top, far_w, far_total = softmax_blocks(far, shut)
            far_v = jnp.concatenate([vt[h, :, pl.ds(at, BLK)] for at in far_at], axis=1)
            far_part = mix(far_v, far_w)
            both = jnp.maximum(top, far_top)
            a = jnp.exp2(top - both)
            b = jnp.exp2(far_top - both)
            acc_ref[h] = part * a + far_part * b
            stat_ref[0, h : h + 1, :] = both
            stat_ref[1, h : h + 1, :] = total * a + far_total * b
            stat_ref[2, h : h + 1, :] = far_top


def first(me, table, q, mine, other, heads, spans):
    tokens = q.shape[0] // heads
    width = q.shape[1]
    own = tokens // BLK
    raw = pl.BlockSpec((BLK * heads, width), lambda c, *_: (c, 0))
    grid_spec = pltpu.PrefetchScalarGridSpec(
        num_scalar_prefetch=2,
        grid=(own,),
        in_specs=[raw, raw, raw],
        out_specs=[
            pl.BlockSpec((heads, BLK, width), lambda c, *_: (0, c, 0)),
            pl.BlockSpec((heads, width, BLK), lambda c, *_: (0, 0, c)),
            pl.BlockSpec((3, heads, BLK), lambda c, *_: (0, 0, c)),
            pl.BlockSpec((heads, RIM, width), lambda c, *_: (0, 0, 0)),
            pl.BlockSpec((heads, width, RIM), lambda c, *_: (0, 0, 0)),
        ],
        scratch_shapes=[
            pltpu.VMEM((2, heads, tokens, width), jnp.bfloat16),
            pltpu.VMEM((heads, width, tokens), jnp.bfloat16),
            pltpu.VMEM((heads, BLK, width), jnp.bfloat16),
            pltpu.VMEM((TILE, TILE), jnp.bfloat16),
            pltpu.VMEM((width, width), jnp.bfloat16),
            pltpu.VMEM((BLK, BLK), jnp.float32),
        ],
    )
    return pl.pallas_call(
        functools.partial(first_kernel, spans),
        grid_spec=grid_spec,
        out_shape=[
            jax.ShapeDtypeStruct((heads, tokens, width), jnp.bfloat16),
            jax.ShapeDtypeStruct((heads, width, tokens), jnp.float32),
            jax.ShapeDtypeStruct((3, heads, tokens), jnp.float32),
            jax.ShapeDtypeStruct((heads, RIM, width), jnp.bfloat16),
            jax.ShapeDtypeStruct((heads, width, RIM), jnp.bfloat16),
        ],
        compiler_params=pltpu.CompilerParams(vmem_limit_bytes=VMEM_BYTES),
        cost_estimate=SMALL,
        name="first",
    )(me, table, q, mine, other)


def take_halves(me_ref, mine_ref, other_ref, tokens, base, both_t, vt):
    heads, width = vt.shape[:2]
    turn = split_order(heads)
    to_heads(mine_ref, tokens, turn, both_t.at[me_ref[1]], base)
    to_heads(other_ref, tokens, turn, both_t.at[1 - me_ref[1]], base)
    eye = unit(width)
    span = slice(base, base + tokens)
    for h in range(heads):
        vt[h, :, span] = contract_last(eye, both_t[1, h, span, :]).astype(jnp.bfloat16)


def finish(done, done_t, rows, order, out_ref):
    eye = unit(rows)
    for h in range(done.shape[0]):
        done[h] = contract_last(eye, done_t[h]).astype(jnp.bfloat16)
    from_heads(done, rows, order, out_ref)


def far_kernel(bys, own, last, me_ref, table_ref, q_ref, *rest):
    halves, rest = rest[: 2 * len(bys)], rest[2 * len(bys) :]
    acc_in, stat_in, acc_ref, stat_ref, *rest = rest
    if last:
        out_ref, *rest = rest
    both_t, vt, scores_a, scores_b, tops_a, tops_b, weights, *rest = rest
    if last:
        order, done_t, done = rest
    heads, rows, _ = q_ref.shape
    i = pl.program_id(0)

    @pl.when(i == 0)
    def _():
        for n in range(len(bys)):
            take_halves(me_ref, halves[2 * n], halves[2 * n + 1], CAP * BLK, n * CAP * BLK, both_t, vt)
        if last:
            order[...] = join_order(heads)

    here = me_ref[0] * own + i * (rows // BLK)
    shut = []
    for by in bys:
        for j in range(CAP):
            row = [jnp.where(table_ref[by * CAP + j, here + a] > 0, 0.0, FLOOR) for a in range(rows // BLK)]
            shut.append(jnp.concatenate([jnp.full((1, BLK), closed, jnp.float32) for closed in row], axis=1))

    def fill(h, scores, tops):
        for j in range(len(shut)):
            block = contract_last(both_t[0, h, j * BLK : (j + 1) * BLK, :], q_ref[h])
            tops[j : j + 1, :] = jnp.max(block, axis=0, keepdims=True)
            scores[j * BLK : (j + 1) * BLK, :] = block

    def use(h, scores, tops):
        row = pl.ds(h, 1)
        far_top = stat_in[2, row, :]
        for j, closed in enumerate(shut):
            far_top = jnp.maximum(far_top, tops[j : j + 1, :] * SCALE + closed)
        far_total = 0.0
        for j, closed in enumerate(shut):
            base = jnp.where(closed < 0.0, -FLOOR, far_top)
            w = jnp.exp2(scores[j * BLK : (j + 1) * BLK, :] * SCALE - base)
            far_total = far_total + jnp.sum(w, axis=0, keepdims=True)
            weights[j * BLK : (j + 1) * BLK, :] = w.astype(jnp.bfloat16)
        top = stat_in[0, row, :]
        both = jnp.maximum(top, far_top)
        a = jnp.exp2(top - both)
        b = jnp.exp2(far_top - both)
        total = stat_in[1, row, :] * a + far_total * b
        part = acc_in[h] * a + mix(vt[h], weights[...]) * b
        acc_ref[h] = part
        stat_ref[0, row, :] = both
        stat_ref[1, row, :] = total
        stat_ref[2, row, :] = far_top
        if last:
            done_t[h] = (part * (1.0 / jnp.where(total > 0.0, total, 1.0))).astype(jnp.bfloat16)

    fill(0, scores_a, tops_a)

    def two_heads(n, carry):
        h = 2 * n
        fill(h + 1, scores_b, tops_b)
        use(h, scores_a, tops_a)
        fill(jnp.minimum(h + 2, heads - 1), scores_a, tops_a)
        use(h + 1, scores_b, tops_b)
        return carry

    lax.fori_loop(0, heads // 2, two_heads, 0)
    if last:
        finish(done, done_t, rows, order[...], out_ref)


def far(bys, me, table, qt, halves, acc, stat, last):
    heads, tokens, width = qt.shape
    rows = min(TILE, tokens)
    keys = len(bys) * CAP * BLK
    parts = pl.BlockSpec((heads, width, rows), lambda i, *_: (0, 0, i))
    stats = pl.BlockSpec((3, heads, rows), lambda i, *_: (0, 0, i))
    whole = pl.BlockSpec(halves[0].shape, lambda i, *_: (0, 0))
    out_specs = [parts, stats]
    out_shape = [
        jax.ShapeDtypeStruct(acc.shape, acc.dtype),
        jax.ShapeDtypeStruct(stat.shape, stat.dtype),
    ]
    scratch = [
        pltpu.VMEM((2, heads, keys, width), jnp.bfloat16),
        pltpu.VMEM((heads, width, keys), jnp.bfloat16),
        pltpu.VMEM((keys, rows), jnp.float32),
        pltpu.VMEM((keys, rows), jnp.float32),
        pltpu.VMEM((keys // BLK, rows), jnp.float32),
        pltpu.VMEM((keys // BLK, rows), jnp.float32),
        pltpu.VMEM((keys, rows), jnp.bfloat16),
    ]
    if last:
        out_specs.append(pl.BlockSpec((rows * heads, width), lambda i, *_: (i, 0)))
        out_shape.append(jax.ShapeDtypeStruct((tokens * heads, width), jnp.bfloat16))
        scratch.append(pltpu.VMEM((TILE, TILE), jnp.bfloat16))
        scratch.append(pltpu.VMEM((heads, width, rows), jnp.bfloat16))
        scratch.append(pltpu.VMEM((heads, rows, width), jnp.bfloat16))
    grid_spec = pltpu.PrefetchScalarGridSpec(
        num_scalar_prefetch=2,
        grid=(tokens // rows,),
        in_specs=[pl.BlockSpec((heads, rows, width), lambda i, *_: (0, i, 0))] + [whole] * len(halves) + [parts, stats],
        out_specs=out_specs,
        scratch_shapes=scratch,
    )
    return pl.pallas_call(
        functools.partial(far_kernel, bys, tokens // BLK, last),
        grid_spec=grid_spec,
        out_shape=out_shape,
        input_output_aliases={3 + len(halves): 0, 4 + len(halves): 1},
        compiler_params=pltpu.CompilerParams(vmem_limit_bytes=VMEM_BYTES),
        cost_estimate=SMALL,
        name="far",
    )(me, table, qt, *halves, acc, stat)


def rim_kernel(
    me_ref, q_ref, mine_ref, other_ref, kx_ref, vx_ref, acc_in, stat_in, out_in, out_ref, both_t, vt, order, diag, done_t, done
):
    heads = q_ref.shape[0]
    c = pl.program_id(0)

    @pl.when(c == 0)
    def _():
        take_halves(me_ref, mine_ref, other_ref, RIM, 0, both_t, vt)
        both_t[0, :, RIM:, :] = kx_ref[...]
        vt[:, :, RIM:] = vx_ref[...]
        order[...] = join_order(heads)
        diag[...] = causal_bias()

    start = pl.multiple_of(c * BLK, BLK)
    causal = diag[...]
    shut = [jnp.where((c + b >= WB - 1) | (me_ref[0] > 0), 0.0, FLOOR) for b in range(WB - 1)] + [None]
    for h in range(heads):
        near = near_scores(contract_last(both_t[0, h, pl.ds(start, WB * BLK), :], q_ref[h]), causal)
        near_top, w, near_total = softmax_blocks(near, shut)
        top = stat_in[0, h : h + 1, :]
        both = jnp.maximum(top, near_top)
        a = jnp.exp2(top - both)
        b = jnp.exp2(near_top - both)
        total = stat_in[1, h : h + 1, :] * a + near_total * b
        part = acc_in[h] * a + mix(vt[h, :, pl.ds(start, WB * BLK)], w) * b
        done_t[h] = (part * (1.0 / total)).astype(jnp.bfloat16)
    finish(done, done_t, BLK, order[...], out_ref)


def rim(me, qt, mine, other, kx, vx, acc, stat, out):
    heads, tokens, width = qt.shape
    grid_spec = pltpu.PrefetchScalarGridSpec(
        num_scalar_prefetch=1,
        grid=(WB - 1,),
        in_specs=[
            pl.BlockSpec((heads, BLK, width), lambda i, *_: (0, i, 0)),
            pl.BlockSpec(mine.shape, lambda i, *_: (0, 0)),
            pl.BlockSpec(mine.shape, lambda i, *_: (0, 0)),
            pl.BlockSpec(kx.shape, lambda i, *_: (0, 0, 0)),
            pl.BlockSpec(vx.shape, lambda i, *_: (0, 0, 0)),
            pl.BlockSpec((heads, width, BLK), lambda i, *_: (0, 0, i)),
            pl.BlockSpec((3, heads, BLK), lambda i, *_: (0, 0, i)),
            pl.BlockSpec(memory_space=pl.ANY),
        ],
        out_specs=pl.BlockSpec((BLK * heads, width), lambda i, *_: (i, 0)),
        scratch_shapes=[
            pltpu.VMEM((2, heads, 2 * RIM, width), jnp.bfloat16),
            pltpu.VMEM((heads, width, 2 * RIM), jnp.bfloat16),
            pltpu.VMEM((TILE, TILE), jnp.bfloat16),
            pltpu.VMEM((BLK, BLK), jnp.float32),
            pltpu.VMEM((heads, width, BLK), jnp.bfloat16),
            pltpu.VMEM((heads, BLK, width), jnp.bfloat16),
        ],
    )
    return pl.pallas_call(
        rim_kernel,
        grid_spec=grid_spec,
        out_shape=jax.ShapeDtypeStruct(out.shape, out.dtype),
        input_output_aliases={8: 0},
        compiler_params=pltpu.CompilerParams(vmem_limit_bytes=VMEM_BYTES),
        cost_estimate=SMALL,
        name="rim",
    )(me, qt, mine, other, kx, vx, acc, stat, out)


def other_core(x):
    return lax.ppermute(x, "rep", [(0, 1), (1, 0)])


def ahead(x, by):
    count = lax.axis_size("ctx")
    return lax.ppermute(x, "ctx", [(i, i + by) for i in range(count - by)])


def local(queries, keys_values, far_list, far_count):
    tokens, heads, _, width = queries.shape
    spans = lax.axis_size("ctx")
    me = jnp.stack([lax.axis_index("ctx"), lax.axis_index("rep")]).astype(jnp.int32)
    q = queries.reshape(tokens * heads, width)
    kv = keys_values.reshape(tokens * heads, width)
    other = other_core(kv)
    table, *pools = route(me, far_list, far_count, kv, spans)
    pieces = [ahead(pool, by) for by, pool in enumerate(pools, 1)]
    rim_mine = ahead(kv[(tokens - RIM) * heads :], 1)
    qt, acc, stat, kx, vx = first(me, table, q, kv, other, heads, spans)
    *pieces, stat = lax.optimization_barrier((*pieces, stat))
    others = [other_core(piece) for piece in pieces]
    bys = list(range(1, spans))
    groups = [bys[n : n + GROUP] for n in range(0, len(bys), GROUP)]
    for group in groups:
        halves = [half for by in group for half in (pieces[by - 1], others[by - 1])]
        acc, stat, *out = far(group, me, table, qt, halves, acc, stat, group is groups[-1])
    rim_mine, stat = lax.optimization_barrier((rim_mine, stat))
    done = rim(me, qt, rim_mine, other_core(rim_mine), kx, vx, acc, stat, out[0])
    return done.reshape(queries.shape)


def solution(mesh):
    in_specs = (
        P(("groups", "ctx"), "head", "rep", None),
        P("rep", ("groups", "ctx"), "head", None),
        P("groups", None),
        P("groups"),
    )
    out_specs = P(("groups", "ctx"), "head", "rep", None)
    return jax.shard_map(local, mesh=mesh, in_specs=in_specs, out_specs=out_specs, check_vma=False)
```

```python
import functools
import math

import jax
import jax.numpy as jnp
from jax import lax
from jax.experimental import pallas as pl
from jax.experimental.pallas import tpu as pltpu
from jax.sharding import PartitionSpec as P

BLK = 128
WB = 4
CAP = 2
RIM = (WB - 1) * BLK
TILE = 256
GROUP = 3
STRIDE = 2

FLOOR = -1.0e30
SCALE = math.log2(math.e) / 12.0
NONE = 1.0e6
VMEM_BYTES = 48 * 1024 * 1024
SMALL = pl.CostEstimate(flops=1024, bytes_accessed=1024, transcendentals=0)


def contract_last(a, b):
    return lax.dot_general(a, b, (((1,), (1,)), ((), ())), preferred_element_type=jnp.float32)


def mix(a, b):
    return jnp.dot(a, b, preferred_element_type=jnp.float32)


def unit(n):
    row = lax.broadcasted_iota(jnp.int32, (n, n), 0)
    col = lax.broadcasted_iota(jnp.int32, (n, n), 1)
    return (row == col).astype(jnp.float32).astype(jnp.bfloat16)


def causal_bias():
    key = lax.broadcasted_iota(jnp.int32, (BLK, BLK), 0)
    query = lax.broadcasted_iota(jnp.int32, (BLK, BLK), 1)
    return jnp.where(key <= query, 0.0, FLOOR)


def softmax_blocks(scores, shut, top=None):
    for block, closed in zip(scores, shut):
        block_top = jnp.max(block, axis=0, keepdims=True) * SCALE
        block_top = block_top if closed is None else block_top + closed
        top = block_top if top is None else jnp.maximum(top, block_top)
    weights, total = [], 0.0
    for block, closed in zip(scores, shut):
        base = top if closed is None else jnp.where(closed < 0.0, -FLOOR, top)
        w = jnp.exp2(block * SCALE - base)
        total = total + jnp.sum(w, axis=0, keepdims=True)
        weights.append(w.astype(jnp.bfloat16))
    return top, jnp.concatenate(weights, axis=0), total


def near_scores(scores, causal):
    blocks = [scores[b * BLK : (b + 1) * BLK, :] for b in range(WB)]
    return blocks[:-1] + [blocks[-1] + causal]


def split_order(heads):
    step = TILE // heads
    row = lax.broadcasted_iota(jnp.int32, (TILE, TILE), 0)
    col = lax.broadcasted_iota(jnp.int32, (TILE, TILE), 1)
    return (col == (row % step) * heads + row // step).astype(jnp.float32).astype(jnp.bfloat16)


def join_order(heads):
    step = TILE // heads
    row = lax.broadcasted_iota(jnp.int32, (TILE, TILE), 0)
    col = lax.broadcasted_iota(jnp.int32, (TILE, TILE), 1)
    return (col == (row % heads) * step + row // heads).astype(jnp.float32).astype(jnp.bfloat16)


def chunk_pairs(rows, order):
    turned = []
    for i in range(0, rows.shape[0], 2 * TILE):
        two = jnp.concatenate([rows[i : i + TILE, :], rows[i + TILE : i + 2 * TILE, :]], axis=1)
        two = mix(order, two).astype(jnp.bfloat16)
        turned += [two[:, : rows.shape[1]], two[:, rows.shape[1] :]]
    return turned


def put_heads(turned, dst, base):
    heads = dst.shape[0]
    step = TILE // heads
    for i, rows in enumerate(turned):
        dst[:, pl.ds(base + i * step, step), :] = rows.reshape(heads, step, rows.shape[-1])


def route_kernel(me_ref, list_ref, count_ref, kv_ref, table_ref, *rest):
    spans = table_ref.shape[0] // (2 * CAP)
    pools, rim_out, sem = rest[:-2], rest[-2], rest[-1]
    edge = pltpu.make_async_copy(
        kv_ref.at[pl.ds(kv_ref.shape[0] - rim_out.shape[0], rim_out.shape[0]), :], rim_out, sem.at[sem.shape[0] - 1]
    )
    edge.start()
    me = me_ref[0]
    listed = list_ref[...]
    entries, total = listed.shape
    own = total // spans
    slot = lax.broadcasted_iota(jnp.int32, (entries, total), 0)
    lane = lax.broadcasted_iota(jnp.int32, (entries, total), 1)
    counted = slot < count_ref[...]
    named = jnp.where(counted, listed.astype(jnp.float32), 2.0 * NONE)

    def pick(user, source):
        low = (source * own).astype(jnp.float32)
        mine = (lane >= user * own) & (lane < (user + 1) * own)
        left = jnp.where(mine & (named >= low) & (named < low + own), named, NONE)
        picked = []
        for _ in range(CAP):
            least = jnp.min(jnp.min(left, axis=0, keepdims=True), axis=1, keepdims=True)
            picked.append(least)
            left = jnp.where(left == least, NONE, left)
        return picked

    row_len = kv_ref.shape[0] // own
    sent = [block for by in range(1, spans) for block in pick(me + by, me)]
    copies = []
    for n, block in enumerate(sent):
        local = block - (me * own).astype(jnp.float32)
        local = jnp.max(jnp.where(local < own, local, 0.0)).astype(jnp.int32)
        start = pl.multiple_of(local * row_len, row_len)
        copy = pltpu.make_async_copy(
            kv_ref.at[pl.ds(start, row_len), :],
            pools[n // CAP].at[pl.ds(n % CAP * row_len, row_len), :],
            sem.at[n],
        )
        copies.append(copy)
    for copy in copies:
        copy.start()
    for by in range(spans):
        source = me - by
        for j, block in enumerate(pick(me, source)):
            used = jnp.max((named == block).astype(jnp.float32), axis=0, keepdims=True)
            local = block - (source * own).astype(jnp.float32)
            local = jnp.where(local < own, local, 0.0)
            row = by * CAP + j
            table_ref[row : row + 1, :] = used.astype(jnp.int32)
            ids = jnp.zeros((1, total), jnp.float32) + local
            table_ref[spans * CAP + row : spans * CAP + row + 1, :] = ids.astype(jnp.int32)
    for copy in copies:
        copy.wait()
    edge.wait()


def route(me, far_list, far_count, kv, spans):
    total = far_list.shape[0]
    rows = kv.shape[0] // (total // spans) * CAP
    pool = jax.ShapeDtypeStruct((rows, kv.shape[1]), kv.dtype)
    edge = jax.ShapeDtypeStruct((rows // CAP * (WB - 1), kv.shape[1]), kv.dtype)
    grid_spec = pltpu.PrefetchScalarGridSpec(
        num_scalar_prefetch=1,
        grid=(1,),
        in_specs=[
            pl.BlockSpec(far_list.shape[::-1], lambda i, *_: (0, 0)),
            pl.BlockSpec((1, total), lambda i, *_: (0, 0)),
            pl.BlockSpec(memory_space=pltpu.HBM),
        ],
        out_specs=[pl.BlockSpec((2 * CAP * spans, total), lambda i, *_: (0, 0))]
        + [pl.BlockSpec(pool.shape, lambda i, *_: (0, 0))] * (spans - 1)
        + [pl.BlockSpec(edge.shape, lambda i, *_: (0, 0))],
        scratch_shapes=[pltpu.SemaphoreType.DMA(((spans - 1) * CAP + 1,))],
    )
    return pl.pallas_call(
        route_kernel,
        grid_spec=grid_spec,
        out_shape=[jax.ShapeDtypeStruct((2 * CAP * spans, total), jnp.int32)] + [pool] * (spans - 1) + [edge],
        cost_estimate=SMALL,
        name="route",
    )(me, far_list.T, far_count[None, :], kv)


def first_kernel(
    spans, me_ref, table_ref, q_ref, mine_ref, other_ref, qt_ref, acc_ref, stat_ref, kx_ref, vx_ref, both_t, vt, qs, order, eye, diag
):
    heads = qt_ref.shape[0]
    own = pl.num_programs(0)
    c = pl.program_id(0)

    @pl.when(c == 0)
    def _():
        order[...] = split_order(heads)
        eye[...] = unit(eye.shape[0])
        diag[...] = causal_bias()

    base = pl.multiple_of(c * BLK, BLK)
    turn = order[...]
    turned = [chunk_pairs(ref[...], turn) for ref in (q_ref, mine_ref, other_ref)]
    put_heads(turned[0], qs, 0)
    put_heads(turned[1], both_t.at[me_ref[1]], base)
    put_heads(turned[2], both_t.at[1 - me_ref[1]], base)
    put_heads(turned[0], qt_ref, 0)
    kt = both_t.at[0]
    flipped = [contract_last(eye[...], both_t[1, h, pl.ds(base, BLK), :]).astype(jnp.bfloat16) for h in range(heads)]
    for h in range(heads):
        vt[h, :, pl.ds(base, BLK)] = flipped[h]

    @pl.when(c < WB - 1)
    def _():
        kx_ref[:, pl.ds(base, BLK), :] = kt[:, pl.ds(base, BLK), :]
        vx_ref[:, :, pl.ds(base, BLK)] = vt[:, :, pl.ds(base, BLK)]
        acc_ref[...] = jnp.zeros_like(acc_ref)
        floor = jnp.full(stat_ref.shape[1:], FLOOR, jnp.float32)
        stat_ref[0] = floor
        stat_ref[1] = jnp.zeros_like(floor)
        stat_ref[2] = floor

    @pl.when(c >= WB - 1)
    def _():
        start = pl.multiple_of((c - (WB - 1)) * BLK, BLK)
        here = me_ref[0] * own + c
        shut = [jnp.where(table_ref[j, here] > 0, 0.0, FLOOR) for j in range(CAP)]
        far_at = [pl.multiple_of(table_ref[spans * CAP + j, here] * BLK, BLK) for j in range(CAP)]
        causal = diag[...]
        for group in range(0, heads, STRIDE):
            found = []
            for h in range(group, group + STRIDE):
                q = qs[h]
                near = near_scores(contract_last(kt[h, pl.ds(start, WB * BLK), :], q), causal)
                far = [contract_last(kt[h, pl.ds(at, BLK), :], q) for at in far_at]
                top, w, total = softmax_blocks(near, [None] * WB)
                part = mix(vt[h, :, pl.ds(start, WB * BLK)], w)
                far_top, far_w, far_total = softmax_blocks(far, shut)
                far_v = jnp.concatenate([vt[h, :, pl.ds(at, BLK)] for at in far_at], axis=1)
                far_part = mix(far_v, far_w)
                both = jnp.maximum(top, far_top)
                a = jnp.exp2(top - both)
                b = jnp.exp2(far_top - both)
                found.append((part * a + far_part * b, both, total * a + far_total * b, far_top))
            for h, (part, *rows) in enumerate(found, group):
                acc_ref[h] = part
                for n, row in enumerate(rows):
                    stat_ref[n, h : h + 1, :] = row


def first(me, table, q, mine, other, heads, spans):
    tokens = q.shape[0] // heads
    width = q.shape[1]
    own = tokens // BLK
    raw = pl.BlockSpec((BLK * heads, width), lambda c, *_: (c, 0))
    grid_spec = pltpu.PrefetchScalarGridSpec(
        num_scalar_prefetch=2,
        grid=(own,),
        in_specs=[raw, raw, raw],
        out_specs=[
            pl.BlockSpec((heads, BLK, width), lambda c, *_: (0, c, 0)),
            pl.BlockSpec((heads, width, BLK), lambda c, *_: (0, 0, c)),
            pl.BlockSpec((3, heads, BLK), lambda c, *_: (0, 0, c)),
            pl.BlockSpec((heads, RIM, width), lambda c, *_: (0, 0, 0)),
            pl.BlockSpec((heads, width, RIM), lambda c, *_: (0, 0, 0)),
        ],
        scratch_shapes=[
            pltpu.VMEM((2, heads, tokens, width), jnp.bfloat16),
            pltpu.VMEM((heads, width, tokens), jnp.bfloat16),
            pltpu.VMEM((heads, BLK, width), jnp.bfloat16),
            pltpu.VMEM((TILE, TILE), jnp.bfloat16),
            pltpu.VMEM((width, width), jnp.bfloat16),
            pltpu.VMEM((BLK, BLK), jnp.float32),
        ],
    )
    return pl.pallas_call(
        functools.partial(first_kernel, spans),
        grid_spec=grid_spec,
        out_shape=[
            jax.ShapeDtypeStruct((heads, tokens, width), jnp.bfloat16),
            jax.ShapeDtypeStruct((heads, width, tokens), jnp.float32),
            jax.ShapeDtypeStruct((3, heads, tokens), jnp.float32),
            jax.ShapeDtypeStruct((heads, RIM, width), jnp.bfloat16),
            jax.ShapeDtypeStruct((heads, width, RIM), jnp.bfloat16),
        ],
        compiler_params=pltpu.CompilerParams(vmem_limit_bytes=VMEM_BYTES),
        cost_estimate=SMALL,
        name="first",
    )(me, table, q, mine, other)


def take_halves(me_ref, mine_ref, other_ref, base, both_t, vt):
    heads, width = vt.shape[:2]
    turn = split_order(heads)
    turned = [chunk_pairs(ref[...], turn) for ref in (mine_ref, other_ref)]
    put_heads(turned[0], both_t.at[me_ref[1]], base)
    put_heads(turned[1], both_t.at[1 - me_ref[1]], base)
    eye = unit(width)
    span = slice(base, base + mine_ref.shape[0] // heads)
    flipped = [contract_last(eye, both_t[1, h, span, :]).astype(jnp.bfloat16) for h in range(heads)]
    for h in range(heads):
        vt[h, :, span] = flipped[h]


def finish(done_t, order, out_ref):
    heads, _, rows = done_t.shape
    step = TILE // heads
    eye = unit(rows)
    done = [contract_last(eye, done_t[h]).astype(jnp.bfloat16) for h in range(heads)]
    ordered = jnp.concatenate([d[i : i + step, :] for i in range(0, rows, step) for d in done], axis=0)
    turned = chunk_pairs(ordered, order)
    for i, chunk in enumerate(turned):
        out_ref[i * TILE : (i + 1) * TILE, :] = chunk


def far_kernel(bys, own, last, me_ref, table_ref, q_ref, *rest):
    halves, rest = rest[: 2 * len(bys)], rest[2 * len(bys) :]
    acc_in, stat_in, *rest = rest
    if last:
        out_ref, *rest = rest
    else:
        acc_ref, stat_ref, *rest = rest
    both_t, vt, scores_a, scores_b, tops_a, tops_b, *rest = rest
    if last:
        order, done_t = rest
    heads, rows, _ = q_ref.shape
    i = pl.program_id(0)

    @pl.when(i == 0)
    def _():
        for n in range(len(bys)):
            take_halves(me_ref, halves[2 * n], halves[2 * n + 1], n * CAP * BLK, both_t, vt)
        if last:
            order[...] = join_order(heads)

    here = me_ref[0] * own + i * (rows // BLK)
    shut = []
    for by in bys:
        for j in range(CAP):
            row = [jnp.where(table_ref[by * CAP + j, here + a] > 0, 0.0, FLOOR) for a in range(rows // BLK)]
            shut.append(jnp.concatenate([jnp.full((1, BLK), closed, jnp.float32) for closed in row], axis=1))

    def fill(h, query, scores, tops):
        for j in range(len(shut)):
            block = contract_last(both_t[0, h, j * BLK : (j + 1) * BLK, :], query)
            tops[j : j + 1, :] = jnp.max(block, axis=0, keepdims=True)
            scores[j * BLK : (j + 1) * BLK, :] = block

    def use(h, before, stats, scores, tops):
        top, total, far_top = stats
        for j, closed in enumerate(shut):
            far_top = jnp.maximum(far_top, tops[j : j + 1, :] * SCALE + closed)
        weights, far_total = [], 0.0
        for j, closed in enumerate(shut):
            base = jnp.where(closed < 0.0, -FLOOR, far_top)
            w = jnp.exp2(scores[j * BLK : (j + 1) * BLK, :] * SCALE - base)
            far_total = far_total + jnp.sum(w, axis=0, keepdims=True)
            weights.append(w.astype(jnp.bfloat16))
        both = jnp.maximum(top, far_top)
        a = jnp.exp2(top - both)
        b = jnp.exp2(far_top - both)
        total = total * a + far_total * b
        part = before * a + mix(vt[h], jnp.concatenate(weights, axis=0)) * b
        return part, (both, total, far_top)

    def keep(h, part, stats):
        if last:
            done_t[h] = (part * (1.0 / stats[1])).astype(jnp.bfloat16)
        else:
            acc_ref[h] = part
            for n, row in enumerate(stats):
                stat_ref[n, pl.ds(h, 1), :] = row

    fill(0, q_ref[0], scores_a, tops_a)

    def two_heads(n, carry):
        h = 2 * n
        later = jnp.minimum(h + 2, heads - 1)
        second, third = q_ref[h + 1], q_ref[later]
        before = acc_in[h], acc_in[h + 1]
        stats = [[stat_in[n, pl.ds(g, 1), :] for n in range(3)] for g in (h, h + 1)]
        fill(h + 1, second, scores_b, tops_b)
        one = use(h, before[0], stats[0], scores_a, tops_a)
        fill(later, third, scores_a, tops_a)
        two = use(h + 1, before[1], stats[1], scores_b, tops_b)
        keep(h, *one)
        keep(h + 1, *two)
        return carry

    lax.fori_loop(0, heads // 2, two_heads, 0)
    if last:
        finish(done_t, order[...], out_ref)


def far(bys, me, table, qt, halves, acc, stat, last):
    heads, tokens, width = qt.shape
    rows = min(TILE, tokens)
    keys = len(bys) * CAP * BLK
    parts = pl.BlockSpec((heads, width, rows), lambda i, *_: (0, 0, i))
    stats = pl.BlockSpec((3, heads, rows), lambda i, *_: (0, 0, i))
    whole = pl.BlockSpec(halves[0].shape, lambda i, *_: (0, 0))
    out_specs = [parts, stats]
    out_shape = [
        jax.ShapeDtypeStruct(acc.shape, acc.dtype),
        jax.ShapeDtypeStruct(stat.shape, stat.dtype),
    ]
    scratch = [
        pltpu.VMEM((2, heads, keys, width), jnp.bfloat16),
        pltpu.VMEM((heads, width, keys), jnp.bfloat16),
        pltpu.VMEM((keys, rows), jnp.float32),
        pltpu.VMEM((keys, rows), jnp.float32),
        pltpu.VMEM((keys // BLK, rows), jnp.float32),
        pltpu.VMEM((keys // BLK, rows), jnp.float32),
    ]
    aliases = {3 + len(halves): 0, 4 + len(halves): 1}
    if last:
        out_specs = [pl.BlockSpec((rows * heads, width), lambda i, *_: (i, 0))]
        out_shape = [jax.ShapeDtypeStruct((tokens * heads, width), jnp.bfloat16)]
        scratch += [pltpu.VMEM((TILE, TILE), jnp.bfloat16), pltpu.VMEM((heads, width, rows), jnp.bfloat16)]
        aliases = {}
    grid_spec = pltpu.PrefetchScalarGridSpec(
        num_scalar_prefetch=2,
        grid=(tokens // rows,),
        in_specs=[pl.BlockSpec((heads, rows, width), lambda i, *_: (0, i, 0))] + [whole] * len(halves) + [parts, stats],
        out_specs=out_specs,
        scratch_shapes=scratch,
    )
    return pl.pallas_call(
        functools.partial(far_kernel, bys, tokens // BLK, last),
        grid_spec=grid_spec,
        out_shape=out_shape,
        input_output_aliases=aliases,
        compiler_params=pltpu.CompilerParams(vmem_limit_bytes=VMEM_BYTES),
        cost_estimate=SMALL,
        name="far",
    )(me, table, qt, *halves, acc, stat)


def rim_kernel(me_ref, q_ref, mine_ref, other_ref, kx_ref, vx_ref, acc_in, stat_in, acc_ref, stat_ref, both_t, vt, diag):
    heads = q_ref.shape[0]
    c = pl.program_id(0)

    @pl.when(c == 0)
    def _():
        take_halves(me_ref, mine_ref, other_ref, 0, both_t, vt)
        both_t[0, :, RIM:, :] = kx_ref[...]
        vt[:, :, RIM:] = vx_ref[...]
        diag[...] = causal_bias()

    start = pl.multiple_of(c * BLK, BLK)
    causal = diag[...]
    shut = [jnp.where((c + b >= WB - 1) | (me_ref[0] > 0), 0.0, FLOOR) for b in range(WB - 1)] + [None]
    for group in range(0, heads, STRIDE):
        found = []
        for h in range(group, group + STRIDE):
            near = near_scores(contract_last(both_t[0, h, pl.ds(start, WB * BLK), :], q_ref[h]), causal)
            near_top, w, near_total = softmax_blocks(near, shut)
            top = stat_in[0, h : h + 1, :]
            both = jnp.maximum(top, near_top)
            a = jnp.exp2(top - both)
            b = jnp.exp2(near_top - both)
            total = stat_in[1, h : h + 1, :] * a + near_total * b
            part = acc_in[h] * a + mix(vt[h, :, pl.ds(start, WB * BLK)], w) * b
            found.append((part, both, total, stat_in[2, h : h + 1, :]))
        for h, (part, *rows) in enumerate(found, group):
            acc_ref[h] = part
            for n, row in enumerate(rows):
                stat_ref[n, h : h + 1, :] = row


def rim(me, qt, mine, other, kx, vx, acc, stat):
    heads, tokens, width = qt.shape
    parts = pl.BlockSpec((heads, width, BLK), lambda i, *_: (0, 0, i))
    stats = pl.BlockSpec((3, heads, BLK), lambda i, *_: (0, 0, i))
    grid_spec = pltpu.PrefetchScalarGridSpec(
        num_scalar_prefetch=1,
        grid=(WB - 1,),
        in_specs=[
            pl.BlockSpec((heads, BLK, width), lambda i, *_: (0, i, 0)),
            pl.BlockSpec(mine.shape, lambda i, *_: (0, 0)),
            pl.BlockSpec(mine.shape, lambda i, *_: (0, 0)),
            pl.BlockSpec(kx.shape, lambda i, *_: (0, 0, 0)),
            pl.BlockSpec(vx.shape, lambda i, *_: (0, 0, 0)),
            parts,
            stats,
        ],
        out_specs=[parts, stats],
        scratch_shapes=[
            pltpu.VMEM((2, heads, 2 * RIM, width), jnp.bfloat16),
            pltpu.VMEM((heads, width, 2 * RIM), jnp.bfloat16),
            pltpu.VMEM((BLK, BLK), jnp.float32),
        ],
    )
    return pl.pallas_call(
        rim_kernel,
        grid_spec=grid_spec,
        out_shape=[
            jax.ShapeDtypeStruct(acc.shape, acc.dtype),
            jax.ShapeDtypeStruct(stat.shape, stat.dtype),
        ],
        input_output_aliases={6: 0, 7: 1},
        compiler_params=pltpu.CompilerParams(vmem_limit_bytes=VMEM_BYTES),
        cost_estimate=SMALL,
        name="rim",
    )(me, qt, mine, other, kx, vx, acc, stat)


def other_core(x):
    return lax.ppermute(x, "rep", [(0, 1), (1, 0)])


def ahead(x, by):
    count = lax.axis_size("ctx")
    return lax.ppermute(x, "ctx", [(i, i + by) for i in range(count - by)])


def local(queries, keys_values, far_list, far_count):
    tokens, heads, _, width = queries.shape
    spans = lax.axis_size("ctx")
    me = jnp.stack([lax.axis_index("ctx"), lax.axis_index("rep")]).astype(jnp.int32)
    q = queries.reshape(tokens * heads, width)
    kv = keys_values.reshape(tokens * heads, width)
    other = other_core(kv)
    table, *pools, edge = route(me, far_list, far_count, kv, spans)
    edge = ahead(edge, 1)
    pieces = [ahead(pool, by) for by, pool in reversed(list(enumerate(pools, 1)))]
    qt, acc, stat, kx, vx = first(me, table, q, kv, other, heads, spans)
    *early, edge, stat = lax.optimization_barrier((*pieces[:-1], edge, stat))
    acc, stat = rim(me, qt, edge, other_core(edge), kx, vx, acc, stat)
    bys = list(range(spans - 1, 1, -1))
    others = [other_core(piece) for piece in early]
    for n in range(0, len(bys), GROUP):
        halves = [half for pair in zip(early[n : n + GROUP], others[n : n + GROUP]) for half in pair]
        acc, stat = far(bys[n : n + GROUP], me, table, qt, halves, acc, stat, False)
    late, stat = lax.optimization_barrier((pieces[-1], stat))
    (done,) = far([1], me, table, qt, [late, other_core(late)], acc, stat, True)
    return done.reshape(queries.shape)


def solution(mesh):
    in_specs = (
        P(("groups", "ctx"), "head", "rep", None),
        P("rep", ("groups", "ctx"), "head", None),
        P("groups", None),
        P("groups"),
    )
    out_specs = P(("groups", "ctx"), "head", "rep", None)
    return jax.shard_map(local, mesh=mesh, in_specs=in_specs, out_specs=out_specs, check_vma=False)
```

```python
import functools
import math

import jax
import jax.numpy as jnp
from jax import lax
from jax.experimental import pallas as pl
from jax.experimental.pallas import tpu as pltpu
from jax.sharding import PartitionSpec as P

BLK = 128
WB = 4
CAP = 2
RIM = (WB - 1) * BLK
TILE = 256
GROUP = 3
STATS = 4
STRIDE = 2

FLOOR = -1.0e30
SCALE = math.log2(math.e) / 12.0
NONE = 1.0e6
VMEM_BYTES = 48 * 1024 * 1024
SMALL = pl.CostEstimate(flops=1024, bytes_accessed=1024, transcendentals=0)


def contract_last(a, b):
    return lax.dot_general(a, b, (((1,), (1,)), ((), ())), preferred_element_type=jnp.float32)


def mix(a, b):
    return jnp.dot(a, b, preferred_element_type=jnp.float32)


def unit(n):
    row = lax.broadcasted_iota(jnp.int32, (n, n), 0)
    col = lax.broadcasted_iota(jnp.int32, (n, n), 1)
    return (row == col).astype(jnp.float32).astype(jnp.bfloat16)


def causal_bias():
    key = lax.broadcasted_iota(jnp.int32, (BLK, BLK), 0)
    query = lax.broadcasted_iota(jnp.int32, (BLK, BLK), 1)
    return jnp.where(key <= query, 0.0, FLOOR)


def softmax_blocks(scores, shut, top=None):
    for block, closed in zip(scores, shut):
        block_top = jnp.max(block, axis=0, keepdims=True) * SCALE
        block_top = block_top if closed is None else block_top + closed
        top = block_top if top is None else jnp.maximum(top, block_top)
    weights, total = [], 0.0
    for block, closed in zip(scores, shut):
        base = top if closed is None else jnp.where(closed < 0.0, -FLOOR, top)
        w = jnp.exp2(block * SCALE - base)
        total = total + jnp.sum(w, axis=0, keepdims=True)
        weights.append(w.astype(jnp.bfloat16))
    return top, jnp.concatenate(weights, axis=0), total


def near_scores(scores, causal):
    blocks = [scores[b * BLK : (b + 1) * BLK, :] for b in range(WB)]
    return blocks[:-1] + [blocks[-1] + causal]


def split_order(heads):
    step = TILE // heads
    row = lax.broadcasted_iota(jnp.int32, (TILE, TILE), 0)
    col = lax.broadcasted_iota(jnp.int32, (TILE, TILE), 1)
    return (col == (row % step) * heads + row // step).astype(jnp.float32).astype(jnp.bfloat16)


def join_order(heads):
    step = TILE // heads
    row = lax.broadcasted_iota(jnp.int32, (TILE, TILE), 0)
    col = lax.broadcasted_iota(jnp.int32, (TILE, TILE), 1)
    return (col == (row % heads) * step + row // heads).astype(jnp.float32).astype(jnp.bfloat16)


def chunk_pairs(rows, order):
    turned = []
    for i in range(0, rows.shape[0], 2 * TILE):
        two = jnp.concatenate([rows[i : i + TILE, :], rows[i + TILE : i + 2 * TILE, :]], axis=1)
        two = mix(order, two).astype(jnp.bfloat16)
        turned += [two[:, : rows.shape[1]], two[:, rows.shape[1] :]]
    return turned


def put_heads(turned, dst, base):
    heads = dst.shape[0]
    step = TILE // heads
    for i, rows in enumerate(turned):
        dst[:, pl.ds(base + i * step, step), :] = rows.reshape(heads, step, rows.shape[-1])


def route_kernel(me_ref, list_ref, count_ref, kv_ref, table_ref, *rest):
    spans = table_ref.shape[0] // (2 * CAP)
    pools, rim_out, sem = rest[:-2], rest[-2], rest[-1]
    edge = pltpu.make_async_copy(
        kv_ref.at[pl.ds(kv_ref.shape[0] - rim_out.shape[0] * (WB - 1), rim_out.shape[0]), :],
        rim_out,
        sem.at[sem.shape[0] - 1],
    )
    edge.start()
    me = me_ref[0]
    listed = list_ref[...]
    entries, total = listed.shape
    own = total // spans
    slot = lax.broadcasted_iota(jnp.int32, (entries, total), 0)
    lane = lax.broadcasted_iota(jnp.int32, (entries, total), 1)
    counted = slot < count_ref[...]
    named = jnp.where(counted, listed.astype(jnp.float32), 2.0 * NONE)

    def pick(user, source):
        low = (source * own).astype(jnp.float32)
        mine = (lane >= user * own) & (lane < (user + 1) * own)
        left = jnp.where(mine & (named >= low) & (named < low + own), named, NONE)
        picked = []
        for _ in range(CAP):
            least = jnp.min(jnp.min(left, axis=0, keepdims=True), axis=1, keepdims=True)
            picked.append(least)
            left = jnp.where(left == least, NONE, left)
        return picked

    row_len = kv_ref.shape[0] // own
    sent = [block for by in range(1, spans) for block in pick(me + by, me)]
    copies = []
    for n, block in enumerate(sent):
        local = block - (me * own).astype(jnp.float32)
        local = jnp.max(jnp.where(local < own, local, 0.0)).astype(jnp.int32)
        start = pl.multiple_of(local * row_len, row_len)
        copy = pltpu.make_async_copy(
            kv_ref.at[pl.ds(start, row_len), :],
            pools[n // CAP].at[pl.ds(n % CAP * row_len, row_len), :],
            sem.at[n],
        )
        copies.append(copy)
    for copy in copies:
        copy.start()
    for by in range(spans):
        source = me - by
        for j, block in enumerate(pick(me, source)):
            used = jnp.max((named == block).astype(jnp.float32), axis=0, keepdims=True)
            local = block - (source * own).astype(jnp.float32)
            local = jnp.where(local < own, local, 0.0)
            row = by * CAP + j
            table_ref[row : row + 1, :] = used.astype(jnp.int32)
            ids = jnp.zeros((1, total), jnp.float32) + local
            table_ref[spans * CAP + row : spans * CAP + row + 1, :] = ids.astype(jnp.int32)
    for copy in copies:
        copy.wait()
    edge.wait()


def route(me, far_list, far_count, kv, spans):
    total = far_list.shape[0]
    rows = kv.shape[0] // (total // spans) * CAP
    pool = jax.ShapeDtypeStruct((rows, kv.shape[1]), kv.dtype)
    edge = jax.ShapeDtypeStruct((rows // CAP, kv.shape[1]), kv.dtype)
    grid_spec = pltpu.PrefetchScalarGridSpec(
        num_scalar_prefetch=1,
        grid=(1,),
        in_specs=[
            pl.BlockSpec(far_list.shape[::-1], lambda i, *_: (0, 0)),
            pl.BlockSpec((1, total), lambda i, *_: (0, 0)),
            pl.BlockSpec(memory_space=pltpu.HBM),
        ],
        out_specs=[pl.BlockSpec((2 * CAP * spans, total), lambda i, *_: (0, 0))]
        + [pl.BlockSpec(pool.shape, lambda i, *_: (0, 0))] * (spans - 1)
        + [pl.BlockSpec(edge.shape, lambda i, *_: (0, 0))],
        scratch_shapes=[pltpu.SemaphoreType.DMA(((spans - 1) * CAP + 1,))],
    )
    return pl.pallas_call(
        route_kernel,
        grid_spec=grid_spec,
        out_shape=[jax.ShapeDtypeStruct((2 * CAP * spans, total), jnp.int32)] + [pool] * (spans - 1) + [edge],
        cost_estimate=SMALL,
        name="route",
    )(me, far_list.T, far_count[None, :], kv)


def first_kernel(
    spans, me_ref, table_ref, q_ref, mine_ref, other_ref, qt_ref, acc_ref, stat_ref, both_t, vt, qs, order, eye, diag
):
    heads = qt_ref.shape[0]
    own = pl.num_programs(0)
    c = pl.program_id(0)

    @pl.when(c == 0)
    def _():
        order[...] = split_order(heads)
        eye[...] = unit(eye.shape[0])
        diag[...] = causal_bias()
        both_t[:, :, :RIM, :] = jnp.zeros((2, heads, RIM, both_t.shape[-1]), jnp.bfloat16)
        vt[:, :, :RIM] = jnp.zeros((heads, vt.shape[1], RIM), jnp.bfloat16)

    start = pl.multiple_of(c * BLK, BLK)
    base = pl.multiple_of(RIM + c * BLK, BLK)
    turn = order[...]
    turned = [chunk_pairs(ref[...], turn) for ref in (q_ref, mine_ref, other_ref)]
    put_heads(turned[0], qs, 0)
    put_heads(turned[1], both_t.at[me_ref[1]], base)
    put_heads(turned[2], both_t.at[1 - me_ref[1]], base)
    put_heads(turned[0], qt_ref, 0)
    kt = both_t.at[0]
    flipped = [contract_last(eye[...], both_t[1, h, pl.ds(base, BLK), :]).astype(jnp.bfloat16) for h in range(heads)]
    for h in range(heads):
        vt[h, :, pl.ds(base, BLK)] = flipped[h]

    here = me_ref[0] * own + c
    shut = [jnp.where(table_ref[j, here] > 0, 0.0, FLOOR) for j in range(CAP)]
    far_at = [
        pl.multiple_of(RIM + jnp.minimum(table_ref[spans * CAP + j, here], c) * BLK, BLK) for j in range(CAP)
    ]
    near_shut = [jnp.where(c + b >= WB - 1, 0.0, FLOOR) for b in range(WB - 1)] + [None]
    causal = diag[...]
    for group in range(0, heads, STRIDE):
        found = []
        for h in range(group, group + STRIDE):
            q = qs[h]
            near = near_scores(contract_last(kt[h, pl.ds(start, WB * BLK), :], q), causal)
            far = [contract_last(kt[h, pl.ds(at, BLK), :], q) for at in far_at]
            top, w, total = softmax_blocks(near, near_shut)
            part = mix(vt[h, :, pl.ds(start, WB * BLK)], w)
            far_top, far_w, far_total = softmax_blocks(far, shut)
            far_v = jnp.concatenate([vt[h, :, pl.ds(at, BLK)] for at in far_at], axis=1)
            far_part = mix(far_v, far_w)
            both = jnp.maximum(top, far_top)
            a = jnp.exp2(top - both)
            b = jnp.exp2(far_top - both)
            found.append((part * a + far_part * b, both, total * a + far_total * b, far_top, top))
        for h, (part, *rows) in enumerate(found, group):
            acc_ref[h] = part
            for n, row in enumerate(rows):
                stat_ref[n, h : h + 1, :] = row


def first(me, table, q, mine, other, heads, spans):
    tokens = q.shape[0] // heads
    width = q.shape[1]
    own = tokens // BLK
    raw = pl.BlockSpec((BLK * heads, width), lambda c, *_: (c, 0))
    grid_spec = pltpu.PrefetchScalarGridSpec(
        num_scalar_prefetch=2,
        grid=(own,),
        in_specs=[raw, raw, raw],
        out_specs=[
            pl.BlockSpec((heads, BLK, width), lambda c, *_: (0, c, 0)),
            pl.BlockSpec((heads, width, BLK), lambda c, *_: (0, 0, c)),
            pl.BlockSpec((STATS, heads, BLK), lambda c, *_: (0, 0, c)),
        ],
        scratch_shapes=[
            pltpu.VMEM((2, heads, RIM + tokens, width), jnp.bfloat16),
            pltpu.VMEM((heads, width, RIM + tokens), jnp.bfloat16),
            pltpu.VMEM((heads, BLK, width), jnp.bfloat16),
            pltpu.VMEM((TILE, TILE), jnp.bfloat16),
            pltpu.VMEM((width, width), jnp.bfloat16),
            pltpu.VMEM((BLK, BLK), jnp.float32),
        ],
    )
    return pl.pallas_call(
        functools.partial(first_kernel, spans),
        grid_spec=grid_spec,
        out_shape=[
            jax.ShapeDtypeStruct((heads, tokens, width), jnp.bfloat16),
            jax.ShapeDtypeStruct((heads, width, tokens), jnp.float32),
            jax.ShapeDtypeStruct((STATS, heads, tokens), jnp.float32),
        ],
        compiler_params=pltpu.CompilerParams(vmem_limit_bytes=VMEM_BYTES),
        cost_estimate=SMALL,
        name="first",
    )(me, table, q, mine, other)


def take_halves(me_ref, mine_ref, other_ref, base, both_t, vt):
    heads, width = vt.shape[:2]
    turn = split_order(heads)
    turned = [chunk_pairs(ref[...], turn) for ref in (mine_ref, other_ref)]
    put_heads(turned[0], both_t.at[me_ref[1]], base)
    put_heads(turned[1], both_t.at[1 - me_ref[1]], base)
    eye = unit(width)
    span = slice(base, base + mine_ref.shape[0] // heads)
    flipped = [contract_last(eye, both_t[1, h, span, :]).astype(jnp.bfloat16) for h in range(heads)]
    for h in range(heads):
        vt[h, :, span] = flipped[h]


def finish(done, order, out_ref):
    heads, rows, _ = done.shape
    step = TILE // heads
    ordered = jnp.concatenate([done[h, i : i + step, :] for i in range(0, rows, step) for h in range(heads)], axis=0)
    for i, chunk in enumerate(chunk_pairs(ordered, order)):
        out_ref[i * TILE : (i + 1) * TILE, :] = chunk


def result(part, total):
    return jnp.transpose(part * (1.0 / total)).astype(jnp.bfloat16)


def far_kernel(bys, own, last, me_ref, table_ref, q_ref, *rest):
    halves, rest = rest[: 2 * len(bys)], rest[2 * len(bys) :]
    acc_in, stat_in, acc_ref, stat_ref, *rest = rest
    if last:
        out_ref, *rest = rest
    both_t, vt, scores_a, scores_b, tops_a, tops_b, *rest = rest
    if last:
        order, done = rest
    heads, rows, _ = q_ref.shape
    i = pl.program_id(0)

    @pl.when(i == 0)
    def _():
        for n in range(len(bys)):
            take_halves(me_ref, halves[2 * n], halves[2 * n + 1], n * CAP * BLK, both_t, vt)
        if last:
            order[...] = join_order(heads)

    here = me_ref[0] * own + i * (rows // BLK)
    shut = []
    for by in bys:
        for j in range(CAP):
            row = [jnp.where(table_ref[by * CAP + j, here + a] > 0, 0.0, FLOOR) for a in range(rows // BLK)]
            shut.append(jnp.concatenate([jnp.full((1, BLK), closed, jnp.float32) for closed in row], axis=1))

    def fill(h, query, scores, tops):
        found = contract_last(both_t[0, h], query)
        for j in range(len(shut)):
            block = found[j * BLK : (j + 1) * BLK, :]
            tops[j : j + 1, :] = jnp.max(block, axis=0, keepdims=True)
            scores[j * BLK : (j + 1) * BLK, :] = block

    def use(h, before, stats, scores, tops):
        top, total, far_top, near_top = stats
        for j, closed in enumerate(shut):
            far_top = jnp.maximum(far_top, tops[j : j + 1, :] * SCALE + closed)
        weights, far_total = [], 0.0
        for j, closed in enumerate(shut):
            base = jnp.where(closed < 0.0, -FLOOR, far_top)
            w = jnp.exp2(scores[j * BLK : (j + 1) * BLK, :] * SCALE - base)
            far_total = far_total + jnp.sum(w, axis=0, keepdims=True)
            weights.append(w.astype(jnp.bfloat16))
        both = jnp.maximum(top, far_top)
        a = jnp.exp2(top - both)
        b = jnp.exp2(far_top - both)
        total = total * a + far_total * b
        part = before * a + mix(vt[h], jnp.concatenate(weights, axis=0)) * b
        return part, (both, total, far_top, near_top)

    def keep(h, part, stats):
        if last:
            done[h] = result(part, stats[1])

        @pl.when((i * rows < RIM) | (not last))
        def _():
            acc_ref[h] = part
            for n, row in enumerate(stats):
                stat_ref[n, pl.ds(h, 1), :] = row

    fill(0, q_ref[0], scores_a, tops_a)

    def two_heads(n, carry):
        h = 2 * n
        later = jnp.minimum(h + 2, heads - 1)
        second, third = q_ref[h + 1], q_ref[later]
        before = acc_in[h], acc_in[h + 1]
        stats = [[stat_in[n, pl.ds(g, 1), :] for n in range(STATS)] for g in (h, h + 1)]
        fill(h + 1, second, scores_b, tops_b)
        one = use(h, before[0], stats[0], scores_a, tops_a)
        fill(later, third, scores_a, tops_a)
        two = use(h + 1, before[1], stats[1], scores_b, tops_b)
        keep(h, *one)
        keep(h + 1, *two)
        return carry

    lax.fori_loop(0, heads // 2, two_heads, 0)
    if last:
        finish(done, order[...], out_ref)


def far(bys, me, table, qt, halves, acc, stat, last):
    heads, tokens, width = qt.shape
    rows = min(TILE, tokens)
    keys = len(bys) * CAP * BLK
    kept = (RIM - 1) // rows if last else tokens // rows
    parts = pl.BlockSpec((heads, width, rows), lambda i, *_: (0, 0, i))
    stats = pl.BlockSpec((STATS, heads, rows), lambda i, *_: (0, 0, i))
    whole = pl.BlockSpec(halves[0].shape, lambda i, *_: (0, 0))
    out_specs = [
        pl.BlockSpec((heads, width, rows), lambda i, *_: (0, 0, jnp.minimum(i, kept))),
        pl.BlockSpec((STATS, heads, rows), lambda i, *_: (0, 0, jnp.minimum(i, kept))),
    ]
    out_shape = [
        jax.ShapeDtypeStruct(acc.shape, acc.dtype),
        jax.ShapeDtypeStruct(stat.shape, stat.dtype),
    ]
    scratch = [
        pltpu.VMEM((2, heads, keys, width), jnp.bfloat16),
        pltpu.VMEM((heads, width, keys), jnp.bfloat16),
        pltpu.VMEM((keys, rows), jnp.float32),
        pltpu.VMEM((keys, rows), jnp.float32),
        pltpu.VMEM((keys // BLK, rows), jnp.float32),
        pltpu.VMEM((keys // BLK, rows), jnp.float32),
    ]
    if last:
        out_specs.append(pl.BlockSpec((rows * heads, width), lambda i, *_: (i, 0)))
        out_shape.append(jax.ShapeDtypeStruct((tokens * heads, width), jnp.bfloat16))
        scratch += [pltpu.VMEM((TILE, TILE), jnp.bfloat16), pltpu.VMEM((heads, rows, width), jnp.bfloat16)]
    grid_spec = pltpu.PrefetchScalarGridSpec(
        num_scalar_prefetch=2,
        grid=(tokens // rows,),
        in_specs=[pl.BlockSpec((heads, rows, width), lambda i, *_: (0, i, 0))] + [whole] * len(halves) + [parts, stats],
        out_specs=out_specs,
        scratch_shapes=scratch,
    )
    return pl.pallas_call(
        functools.partial(far_kernel, bys, tokens // BLK, last),
        grid_spec=grid_spec,
        out_shape=out_shape,
        input_output_aliases={3 + len(halves): 0, 4 + len(halves): 1},
        compiler_params=pltpu.CompilerParams(vmem_limit_bytes=VMEM_BYTES),
        cost_estimate=SMALL,
        name="far",
    )(me, table, qt, *halves, acc, stat)


def rim_kernel(
    me_ref, q_ref, edge_mine, edge_other, tip_mine, tip_other, acc_in, stat_in, out_in, out_ref, both_t, vt, order, done
):
    heads = q_ref.shape[0]
    c = pl.program_id(0)

    @pl.when(c == 0)
    def _():
        take_halves(me_ref, edge_mine, edge_other, 0, both_t, vt)
        take_halves(me_ref, tip_mine, tip_other, BLK, both_t, vt)
        order[...] = join_order(heads)

    for first_block in range(WB - 1):

        @pl.when(c == first_block)
        def _(first_block=first_block):
            blocks = range(first_block, WB - 1)
            shut = [jnp.where(me_ref[0] > 0, 0.0, FLOOR)] * len(blocks)
            span = slice(first_block * BLK, RIM)
            for h in range(heads):
                found = contract_last(both_t[0, h, span, :], q_ref[h])
                near = [found[n * BLK : (n + 1) * BLK, :] for n in range(len(blocks))]
                near_top, w, near_total = softmax_blocks(near, shut, stat_in[3, h : h + 1, :])
                top = stat_in[0, h : h + 1, :]
                both = jnp.maximum(top, near_top)
                a = jnp.exp2(top - both)
                b = jnp.exp2(near_top - both)
                total = stat_in[1, h : h + 1, :] * a + near_total * b
                done[h] = result(acc_in[h] * a + mix(vt[h, :, span], w) * b, total)

    finish(done, order[...], out_ref)


def rim(me, qt, halves, acc, stat, out):
    heads, tokens, width = qt.shape
    grid_spec = pltpu.PrefetchScalarGridSpec(
        num_scalar_prefetch=1,
        grid=(WB - 1,),
        in_specs=[pl.BlockSpec((heads, BLK, width), lambda i, *_: (0, i, 0))]
        + [pl.BlockSpec(half.shape, lambda i, *_: (0, 0)) for half in halves]
        + [
            pl.BlockSpec((heads, width, BLK), lambda i, *_: (0, 0, i)),
            pl.BlockSpec((STATS, heads, BLK), lambda i, *_: (0, 0, i)),
            pl.BlockSpec(memory_space=pl.ANY),
        ],
        out_specs=pl.BlockSpec((BLK * heads, width), lambda i, *_: (i, 0)),
        scratch_shapes=[
            pltpu.VMEM((2, heads, RIM, width), jnp.bfloat16),
            pltpu.VMEM((heads, width, RIM), jnp.bfloat16),
            pltpu.VMEM((TILE, TILE), jnp.bfloat16),
            pltpu.VMEM((heads, BLK, width), jnp.bfloat16),
        ],
    )
    return pl.pallas_call(
        rim_kernel,
        grid_spec=grid_spec,
        out_shape=jax.ShapeDtypeStruct(out.shape, out.dtype),
        input_output_aliases={4 + len(halves): 0},
        compiler_params=pltpu.CompilerParams(vmem_limit_bytes=VMEM_BYTES),
        cost_estimate=SMALL,
        name="rim",
    )(me, qt, *halves, acc, stat, out)


def other_core(x):
    return lax.ppermute(x, "rep", [(0, 1), (1, 0)])


def ahead(x, by):
    count = lax.axis_size("ctx")
    return lax.ppermute(x, "ctx", [(i, i + by) for i in range(count - by)])


def local(queries, keys_values, far_list, far_count):
    tokens, heads, _, width = queries.shape
    spans = lax.axis_size("ctx")
    me = jnp.stack([lax.axis_index("ctx"), lax.axis_index("rep")]).astype(jnp.int32)
    q = queries.reshape(tokens * heads, width)
    kv = keys_values.reshape(tokens * heads, width)
    tip = kv[(tokens - (WB - 2) * BLK) * heads :]
    far_count, tip = lax.optimization_barrier((far_count, tip))
    tip = ahead(tip, 1)
    other = other_core(kv)
    table, *pools, edge = route(me, far_list, far_count, kv, spans)
    pieces = [ahead(pool, by) for by, pool in enumerate(pools, 1)]
    edge = ahead(edge, 1)
    qt, acc, stat = first(me, table, q, kv, other, heads, spans)
    *pieces, tip, stat = lax.optimization_barrier((*pieces, tip, stat))
    others = [other_core(piece) for piece in pieces]
    tip_other = other_core(tip)
    bys = list(range(1, spans))
    for n in range(0, len(bys), GROUP):
        halves = [half for pair in zip(pieces[n : n + GROUP], others[n : n + GROUP]) for half in pair]
        acc, stat, *out = far(bys[n : n + GROUP], me, table, qt, halves, acc, stat, n + GROUP >= len(bys))
    edge, stat = lax.optimization_barrier((edge, stat))
    done = rim(me, qt, [edge, other_core(edge), tip, tip_other], acc, stat, out[0])
    return done.reshape(queries.shape)


def solution(mesh):
    in_specs = (
        P(("groups", "ctx"), "head", "rep", None),
        P("rep", ("groups", "ctx"), "head", None),
        P("groups", None),
        P("groups"),
    )
    out_specs = P(("groups", "ctx"), "head", "rep", None)
    return jax.shard_map(local, mesh=mesh, in_specs=in_specs, out_specs=out_specs, check_vma=False)
```

```python
import functools
import math

import jax
import jax.numpy as jnp
from jax import lax
from jax.experimental import pallas as pl
from jax.experimental.pallas import tpu as pltpu
from jax.sharding import PartitionSpec as P

BLK = 128
WB = 4
CAP = 2
RIM = (WB - 1) * BLK
TILE = 256
GROUP = 3
STATS = 4
STRIDE = 2

FLOOR = -1.0e30
SCALE = math.log2(math.e) / 12.0
NONE = 1.0e6
VMEM_BYTES = 48 * 1024 * 1024
SMALL = pl.CostEstimate(flops=1024, bytes_accessed=1024, transcendentals=0)


def contract_last(a, b):
    return lax.dot_general(a, b, (((1,), (1,)), ((), ())), preferred_element_type=jnp.float32)


def mix(a, b):
    return jnp.dot(a, b, preferred_element_type=jnp.float32)


def unit(n):
    row = lax.broadcasted_iota(jnp.int32, (n, n), 0)
    col = lax.broadcasted_iota(jnp.int32, (n, n), 1)
    return (row == col).astype(jnp.float32).astype(jnp.bfloat16)


def causal_bias():
    key = lax.broadcasted_iota(jnp.int32, (BLK, BLK), 0)
    query = lax.broadcasted_iota(jnp.int32, (BLK, BLK), 1)
    return jnp.where(key <= query, 0.0, FLOOR)


def softmax_blocks(scores, shut, top=None):
    for block, closed in zip(scores, shut):
        block_top = jnp.max(block, axis=0, keepdims=True) * SCALE
        block_top = block_top if closed is None else block_top + closed
        top = block_top if top is None else jnp.maximum(top, block_top)
    weights, total = [], 0.0
    for block, closed in zip(scores, shut):
        base = top if closed is None else jnp.where(closed < 0.0, -FLOOR, top)
        w = jnp.exp2(block * SCALE - base)
        total = total + jnp.sum(w, axis=0, keepdims=True)
        weights.append(w.astype(jnp.bfloat16))
    return top, jnp.concatenate(weights, axis=0), total


def near_scores(scores, causal):
    blocks = [scores[b * BLK : (b + 1) * BLK, :] for b in range(WB)]
    return blocks[:-1] + [blocks[-1] + causal]


def split_order(heads):
    step = TILE // heads
    row = lax.broadcasted_iota(jnp.int32, (TILE, TILE), 0)
    col = lax.broadcasted_iota(jnp.int32, (TILE, TILE), 1)
    source = (row & (step - 1)) * heads + (row >> (step.bit_length() - 1))
    return (col == source).astype(jnp.float32).astype(jnp.bfloat16)


def join_order(heads):
    step = TILE // heads
    row = lax.broadcasted_iota(jnp.int32, (TILE, TILE), 0)
    col = lax.broadcasted_iota(jnp.int32, (TILE, TILE), 1)
    source = (row & (heads - 1)) * step + (row >> (heads.bit_length() - 1))
    return (col == source).astype(jnp.float32).astype(jnp.bfloat16)


def chunk_pairs(rows, order):
    turned = []
    for i in range(0, rows.shape[0], 2 * TILE):
        two = jnp.concatenate([rows[i : i + TILE, :], rows[i + TILE : i + 2 * TILE, :]], axis=1)
        two = mix(order, two).astype(jnp.bfloat16)
        turned += [two[:, : rows.shape[1]], two[:, rows.shape[1] :]]
    return turned


def put_heads(turned, dst, base):
    heads = dst.shape[0]
    step = TILE // heads
    for i, rows in enumerate(turned):
        dst[:, pl.ds(base + i * step, step), :] = rows.reshape(heads, step, rows.shape[-1])


def route_kernel(me_ref, list_ref, count_ref, kv_ref, table_ref, *rest):
    spans = table_ref.shape[0] // (2 * CAP)
    pools, rim_out, sem = rest[:-2], rest[-2], rest[-1]
    edge = pltpu.make_async_copy(
        kv_ref.at[pl.ds(kv_ref.shape[0] - rim_out.shape[0] * (WB - 1), rim_out.shape[0]), :],
        rim_out,
        sem.at[sem.shape[0] - 1],
    )
    edge.start()
    me = me_ref[0]
    listed = list_ref[...]
    entries, total = listed.shape
    own = total // spans
    slot = lax.broadcasted_iota(jnp.int32, (entries, total), 0)
    lane = lax.broadcasted_iota(jnp.int32, (entries, total), 1)
    counted = slot < count_ref[...]
    named = jnp.where(counted, listed.astype(jnp.float32), 2.0 * NONE)

    def pick(user, source):
        low = (source * own).astype(jnp.float32)
        mine = (lane >= user * own) & (lane < (user + 1) * own)
        left = jnp.where(mine & (named >= low) & (named < low + own), named, NONE)
        picked = []
        for _ in range(CAP):
            least = jnp.min(jnp.min(left, axis=0, keepdims=True), axis=1, keepdims=True)
            picked.append(least)
            left = jnp.where(left == least, NONE, left)
        return picked

    row_len = kv_ref.shape[0] // own
    sent = [block for by in range(1, spans) for block in pick(me + by, me)]
    copies = []
    for n, block in enumerate(sent):
        local = block - (me * own).astype(jnp.float32)
        local = jnp.max(jnp.where(local < own, local, 0.0)).astype(jnp.int32)
        start = pl.multiple_of(local * row_len, row_len)
        copy = pltpu.make_async_copy(
            kv_ref.at[pl.ds(start, row_len), :],
            pools[n // CAP].at[pl.ds(n % CAP * row_len, row_len), :],
            sem.at[n],
        )
        copies.append(copy)
    for copy in copies:
        copy.start()
    for by in range(spans):
        source = me - by
        for j, block in enumerate(pick(me, source)):
            used = jnp.max((named == block).astype(jnp.float32), axis=0, keepdims=True)
            local = block - (source * own).astype(jnp.float32)
            local = jnp.where(local < own, local, 0.0)
            row = by * CAP + j
            table_ref[row : row + 1, :] = used.astype(jnp.int32)
            ids = jnp.zeros((1, total), jnp.float32) + local
            table_ref[spans * CAP + row : spans * CAP + row + 1, :] = ids.astype(jnp.int32)
    for copy in copies:
        copy.wait()
    edge.wait()


def route(me, far_list, far_count, kv, spans):
    total = far_list.shape[0]
    rows = kv.shape[0] // (total // spans) * CAP
    pool = jax.ShapeDtypeStruct((rows, kv.shape[1]), kv.dtype)
    edge = jax.ShapeDtypeStruct((rows // CAP, kv.shape[1]), kv.dtype)
    grid_spec = pltpu.PrefetchScalarGridSpec(
        num_scalar_prefetch=1,
        grid=(1,),
        in_specs=[
            pl.BlockSpec(far_list.shape[::-1], lambda i, *_: (0, 0)),
            pl.BlockSpec((1, total), lambda i, *_: (0, 0)),
            pl.BlockSpec(memory_space=pltpu.HBM),
        ],
        out_specs=[pl.BlockSpec((2 * CAP * spans, total), lambda i, *_: (0, 0))]
        + [pl.BlockSpec(pool.shape, lambda i, *_: (0, 0))] * (spans - 1)
        + [pl.BlockSpec(edge.shape, lambda i, *_: (0, 0))],
        scratch_shapes=[pltpu.SemaphoreType.DMA(((spans - 1) * CAP + 1,))],
    )
    return pl.pallas_call(
        route_kernel,
        grid_spec=grid_spec,
        out_shape=[jax.ShapeDtypeStruct((2 * CAP * spans, total), jnp.int32)] + [pool] * (spans - 1) + [edge],
        cost_estimate=SMALL,
        name="route",
    )(me, far_list.T, far_count[None, :], kv)


def first_kernel(
    spans, me_ref, table_ref, q_ref, mine_ref, other_ref, qt_ref, acc_ref, stat_ref, both_t, vt, qs, order, eye, diag
):
    heads = qt_ref.shape[0]
    own = pl.num_programs(0)
    c = pl.program_id(0)

    @pl.when(c == 0)
    def _():
        order[...] = split_order(heads)
        eye[...] = unit(eye.shape[0])
        diag[...] = causal_bias()
        both_t[:, :, :RIM, :] = jnp.zeros((2, heads, RIM, both_t.shape[-1]), jnp.bfloat16)
        vt[:, :, :RIM] = jnp.zeros((heads, vt.shape[1], RIM), jnp.bfloat16)

    start = pl.multiple_of(c * BLK, BLK)
    base = pl.multiple_of(RIM + c * BLK, BLK)
    turn = order[...]
    turned = [chunk_pairs(ref[...], turn) for ref in (q_ref, mine_ref, other_ref)]
    put_heads(turned[0], qs, 0)
    put_heads(turned[1], both_t.at[me_ref[1]], base)
    put_heads(turned[2], both_t.at[1 - me_ref[1]], base)
    put_heads(turned[0], qt_ref, 0)
    kt = both_t.at[0]
    flipped = [contract_last(eye[...], both_t[1, h, pl.ds(base, BLK), :]).astype(jnp.bfloat16) for h in range(heads)]
    for h in range(heads):
        vt[h, :, pl.ds(base, BLK)] = flipped[h]

    here = me_ref[0] * own + c
    shut = [jnp.where(table_ref[j, here] > 0, 0.0, FLOOR) for j in range(CAP)]
    far_at = [
        pl.multiple_of(RIM + jnp.minimum(table_ref[spans * CAP + j, here], c) * BLK, BLK) for j in range(CAP)
    ]
    near_shut = [jnp.where(c + b >= WB - 1, 0.0, FLOOR) for b in range(WB - 1)] + [None]
    causal = diag[...]
    for group in range(0, heads, STRIDE):
        found = []
        for h in range(group, group + STRIDE):
            q = qs[h]
            near = near_scores(contract_last(kt[h, pl.ds(start, WB * BLK), :], q), causal)
            far = [contract_last(kt[h, pl.ds(at, BLK), :], q) for at in far_at]
            top, w, total = softmax_blocks(near, near_shut)
            part = mix(vt[h, :, pl.ds(start, WB * BLK)], w)
            far_top, far_w, far_total = softmax_blocks(far, shut)
            far_v = jnp.concatenate([vt[h, :, pl.ds(at, BLK)] for at in far_at], axis=1)
            far_part = mix(far_v, far_w)
            both = jnp.maximum(top, far_top)
            a = jnp.exp2(top - both)
            b = jnp.exp2(far_top - both)
            found.append((part * a + far_part * b, both, total * a + far_total * b, far_top, top))
        for h, (part, *rows) in enumerate(found, group):
            acc_ref[h] = part
            for n, row in enumerate(rows):
                stat_ref[n, h : h + 1, :] = row


def first(me, table, q, mine, other, heads, spans):
    tokens = q.shape[0] // heads
    width = q.shape[1]
    own = tokens // BLK
    raw = pl.BlockSpec((BLK * heads, width), lambda c, *_: (c, 0))
    grid_spec = pltpu.PrefetchScalarGridSpec(
        num_scalar_prefetch=2,
        grid=(own,),
        in_specs=[raw, raw, raw],
        out_specs=[
            pl.BlockSpec((heads, BLK, width), lambda c, *_: (0, c, 0)),
            pl.BlockSpec((heads, width, BLK), lambda c, *_: (0, 0, c)),
            pl.BlockSpec((STATS, heads, BLK), lambda c, *_: (0, 0, c)),
        ],
        scratch_shapes=[
            pltpu.VMEM((2, heads, RIM + tokens, width), jnp.bfloat16),
            pltpu.VMEM((heads, width, RIM + tokens), jnp.bfloat16),
            pltpu.VMEM((heads, BLK, width), jnp.bfloat16),
            pltpu.VMEM((TILE, TILE), jnp.bfloat16),
            pltpu.VMEM((width, width), jnp.bfloat16),
            pltpu.VMEM((BLK, BLK), jnp.float32),
        ],
    )
    return pl.pallas_call(
        functools.partial(first_kernel, spans),
        grid_spec=grid_spec,
        out_shape=[
            jax.ShapeDtypeStruct((heads, tokens, width), jnp.bfloat16),
            jax.ShapeDtypeStruct((heads, width, tokens), jnp.float32),
            jax.ShapeDtypeStruct((STATS, heads, tokens), jnp.float32),
        ],
        compiler_params=pltpu.CompilerParams(vmem_limit_bytes=VMEM_BYTES),
        cost_estimate=SMALL,
        name="first",
    )(me, table, q, mine, other)


def take_halves(me_ref, mine_ref, other_ref, base, turn, both_t, vt):
    heads, width = vt.shape[:2]
    turned = [chunk_pairs(ref[...], turn) for ref in (mine_ref, other_ref)]
    put_heads(turned[0], both_t.at[me_ref[1]], base)
    put_heads(turned[1], both_t.at[1 - me_ref[1]], base)
    eye = unit(width)
    span = slice(base, base + mine_ref.shape[0] // heads)
    flipped = [contract_last(eye, both_t[1, h, span, :]).astype(jnp.bfloat16) for h in range(heads)]
    for h in range(heads):
        vt[h, :, span] = flipped[h]


def finish(done, order, out_ref):
    heads, rows, _ = done.shape
    step = TILE // heads
    ordered = jnp.concatenate([done[h, i : i + step, :] for i in range(0, rows, step) for h in range(heads)], axis=0)
    for i, chunk in enumerate(chunk_pairs(ordered, order)):
        out_ref[i * TILE : (i + 1) * TILE, :] = chunk


def result(part, total):
    return jnp.transpose(part * (1.0 / total)).astype(jnp.bfloat16)


def far_kernel(bys, own, last, me_ref, table_ref, q_ref, *rest):
    halves, rest = rest[: 2 * len(bys)], rest[2 * len(bys) :]
    acc_in, stat_in, *rest = rest
    if last:
        out_ref, *rest = rest
    else:
        acc_ref, stat_ref, *rest = rest
    both_t, vt, scores_a, scores_b, tops_a, tops_b, *rest = rest
    if last:
        order, done = rest
    heads, rows, _ = q_ref.shape
    i = pl.program_id(0)

    @pl.when(i == 0)
    def _():
        turn = split_order(heads)
        for n in range(len(bys)):
            take_halves(me_ref, halves[2 * n], halves[2 * n + 1], n * CAP * BLK, turn, both_t, vt)
        if last:
            order[...] = join_order(heads)

    here = me_ref[0] * own + i * (rows // BLK)
    shut = []
    for by in bys:
        for j in range(CAP):
            row = [jnp.where(table_ref[by * CAP + j, here + a] > 0, 0.0, FLOOR) for a in range(rows // BLK)]
            shut.append(jnp.concatenate([jnp.full((1, BLK), closed, jnp.float32) for closed in row], axis=1))

    def fill(h, query, scores, tops):
        found = contract_last(both_t[0, h], query)
        for j in range(len(shut)):
            block = found[j * BLK : (j + 1) * BLK, :]
            tops[j : j + 1, :] = jnp.max(block, axis=0, keepdims=True)
            scores[j * BLK : (j + 1) * BLK, :] = block

    def use(h, before, stats, scores, tops):
        top, total, far_top, near_top = stats
        for j, closed in enumerate(shut):
            far_top = jnp.maximum(far_top, tops[j : j + 1, :] * SCALE + closed)
        weights, far_total = [], 0.0
        for j, closed in enumerate(shut):
            base = jnp.where(closed < 0.0, -FLOOR, far_top)
            w = jnp.exp2(scores[j * BLK : (j + 1) * BLK, :] * SCALE - base)
            far_total = far_total + jnp.sum(w, axis=0, keepdims=True)
            weights.append(w.astype(jnp.bfloat16))
        both = jnp.maximum(top, far_top)
        a = jnp.exp2(top - both)
        b = jnp.exp2(far_top - both)
        total = total * a + far_total * b
        part = before * a + mix(vt[h], jnp.concatenate(weights, axis=0)) * b
        return part, (both, total, far_top, near_top)

    def keep(h, part, stats):
        if last:
            done[h] = result(part, stats[1])
        else:
            acc_ref[h] = part
            for n, row in enumerate(stats):
                stat_ref[n, pl.ds(h, 1), :] = row

    fill(0, q_ref[0], scores_a, tops_a)

    def two_heads(n, carry):
        h = 2 * n
        later = jnp.minimum(h + 2, heads - 1)
        second, third = q_ref[h + 1], q_ref[later]
        before = acc_in[h], acc_in[h + 1]
        stats = [[stat_in[n, pl.ds(g, 1), :] for n in range(STATS)] for g in (h, h + 1)]
        fill(h + 1, second, scores_b, tops_b)
        one = use(h, before[0], stats[0], scores_a, tops_a)
        fill(later, third, scores_a, tops_a)
        two = use(h + 1, before[1], stats[1], scores_b, tops_b)
        keep(h, *one)
        keep(h + 1, *two)
        return carry

    lax.fori_loop(0, heads // 2, two_heads, 0)
    if last:
        finish(done, order[...], out_ref)


def far(bys, me, table, qt, halves, acc, stat, last):
    heads, tokens, width = qt.shape
    rows = min(TILE, tokens)
    keys = len(bys) * CAP * BLK
    parts = pl.BlockSpec((heads, width, rows), lambda i, *_: (0, 0, i))
    stats = pl.BlockSpec((STATS, heads, rows), lambda i, *_: (0, 0, i))
    whole = pl.BlockSpec(halves[0].shape, lambda i, *_: (0, 0))
    scratch = [
        pltpu.VMEM((2, heads, keys, width), jnp.bfloat16),
        pltpu.VMEM((heads, width, keys), jnp.bfloat16),
        pltpu.VMEM((keys, rows), jnp.float32),
        pltpu.VMEM((keys, rows), jnp.float32),
        pltpu.VMEM((keys // BLK, rows), jnp.float32),
        pltpu.VMEM((keys // BLK, rows), jnp.float32),
    ]
    if last:
        out_specs = pl.BlockSpec((rows * heads, width), lambda i, *_: (i, 0))
        out_shape = jax.ShapeDtypeStruct((tokens * heads, width), jnp.bfloat16)
        aliases = {}
        scratch += [pltpu.VMEM((TILE, TILE), jnp.bfloat16), pltpu.VMEM((heads, rows, width), jnp.bfloat16)]
    else:
        out_specs = [parts, stats]
        out_shape = [
            jax.ShapeDtypeStruct(acc.shape, acc.dtype),
            jax.ShapeDtypeStruct(stat.shape, stat.dtype),
        ]
        aliases = {3 + len(halves): 0, 4 + len(halves): 1}
    grid_spec = pltpu.PrefetchScalarGridSpec(
        num_scalar_prefetch=2,
        grid=(tokens // rows,),
        in_specs=[pl.BlockSpec((heads, rows, width), lambda i, *_: (0, i, 0))] + [whole] * len(halves) + [parts, stats],
        out_specs=out_specs,
        scratch_shapes=scratch,
    )
    return pl.pallas_call(
        functools.partial(far_kernel, bys, tokens // BLK, last),
        grid_spec=grid_spec,
        out_shape=out_shape,
        input_output_aliases=aliases,
        compiler_params=pltpu.CompilerParams(vmem_limit_bytes=VMEM_BYTES),
        cost_estimate=SMALL,
        name="far",
    )(me, table, qt, *halves, acc, stat)


def rim_kernel(
    me_ref, q_ref, edge_mine, edge_other, tip_mine, tip_other, acc_in, stat_in, acc_ref, stat_ref, both_t, vt
):
    heads = q_ref.shape[0]
    c = pl.program_id(0)

    @pl.when(c == 0)
    def _():
        turn = split_order(heads)
        take_halves(me_ref, edge_mine, edge_other, 0, turn, both_t, vt)
        take_halves(me_ref, tip_mine, tip_other, BLK, turn, both_t, vt)

    for first_block in range(WB - 1):

        @pl.when(c == first_block)
        def _(first_block=first_block):
            blocks = range(first_block, WB - 1)
            shut = [jnp.where(me_ref[0] > 0, 0.0, FLOOR)] * len(blocks)
            span = slice(first_block * BLK, RIM)
            for group in range(0, heads, STRIDE):
                kept = []
                for h in range(group, group + STRIDE):
                    found = contract_last(both_t[0, h, span, :], q_ref[h])
                    near = [found[n * BLK : (n + 1) * BLK, :] for n in range(len(blocks))]
                    near_top, w, near_total = softmax_blocks(near, shut, stat_in[3, h : h + 1, :])
                    top = stat_in[0, h : h + 1, :]
                    both = jnp.maximum(top, near_top)
                    a = jnp.exp2(top - both)
                    b = jnp.exp2(near_top - both)
                    total = stat_in[1, h : h + 1, :] * a + near_total * b
                    part = acc_in[h] * a + mix(vt[h, :, span], w) * b
                    kept.append((part, both, total, stat_in[2, h : h + 1, :], near_top))
                for h, (part, *rows) in enumerate(kept, group):
                    acc_ref[h] = part
                    for n, row in enumerate(rows):
                        stat_ref[n, h : h + 1, :] = row


def rim(me, qt, halves, acc, stat):
    heads, tokens, width = qt.shape
    parts = pl.BlockSpec((heads, width, BLK), lambda i, *_: (0, 0, i))
    stats = pl.BlockSpec((STATS, heads, BLK), lambda i, *_: (0, 0, i))
    grid_spec = pltpu.PrefetchScalarGridSpec(
        num_scalar_prefetch=1,
        grid=(WB - 1,),
        in_specs=[pl.BlockSpec((heads, BLK, width), lambda i, *_: (0, i, 0))]
        + [pl.BlockSpec(half.shape, lambda i, *_: (0, 0)) for half in halves]
        + [parts, stats],
        out_specs=[parts, stats],
        scratch_shapes=[
            pltpu.VMEM((2, heads, RIM, width), jnp.bfloat16),
            pltpu.VMEM((heads, width, RIM), jnp.bfloat16),
        ],
    )
    return pl.pallas_call(
        rim_kernel,
        grid_spec=grid_spec,
        out_shape=[
            jax.ShapeDtypeStruct(acc.shape, acc.dtype),
            jax.ShapeDtypeStruct(stat.shape, stat.dtype),
        ],
        input_output_aliases={2 + len(halves): 0, 3 + len(halves): 1},
        compiler_params=pltpu.CompilerParams(vmem_limit_bytes=VMEM_BYTES),
        cost_estimate=SMALL,
        name="rim",
    )(me, qt, *halves, acc, stat)


def other_core(x):
    return lax.ppermute(x, "rep", [(0, 1), (1, 0)])


def ahead(x, by):
    count = lax.axis_size("ctx")
    return lax.ppermute(x, "ctx", [(i, i + by) for i in range(count - by)])


def local(queries, keys_values, far_list, far_count):
    tokens, heads, _, width = queries.shape
    spans = lax.axis_size("ctx")
    me = jnp.stack([lax.axis_index("ctx"), lax.axis_index("rep")]).astype(jnp.int32)
    q = queries.reshape(tokens * heads, width)
    kv = keys_values.reshape(tokens * heads, width)
    tip = kv[(tokens - (WB - 2) * BLK) * heads :]
    far_count, tip = lax.optimization_barrier((far_count, tip))
    tip = ahead(tip, 1)
    other = other_core(kv)
    table, *pools, edge = route(me, far_list, far_count, kv, spans)
    pieces = {by: ahead(pool, by) for by, pool in enumerate(pools, 1)}
    edge = ahead(edge, 1)
    qt, acc, stat = first(me, table, q, kv, other, heads, spans)
    late = min(2, spans - 1)
    bys = [by for by in pieces if by != late]
    tip, stat = lax.optimization_barrier((tip, stat))
    *early, edge, stat = lax.optimization_barrier((*[pieces[by] for by in bys], edge, stat))
    acc, stat = rim(me, qt, [edge, other_core(edge), tip, other_core(tip)], acc, stat)
    others = [other_core(piece) for piece in early]
    for n in range(0, len(bys), GROUP):
        halves = [half for pair in zip(early[n : n + GROUP], others[n : n + GROUP]) for half in pair]
        acc, stat = far(bys[n : n + GROUP], me, table, qt, halves, acc, stat, False)
    piece, stat = lax.optimization_barrier((pieces[late], stat))
    done = far([late], me, table, qt, [piece, other_core(piece)], acc, stat, True)
    return done.reshape(queries.shape)


def solution(mesh):
    in_specs = (
        P(("groups", "ctx"), "head", "rep", None),
        P("rep", ("groups", "ctx"), "head", None),
        P("groups", None),
        P("groups"),
    )
    out_specs = P(("groups", "ctx"), "head", "rep", None)
    return jax.shard_map(local, mesh=mesh, in_specs=in_specs, out_specs=out_specs, check_vma=False)
```

```python
import functools
import math

import jax
import jax.numpy as jnp
from jax import lax
from jax.experimental import pallas as pl
from jax.experimental.pallas import tpu as pltpu
from jax.sharding import PartitionSpec as P

BLK = 128
WB = 4
CAP = 2
RIM = (WB - 1) * BLK
TILE = 256
GROUP = 3
STATS = 4
STRIDE = 4

FLOOR = -1.0e30
SCALE = math.log2(math.e) / 12.0
NONE = 1.0e6
VMEM_BYTES = 48 * 1024 * 1024
SMALL = pl.CostEstimate(flops=1024, bytes_accessed=1024, transcendentals=0)


def contract_last(a, b):
    return lax.dot_general(a, b, (((1,), (1,)), ((), ())), preferred_element_type=jnp.float32)


def mix(a, b):
    return jnp.dot(a, b, preferred_element_type=jnp.float32)


def unit(n):
    row = lax.broadcasted_iota(jnp.int32, (n, n), 0)
    col = lax.broadcasted_iota(jnp.int32, (n, n), 1)
    return (row == col).astype(jnp.float32).astype(jnp.bfloat16)


def causal_bias():
    key = lax.broadcasted_iota(jnp.int32, (BLK, BLK), 0)
    query = lax.broadcasted_iota(jnp.int32, (BLK, BLK), 1)
    return jnp.where(key <= query, 0.0, FLOOR)


def softmax_blocks(scores, shut, top=None):
    for block, closed in zip(scores, shut):
        block_top = jnp.max(block, axis=0, keepdims=True) * SCALE
        block_top = block_top if closed is None else block_top + closed
        top = block_top if top is None else jnp.maximum(top, block_top)
    weights, total = [], 0.0
    for block, closed in zip(scores, shut):
        base = top if closed is None else jnp.where(closed < 0.0, -FLOOR, top)
        w = jnp.exp2(block * SCALE - base)
        total = total + jnp.sum(w, axis=0, keepdims=True)
        weights.append(w.astype(jnp.bfloat16))
    return top, jnp.concatenate(weights, axis=0), total


def near_scores(scores, causal):
    blocks = [scores[b * BLK : (b + 1) * BLK, :] for b in range(WB)]
    return blocks[:-1] + [blocks[-1] + causal]


def split_order(heads):
    step = TILE // heads
    row = lax.broadcasted_iota(jnp.int32, (TILE, TILE), 0)
    col = lax.broadcasted_iota(jnp.int32, (TILE, TILE), 1)
    source = (row & (step - 1)) * heads + (row >> (step.bit_length() - 1))
    return (col == source).astype(jnp.float32).astype(jnp.bfloat16)


def join_order(heads):
    step = TILE // heads
    row = lax.broadcasted_iota(jnp.int32, (TILE, TILE), 0)
    col = lax.broadcasted_iota(jnp.int32, (TILE, TILE), 1)
    source = (row & (heads - 1)) * step + (row >> (heads.bit_length() - 1))
    return (col == source).astype(jnp.float32).astype(jnp.bfloat16)


def chunk_pairs(rows, order):
    turned = []
    for i in range(0, rows.shape[0], 2 * TILE):
        two = jnp.concatenate([rows[i : i + TILE, :], rows[i + TILE : i + 2 * TILE, :]], axis=1)
        two = mix(order, two).astype(jnp.bfloat16)
        turned += [two[:, : rows.shape[1]], two[:, rows.shape[1] :]]
    return turned


def put_heads(turned, dst, base):
    heads = dst.shape[0]
    step = TILE // heads
    for i, rows in enumerate(turned):
        dst[:, pl.ds(base + i * step, step), :] = rows.reshape(heads, step, rows.shape[-1])


def route_kernel(me_ref, list_ref, count_ref, kv_ref, table_ref, *rest):
    spans = table_ref.shape[0] // (2 * CAP)
    pools, rim_out, sem = rest[:-2], rest[-2], rest[-1]
    edge = pltpu.make_async_copy(
        kv_ref.at[pl.ds(kv_ref.shape[0] - rim_out.shape[0] * (WB - 1), rim_out.shape[0]), :],
        rim_out,
        sem.at[sem.shape[0] - 1],
    )
    edge.start()
    me = me_ref[0]
    listed = list_ref[...]
    entries, total = listed.shape
    own = total // spans
    slot = lax.broadcasted_iota(jnp.int32, (entries, total), 0)
    lane = lax.broadcasted_iota(jnp.int32, (entries, total), 1)
    counted = slot < count_ref[...]
    named = jnp.where(counted, listed.astype(jnp.float32), 2.0 * NONE)

    def pick(user, source):
        low = (source * own).astype(jnp.float32)
        mine = (lane >= user * own) & (lane < (user + 1) * own)
        left = jnp.where(mine & (named >= low) & (named < low + own), named, NONE)
        picked = []
        for _ in range(CAP):
            least = jnp.min(jnp.min(left, axis=0, keepdims=True), axis=1, keepdims=True)
            picked.append(least)
            left = jnp.where(left == least, NONE, left)
        return picked

    row_len = kv_ref.shape[0] // own
    sent = [block for by in range(1, spans) for block in pick(me + by, me)]
    copies = []
    for n, block in enumerate(sent):
        local = block - (me * own).astype(jnp.float32)
        local = jnp.max(jnp.where(local < own, local, 0.0)).astype(jnp.int32)
        start = pl.multiple_of(local * row_len, row_len)
        copy = pltpu.make_async_copy(
            kv_ref.at[pl.ds(start, row_len), :],
            pools[n // CAP].at[pl.ds(n % CAP * row_len, row_len), :],
            sem.at[n],
        )
        copies.append(copy)
    for copy in copies:
        copy.start()
    for by in range(spans):
        source = me - by
        for j, block in enumerate(pick(me, source)):
            used = jnp.max((named == block).astype(jnp.float32), axis=0, keepdims=True)
            local = block - (source * own).astype(jnp.float32)
            local = jnp.where(local < own, local, 0.0)
            row = by * CAP + j
            table_ref[row : row + 1, :] = used.astype(jnp.int32)
            ids = jnp.zeros((1, total), jnp.float32) + local
            table_ref[spans * CAP + row : spans * CAP + row + 1, :] = ids.astype(jnp.int32)
    for copy in copies:
        copy.wait()
    edge.wait()


def route(me, far_list, far_count, kv, spans):
    total = far_list.shape[0]
    rows = kv.shape[0] // (total // spans) * CAP
    pool = jax.ShapeDtypeStruct((rows, kv.shape[1]), kv.dtype)
    edge = jax.ShapeDtypeStruct((rows // CAP, kv.shape[1]), kv.dtype)
    grid_spec = pltpu.PrefetchScalarGridSpec(
        num_scalar_prefetch=1,
        grid=(1,),
        in_specs=[
            pl.BlockSpec(far_list.shape[::-1], lambda i, *_: (0, 0)),
            pl.BlockSpec((1, total), lambda i, *_: (0, 0)),
            pl.BlockSpec(memory_space=pltpu.HBM),
        ],
        out_specs=[pl.BlockSpec((2 * CAP * spans, total), lambda i, *_: (0, 0))]
        + [pl.BlockSpec(pool.shape, lambda i, *_: (0, 0))] * (spans - 1)
        + [pl.BlockSpec(edge.shape, lambda i, *_: (0, 0))],
        scratch_shapes=[pltpu.SemaphoreType.DMA(((spans - 1) * CAP + 1,))],
    )
    return pl.pallas_call(
        route_kernel,
        grid_spec=grid_spec,
        out_shape=[jax.ShapeDtypeStruct((2 * CAP * spans, total), jnp.int32)] + [pool] * (spans - 1) + [edge],
        cost_estimate=SMALL,
        name="route",
    )(me, far_list.T, far_count[None, :], kv)


def first_kernel(
    spans, me_ref, table_ref, q_ref, mine_ref, other_ref, qt_ref, acc_ref, stat_ref, both_t, vt, qs, order, eye, diag
):
    heads = qt_ref.shape[0]
    own = pl.num_programs(0)
    c = pl.program_id(0)

    @pl.when(c == 0)
    def _():
        order[...] = split_order(heads)
        eye[...] = unit(eye.shape[0])
        diag[...] = causal_bias()
        both_t[:, :, :RIM, :] = jnp.zeros((2, heads, RIM, both_t.shape[-1]), jnp.bfloat16)
        vt[:, :, :RIM] = jnp.zeros((heads, vt.shape[1], RIM), jnp.bfloat16)

    start = pl.multiple_of(c * BLK, BLK)
    base = pl.multiple_of(RIM + c * BLK, BLK)
    turn = order[...]
    turned = [chunk_pairs(ref[...], turn) for ref in (q_ref, mine_ref, other_ref)]
    put_heads(turned[0], qs, 0)
    put_heads(turned[1], both_t.at[me_ref[1]], base)
    put_heads(turned[2], both_t.at[1 - me_ref[1]], base)
    put_heads(turned[0], qt_ref, 0)
    kt = both_t.at[0]
    flipped = [contract_last(eye[...], both_t[1, h, pl.ds(base, BLK), :]).astype(jnp.bfloat16) for h in range(heads)]
    for h in range(heads):
        vt[h, :, pl.ds(base, BLK)] = flipped[h]

    here = me_ref[0] * own + c
    shut = [jnp.where(table_ref[j, here] > 0, 0.0, FLOOR) for j in range(CAP)]
    far_at = [
        pl.multiple_of(RIM + jnp.minimum(table_ref[spans * CAP + j, here], c) * BLK, BLK) for j in range(CAP)
    ]
    near_shut = [jnp.where(c + b >= WB - 1, 0.0, FLOOR) for b in range(WB - 1)] + [None]
    causal = diag[...]
    for group in range(0, heads, STRIDE):
        found = []
        for h in range(group, group + STRIDE):
            q = qs[h]
            near = near_scores(contract_last(kt[h, pl.ds(start, WB * BLK), :], q), causal)
            far = [contract_last(kt[h, pl.ds(at, BLK), :], q) for at in far_at]
            top, w, total = softmax_blocks(near, near_shut)
            part = mix(vt[h, :, pl.ds(start, WB * BLK)], w)
            far_top, far_w, far_total = softmax_blocks(far, shut)
            far_v = jnp.concatenate([vt[h, :, pl.ds(at, BLK)] for at in far_at], axis=1)
            far_part = mix(far_v, far_w)
            both = jnp.maximum(top, far_top)
            a = jnp.exp2(top - both)
            b = jnp.exp2(far_top - both)
            found.append((part * a + far_part * b, both, total * a + far_total * b, far_top, top))
        for h, (part, *rows) in enumerate(found, group):
            acc_ref[0, h] = part
            for n, row in enumerate(rows):
                stat_ref[n, h : h + 1, :] = row


def first(me, table, q, mine, other, heads, spans):
    tokens = q.shape[0] // heads
    width = q.shape[1]
    own = tokens // BLK
    raw = pl.BlockSpec((BLK * heads, width), lambda c, *_: (c, 0))
    grid_spec = pltpu.PrefetchScalarGridSpec(
        num_scalar_prefetch=2,
        grid=(own,),
        in_specs=[raw, raw, raw],
        out_specs=[
            pl.BlockSpec((heads, BLK, width), lambda c, *_: (0, c, 0)),
            pl.BlockSpec((1, heads, width, BLK), lambda c, *_: (c, 0, 0, 0)),
            pl.BlockSpec((STATS, heads, BLK), lambda c, *_: (0, 0, c)),
        ],
        scratch_shapes=[
            pltpu.VMEM((2, heads, RIM + tokens, width), jnp.bfloat16),
            pltpu.VMEM((heads, width, RIM + tokens), jnp.bfloat16),
            pltpu.VMEM((heads, BLK, width), jnp.bfloat16),
            pltpu.VMEM((TILE, TILE), jnp.bfloat16),
            pltpu.VMEM((width, width), jnp.bfloat16),
            pltpu.VMEM((BLK, BLK), jnp.float32),
        ],
    )
    return pl.pallas_call(
        functools.partial(first_kernel, spans),
        grid_spec=grid_spec,
        out_shape=[
            jax.ShapeDtypeStruct((heads, tokens, width), jnp.bfloat16),
            jax.ShapeDtypeStruct((own, heads, width, BLK), jnp.float32),
            jax.ShapeDtypeStruct((STATS, heads, tokens), jnp.float32),
        ],
        compiler_params=pltpu.CompilerParams(vmem_limit_bytes=VMEM_BYTES),
        cost_estimate=SMALL,
        name="first",
    )(me, table, q, mine, other)


def take_halves(me_ref, mine_ref, other_ref, base, turn, both_t, vt):
    heads, width = vt.shape[:2]
    turned = [chunk_pairs(ref[...], turn) for ref in (mine_ref, other_ref)]
    put_heads(turned[0], both_t.at[me_ref[1]], base)
    put_heads(turned[1], both_t.at[1 - me_ref[1]], base)
    eye = unit(width)
    span = slice(base, base + mine_ref.shape[0] // heads)
    flipped = [contract_last(eye, both_t[1, h, span, :]).astype(jnp.bfloat16) for h in range(heads)]
    for h in range(heads):
        vt[h, :, span] = flipped[h]


def finish(done, order, out_ref):
    heads, rows, _ = done.shape
    step = TILE // heads
    ordered = jnp.concatenate([done[h, i : i + step, :] for i in range(0, rows, step) for h in range(heads)], axis=0)
    for i, chunk in enumerate(chunk_pairs(ordered, order)):
        out_ref[i * TILE : (i + 1) * TILE, :] = chunk


def result(part, total):
    return jnp.transpose(part * (1.0 / total)).astype(jnp.bfloat16)


def far_kernel(bys, own, last, me_ref, table_ref, q_ref, *rest):
    halves, rest = rest[: 2 * len(bys)], rest[2 * len(bys) :]
    acc_in, stat_in, *rest = rest
    if last:
        out_ref, *rest = rest
    else:
        acc_ref, stat_ref, *rest = rest
    both_t, vt, scores_a, scores_b, tops_a, tops_b, *rest = rest
    if last:
        order, done = rest
    heads, rows, _ = q_ref.shape
    i = pl.program_id(0)

    @pl.when(i == 0)
    def _():
        turn = split_order(heads)
        for n in range(len(bys)):
            take_halves(me_ref, halves[2 * n], halves[2 * n + 1], n * CAP * BLK, turn, both_t, vt)
        if last:
            order[...] = join_order(heads)

    here = me_ref[0] * own + i * (rows // BLK)
    shut = []
    for by in bys:
        for j in range(CAP):
            row = [jnp.where(table_ref[by * CAP + j, here + a] > 0, 0.0, FLOOR) for a in range(rows // BLK)]
            shut.append(jnp.concatenate([jnp.full((1, BLK), closed, jnp.float32) for closed in row], axis=1))

    def fill(h, query, scores, tops):
        found = contract_last(both_t[0, h], query)
        for j in range(len(shut)):
            block = found[j * BLK : (j + 1) * BLK, :]
            tops[j : j + 1, :] = jnp.max(block, axis=0, keepdims=True)
            scores[j * BLK : (j + 1) * BLK, :] = block

    def use(h, before, stats, scores, tops):
        top, total, far_top, near_top = stats
        for j, closed in enumerate(shut):
            far_top = jnp.maximum(far_top, tops[j : j + 1, :] * SCALE + closed)
        weights, far_total = [], 0.0
        for j, closed in enumerate(shut):
            base = jnp.where(closed < 0.0, -FLOOR, far_top)
            w = jnp.exp2(scores[j * BLK : (j + 1) * BLK, :] * SCALE - base)
            far_total = far_total + jnp.sum(w, axis=0, keepdims=True)
            weights.append(w.astype(jnp.bfloat16))
        both = jnp.maximum(top, far_top)
        a = jnp.exp2(top - both)
        b = jnp.exp2(far_top - both)
        total = total * a + far_total * b
        part = before * a + mix(vt[h], jnp.concatenate(weights, axis=0)) * b
        return part, (both, total, far_top, near_top)

    def keep(h, part, stats):
        if last:
            done[h] = result(part, stats[1])
        else:
            for a in range(rows // BLK):
                acc_ref[a, h] = part[:, a * BLK : (a + 1) * BLK]
            for n, row in enumerate(stats):
                stat_ref[n, pl.ds(h, 1), :] = row

    fill(0, q_ref[0], scores_a, tops_a)

    def next_heads(n, carry):
        base = STRIDE * n
        members = [base + m for m in range(STRIDE)]
        queries = [q_ref[h] for h in members[1:]] + [q_ref[jnp.minimum(base + STRIDE, heads - 1)]]
        before = [jnp.concatenate([acc_in[a, h] for a in range(rows // BLK)], axis=1) for h in members]
        stats = [[stat_in[n, pl.ds(h, 1), :] for n in range(STATS)] for h in members]
        kept = []
        for m, h in enumerate(members):
            slots = (scores_a, tops_a, scores_b, tops_b) if m % 2 == 0 else (scores_b, tops_b, scores_a, tops_a)
            fill(jnp.minimum(h + 1, heads - 1), queries[m], *slots[2:])
            kept.append(use(h, before[m], stats[m], *slots[:2]))
        for h, found in zip(members, kept):
            keep(h, *found)
        return carry

    lax.fori_loop(0, heads // STRIDE, next_heads, 0)
    if last:
        finish(done, order[...], out_ref)


def far(bys, me, table, qt, halves, acc, stat, last):
    heads, tokens, width = qt.shape
    rows = min(TILE, tokens)
    keys = len(bys) * CAP * BLK
    parts = pl.BlockSpec((rows // BLK, heads, width, BLK), lambda i, *_: (i, 0, 0, 0))
    stats = pl.BlockSpec((STATS, heads, rows), lambda i, *_: (0, 0, i))
    whole = pl.BlockSpec(halves[0].shape, lambda i, *_: (0, 0))
    scratch = [
        pltpu.VMEM((2, heads, keys, width), jnp.bfloat16),
        pltpu.VMEM((heads, width, keys), jnp.bfloat16),
        pltpu.VMEM((keys, rows), jnp.float32),
        pltpu.VMEM((keys, rows), jnp.float32),
        pltpu.VMEM((keys // BLK, rows), jnp.float32),
        pltpu.VMEM((keys // BLK, rows), jnp.float32),
    ]
    if last:
        out_specs = pl.BlockSpec((rows * heads, width), lambda i, *_: (i, 0))
        out_shape = jax.ShapeDtypeStruct((tokens * heads, width), jnp.bfloat16)
        aliases = {}
        scratch += [pltpu.VMEM((TILE, TILE), jnp.bfloat16), pltpu.VMEM((heads, rows, width), jnp.bfloat16)]
    else:
        out_specs = [parts, stats]
        out_shape = [
            jax.ShapeDtypeStruct(acc.shape, acc.dtype),
            jax.ShapeDtypeStruct(stat.shape, stat.dtype),
        ]
        aliases = {3 + len(halves): 0, 4 + len(halves): 1}
    grid_spec = pltpu.PrefetchScalarGridSpec(
        num_scalar_prefetch=2,
        grid=(tokens // rows,),
        in_specs=[pl.BlockSpec((heads, rows, width), lambda i, *_: (0, i, 0))] + [whole] * len(halves) + [parts, stats],
        out_specs=out_specs,
        scratch_shapes=scratch,
    )
    return pl.pallas_call(
        functools.partial(far_kernel, bys, tokens // BLK, last),
        grid_spec=grid_spec,
        out_shape=out_shape,
        input_output_aliases=aliases,
        compiler_params=pltpu.CompilerParams(vmem_limit_bytes=VMEM_BYTES),
        cost_estimate=SMALL,
        name="far",
    )(me, table, qt, *halves, acc, stat)


def rim_kernel(
    me_ref, q_ref, edge_mine, edge_other, tip_mine, tip_other, acc_in, stat_in, acc_ref, stat_ref, both_t, vt
):
    heads = q_ref.shape[0]
    c = pl.program_id(0)

    @pl.when(c == 0)
    def _():
        turn = split_order(heads)
        take_halves(me_ref, edge_mine, edge_other, 0, turn, both_t, vt)
        take_halves(me_ref, tip_mine, tip_other, BLK, turn, both_t, vt)

    for first_block in range(WB - 1):

        @pl.when(c == first_block)
        def _(first_block=first_block):
            blocks = range(first_block, WB - 1)
            shut = [jnp.where(me_ref[0] > 0, 0.0, FLOOR)] * len(blocks)
            span = slice(first_block * BLK, RIM)
            kept = []
            for h in range(heads):
                found = contract_last(both_t[0, h, span, :], q_ref[h])
                near = [found[n * BLK : (n + 1) * BLK, :] for n in range(len(blocks))]
                near_top, w, near_total = softmax_blocks(near, shut, stat_in[3, h : h + 1, :])
                top = stat_in[0, h : h + 1, :]
                both = jnp.maximum(top, near_top)
                a = jnp.exp2(top - both)
                b = jnp.exp2(near_top - both)
                total = stat_in[1, h : h + 1, :] * a + near_total * b
                part = acc_in[0, h] * a + mix(vt[h, :, span], w) * b
                kept.append((part, both, total, stat_in[2, h : h + 1, :], near_top))
            for h, (part, *rows) in enumerate(kept):
                acc_ref[0, h] = part
                for n, row in enumerate(rows):
                    stat_ref[n, h : h + 1, :] = row


def rim(me, qt, halves, acc, stat):
    heads, tokens, width = qt.shape
    parts = pl.BlockSpec((1, heads, width, BLK), lambda i, *_: (i, 0, 0, 0))
    stats = pl.BlockSpec((STATS, heads, BLK), lambda i, *_: (0, 0, i))
    grid_spec = pltpu.PrefetchScalarGridSpec(
        num_scalar_prefetch=1,
        grid=(WB - 1,),
        in_specs=[pl.BlockSpec((heads, BLK, width), lambda i, *_: (0, i, 0))]
        + [pl.BlockSpec(half.shape, lambda i, *_: (0, 0)) for half in halves]
        + [parts, stats],
        out_specs=[parts, stats],
        scratch_shapes=[
            pltpu.VMEM((2, heads, RIM, width), jnp.bfloat16),
            pltpu.VMEM((heads, width, RIM), jnp.bfloat16),
        ],
    )
    return pl.pallas_call(
        rim_kernel,
        grid_spec=grid_spec,
        out_shape=[
            jax.ShapeDtypeStruct(acc.shape, acc.dtype),
            jax.ShapeDtypeStruct(stat.shape, stat.dtype),
        ],
        input_output_aliases={2 + len(halves): 0, 3 + len(halves): 1},
        compiler_params=pltpu.CompilerParams(vmem_limit_bytes=VMEM_BYTES),
        cost_estimate=SMALL,
        name="rim",
    )(me, qt, *halves, acc, stat)


def other_core(x):
    return lax.ppermute(x, "rep", [(0, 1), (1, 0)])


def ahead(x, by):
    count = lax.axis_size("ctx")
    return lax.ppermute(x, "ctx", [(i, i + by) for i in range(count - by)])


def local(queries, keys_values, far_list, far_count):
    tokens, heads, _, width = queries.shape
    spans = lax.axis_size("ctx")
    me = jnp.stack([lax.axis_index("ctx"), lax.axis_index("rep")]).astype(jnp.int32)
    q = queries.reshape(tokens * heads, width)
    kv = keys_values.reshape(tokens * heads, width)
    tip = kv[(tokens - (WB - 2) * BLK) * heads :]
    far_count, tip = lax.optimization_barrier((far_count, tip))
    tip = ahead(tip, 1)
    other = other_core(kv)
    table, *pools, edge = route(me, far_list, far_count, kv, spans)
    pieces = {by: ahead(pool, by) for by, pool in enumerate(pools, 1)}
    edge = ahead(edge, 1)
    qt, acc, stat = first(me, table, q, kv, other, heads, spans)
    late = min(2, spans - 1)
    bys = [by for by in pieces if by != late]
    tip, stat = lax.optimization_barrier((tip, stat))
    *early, edge, stat = lax.optimization_barrier((*[pieces[by] for by in bys], edge, stat))
    acc, stat = rim(me, qt, [edge, other_core(edge), tip, other_core(tip)], acc, stat)
    others = [other_core(piece) for piece in early]
    for n in range(0, len(bys), GROUP):
        halves = [half for pair in zip(early[n : n + GROUP], others[n : n + GROUP]) for half in pair]
        acc, stat = far(bys[n : n + GROUP], me, table, qt, halves, acc, stat, False)
    piece, stat = lax.optimization_barrier((pieces[late], stat))
    done = far([late], me, table, qt, [piece, other_core(piece)], acc, stat, True)
    return done.reshape(queries.shape)


def solution(mesh):
    in_specs = (
        P(("groups", "ctx"), "head", "rep", None),
        P("rep", ("groups", "ctx"), "head", None),
        P("groups", None),
        P("groups"),
    )
    out_specs = P(("groups", "ctx"), "head", "rep", None)
    return jax.shard_map(local, mesh=mesh, in_specs=in_specs, out_specs=out_specs, check_vma=False)
```

```python
import functools
import math

import jax
import jax.numpy as jnp
from jax import lax
from jax.experimental import pallas as pl
from jax.experimental.pallas import tpu as pltpu
from jax.sharding import PartitionSpec as P

BLK = 128
WB = 4
CAP = 2
RIM = (WB - 1) * BLK
TILE = 256
GROUP = 3
STATS = 4
STRIDE = 4

FLOOR = -1.0e30
SCALE = math.log2(math.e) / 12.0
NONE = 1.0e6
VMEM_BYTES = 48 * 1024 * 1024
SMALL = pl.CostEstimate(flops=1024, bytes_accessed=1024, transcendentals=0)


def contract_last(a, b):
    return lax.dot_general(a, b, (((1,), (1,)), ((), ())), preferred_element_type=jnp.float32)


def mix(a, b):
    return jnp.dot(a, b, preferred_element_type=jnp.float32)


def unit(n):
    row = lax.broadcasted_iota(jnp.int32, (n, n), 0)
    col = lax.broadcasted_iota(jnp.int32, (n, n), 1)
    return (row == col).astype(jnp.float32).astype(jnp.bfloat16)


def causal_bias():
    key = lax.broadcasted_iota(jnp.int32, (BLK, BLK), 0)
    query = lax.broadcasted_iota(jnp.int32, (BLK, BLK), 1)
    return jnp.where(key <= query, 0.0, FLOOR)


def softmax_blocks(scores, shut, top=None):
    for block, closed in zip(scores, shut):
        block_top = jnp.max(block, axis=0, keepdims=True) * SCALE
        block_top = block_top if closed is None else block_top + closed
        top = block_top if top is None else jnp.maximum(top, block_top)
    weights, total = [], 0.0
    for block, closed in zip(scores, shut):
        base = top if closed is None else jnp.where(closed < 0.0, -FLOOR, top)
        w = jnp.exp2(block * SCALE - base)
        total = total + jnp.sum(w, axis=0, keepdims=True)
        weights.append(w.astype(jnp.bfloat16))
    return top, jnp.concatenate(weights, axis=0), total


def near_scores(scores, causal):
    blocks = [scores[b * BLK : (b + 1) * BLK, :] for b in range(WB)]
    return blocks[:-1] + [blocks[-1] + causal]


def split_order(heads):
    step = TILE // heads
    row = lax.broadcasted_iota(jnp.int32, (TILE, TILE), 0)
    col = lax.broadcasted_iota(jnp.int32, (TILE, TILE), 1)
    source = (row & (step - 1)) * heads + (row >> (step.bit_length() - 1))
    return (col == source).astype(jnp.float32).astype(jnp.bfloat16)


def join_order(heads):
    step = TILE // heads
    row = lax.broadcasted_iota(jnp.int32, (TILE, TILE), 0)
    col = lax.broadcasted_iota(jnp.int32, (TILE, TILE), 1)
    source = (row & (heads - 1)) * step + (row >> (heads.bit_length() - 1))
    return (col == source).astype(jnp.float32).astype(jnp.bfloat16)


def chunk_pairs(rows, order):
    turned = []
    for i in range(0, rows.shape[0], 2 * TILE):
        two = jnp.concatenate([rows[i : i + TILE, :], rows[i + TILE : i + 2 * TILE, :]], axis=1)
        two = mix(order, two).astype(jnp.bfloat16)
        turned += [two[:, : rows.shape[1]], two[:, rows.shape[1] :]]
    return turned


def put_heads(turned, dst, base):
    heads = dst.shape[0]
    step = TILE // heads
    for i, rows in enumerate(turned):
        dst[:, pl.ds(base + i * step, step), :] = rows.reshape(heads, step, rows.shape[-1])


def route_kernel(me_ref, list_ref, count_ref, kv_ref, table_ref, *rest):
    spans = table_ref.shape[0] // (2 * CAP)
    pools, rim_out, sem = rest[:-2], rest[-2], rest[-1]
    edge = pltpu.make_async_copy(
        kv_ref.at[pl.ds(kv_ref.shape[0] - rim_out.shape[0] * (WB - 1), rim_out.shape[0]), :],
        rim_out,
        sem.at[sem.shape[0] - 1],
    )
    edge.start()
    me = me_ref[0]
    listed = list_ref[...]
    entries, total = listed.shape
    own = total // spans
    slot = lax.broadcasted_iota(jnp.int32, (entries, total), 0)
    lane = lax.broadcasted_iota(jnp.int32, (entries, total), 1)
    counted = slot < count_ref[...]
    named = jnp.where(counted, listed.astype(jnp.float32), 2.0 * NONE)

    def pick(user, source):
        low = (source * own).astype(jnp.float32)
        mine = (lane >= user * own) & (lane < (user + 1) * own)
        left = jnp.where(mine & (named >= low) & (named < low + own), named, NONE)
        picked = []
        for _ in range(CAP):
            least = jnp.min(jnp.min(left, axis=0, keepdims=True), axis=1, keepdims=True)
            picked.append(least)
            left = jnp.where(left == least, NONE, left)
        return picked

    row_len = kv_ref.shape[0] // own
    sent = [block for by in range(1, spans) for block in pick(me + by, me)]
    copies = []
    for n, block in enumerate(sent):
        local = block - (me * own).astype(jnp.float32)
        local = jnp.max(jnp.where(local < own, local, 0.0)).astype(jnp.int32)
        start = pl.multiple_of(local * row_len, row_len)
        copy = pltpu.make_async_copy(
            kv_ref.at[pl.ds(start, row_len), :],
            pools[n // CAP].at[pl.ds(n % CAP * row_len, row_len), :],
            sem.at[n],
        )
        copies.append(copy)
    for copy in copies:
        copy.start()
    for by in range(spans):
        source = me - by
        for j, block in enumerate(pick(me, source)):
            used = jnp.max((named == block).astype(jnp.float32), axis=0, keepdims=True)
            local = block - (source * own).astype(jnp.float32)
            local = jnp.where(local < own, local, 0.0)
            row = by * CAP + j
            table_ref[row : row + 1, :] = used.astype(jnp.int32)
            ids = jnp.zeros((1, total), jnp.float32) + local
            table_ref[spans * CAP + row : spans * CAP + row + 1, :] = ids.astype(jnp.int32)
    for copy in copies:
        copy.wait()
    edge.wait()


def route(me, far_list, far_count, kv, spans):
    total = far_list.shape[0]
    rows = kv.shape[0] // (total // spans) * CAP
    pool = jax.ShapeDtypeStruct((rows, kv.shape[1]), kv.dtype)
    edge = jax.ShapeDtypeStruct((rows // CAP, kv.shape[1]), kv.dtype)
    grid_spec = pltpu.PrefetchScalarGridSpec(
        num_scalar_prefetch=1,
        grid=(1,),
        in_specs=[
            pl.BlockSpec(far_list.shape[::-1], lambda i, *_: (0, 0)),
            pl.BlockSpec((1, total), lambda i, *_: (0, 0)),
            pl.BlockSpec(memory_space=pltpu.HBM),
        ],
        out_specs=[pl.BlockSpec((2 * CAP * spans, total), lambda i, *_: (0, 0))]
        + [pl.BlockSpec(pool.shape, lambda i, *_: (0, 0))] * (spans - 1)
        + [pl.BlockSpec(edge.shape, lambda i, *_: (0, 0))],
        scratch_shapes=[pltpu.SemaphoreType.DMA(((spans - 1) * CAP + 1,))],
    )
    return pl.pallas_call(
        route_kernel,
        grid_spec=grid_spec,
        out_shape=[jax.ShapeDtypeStruct((2 * CAP * spans, total), jnp.int32)] + [pool] * (spans - 1) + [edge],
        cost_estimate=SMALL,
        name="route",
    )(me, far_list.T, far_count[None, :], kv)


def first_kernel(
    spans, me_ref, table_ref, q_ref, mine_ref, other_ref, qt_ref, acc_ref, stat_ref, both_t, vt, qs, qf, order, eye, diag
):
    heads = qt_ref.shape[1]
    own = pl.num_programs(0)
    c = pl.program_id(0)

    @pl.when(c == 0)
    def _():
        order[...] = split_order(heads)
        eye[...] = unit(eye.shape[0])
        diag[...] = causal_bias()
        both_t[:, :, :RIM, :] = jnp.zeros((2, heads, RIM, both_t.shape[-1]), jnp.bfloat16)
        vt[:, :, :RIM] = jnp.zeros((heads, vt.shape[1], RIM), jnp.bfloat16)

    start = pl.multiple_of(c * BLK, BLK)
    base = pl.multiple_of(RIM + c * BLK, BLK)
    turn = order[...]
    turned = [chunk_pairs(ref[...], turn) for ref in (q_ref, mine_ref, other_ref)]
    put_heads(turned[0], qs, 0)
    put_heads(turned[1], both_t.at[me_ref[1]], base)
    put_heads(turned[2], both_t.at[1 - me_ref[1]], base)
    kt = both_t.at[0]
    flipped = [contract_last(eye[...], both_t[1, h, pl.ds(base, BLK), :]).astype(jnp.bfloat16) for h in range(heads)]
    asked = [contract_last(eye[...], qs[h]).astype(jnp.bfloat16) for h in range(heads)]
    for h in range(heads):
        vt[h, :, pl.ds(base, BLK)] = flipped[h]
        qf[h] = asked[h]
        qt_ref[0, h] = asked[h]

    here = me_ref[0] * own + c
    shut = [jnp.where(table_ref[j, here] > 0, 0.0, FLOOR) for j in range(CAP)]
    far_at = [
        pl.multiple_of(RIM + jnp.minimum(table_ref[spans * CAP + j, here], c) * BLK, BLK) for j in range(CAP)
    ]
    near_shut = [jnp.where(c + b >= WB - 1, 0.0, FLOOR) for b in range(WB - 1)] + [None]
    causal = diag[...]
    for group in range(0, heads, STRIDE):
        found = []
        for h in range(group, group + STRIDE):
            q = qf[h]
            near = near_scores(mix(kt[h, pl.ds(start, WB * BLK), :], q), causal)
            far = [mix(kt[h, pl.ds(at, BLK), :], q) for at in far_at]
            top, w, total = softmax_blocks(near, near_shut)
            part = mix(vt[h, :, pl.ds(start, WB * BLK)], w)
            far_top, far_w, far_total = softmax_blocks(far, shut)
            far_v = jnp.concatenate([vt[h, :, pl.ds(at, BLK)] for at in far_at], axis=1)
            far_part = mix(far_v, far_w)
            both = jnp.maximum(top, far_top)
            a = jnp.exp2(top - both)
            b = jnp.exp2(far_top - both)
            found.append((part * a + far_part * b, both, total * a + far_total * b, far_top, top))
        for h, (part, *rows) in enumerate(found, group):
            acc_ref[0, h] = part
            for n, row in enumerate(rows):
                stat_ref[n, h : h + 1, :] = row


def first(me, table, q, mine, other, heads, spans):
    tokens = q.shape[0] // heads
    width = q.shape[1]
    own = tokens // BLK
    raw = pl.BlockSpec((BLK * heads, width), lambda c, *_: (c, 0))
    grid_spec = pltpu.PrefetchScalarGridSpec(
        num_scalar_prefetch=2,
        grid=(own,),
        in_specs=[raw, raw, raw],
        out_specs=[
            pl.BlockSpec((1, heads, width, BLK), lambda c, *_: (c, 0, 0, 0)),
            pl.BlockSpec((1, heads, width, BLK), lambda c, *_: (c, 0, 0, 0)),
            pl.BlockSpec((STATS, heads, BLK), lambda c, *_: (0, 0, c)),
        ],
        scratch_shapes=[
            pltpu.VMEM((2, heads, RIM + tokens, width), jnp.bfloat16),
            pltpu.VMEM((heads, width, RIM + tokens), jnp.bfloat16),
            pltpu.VMEM((heads, BLK, width), jnp.bfloat16),
            pltpu.VMEM((heads, width, BLK), jnp.bfloat16),
            pltpu.VMEM((TILE, TILE), jnp.bfloat16),
            pltpu.VMEM((width, width), jnp.bfloat16),
            pltpu.VMEM((BLK, BLK), jnp.float32),
        ],
    )
    return pl.pallas_call(
        functools.partial(first_kernel, spans),
        grid_spec=grid_spec,
        out_shape=[
            jax.ShapeDtypeStruct((own, heads, width, BLK), jnp.bfloat16),
            jax.ShapeDtypeStruct((own, heads, width, BLK), jnp.float32),
            jax.ShapeDtypeStruct((STATS, heads, tokens), jnp.float32),
        ],
        compiler_params=pltpu.CompilerParams(vmem_limit_bytes=VMEM_BYTES),
        cost_estimate=SMALL,
        name="first",
    )(me, table, q, mine, other)


def take_halves(me_ref, mine_ref, other_ref, base, turn, both_t, vt):
    heads, width = vt.shape[:2]
    turned = [chunk_pairs(ref[...], turn) for ref in (mine_ref, other_ref)]
    put_heads(turned[0], both_t.at[me_ref[1]], base)
    put_heads(turned[1], both_t.at[1 - me_ref[1]], base)
    eye = unit(width)
    span = slice(base, base + mine_ref.shape[0] // heads)
    flipped = [contract_last(eye, both_t[1, h, span, :]).astype(jnp.bfloat16) for h in range(heads)]
    for h in range(heads):
        vt[h, :, span] = flipped[h]


def finish(done, order, out_ref):
    heads, rows, _ = done.shape
    step = TILE // heads
    ordered = jnp.concatenate([done[h, i : i + step, :] for i in range(0, rows, step) for h in range(heads)], axis=0)
    for i, chunk in enumerate(chunk_pairs(ordered, order)):
        out_ref[i * TILE : (i + 1) * TILE, :] = chunk


def result(part, total):
    return jnp.transpose(part * (1.0 / total)).astype(jnp.bfloat16)


def far_kernel(bys, own, last, me_ref, table_ref, q_ref, *rest):
    halves, rest = rest[: 2 * len(bys)], rest[2 * len(bys) :]
    acc_in, stat_in, *rest = rest
    if last:
        out_ref, *rest = rest
    else:
        acc_ref, stat_ref, *rest = rest
    both_t, vt, scores_a, scores_b, tops_a, tops_b, *rest = rest
    if last:
        order, done = rest
    heads, rows = q_ref.shape[1], q_ref.shape[0] * BLK

    def query(h):
        return jnp.concatenate([q_ref[a, h] for a in range(rows // BLK)], axis=1)

    i = pl.program_id(0)

    @pl.when(i == 0)
    def _():
        turn = split_order(heads)
        for n in range(len(bys)):
            take_halves(me_ref, halves[2 * n], halves[2 * n + 1], n * CAP * BLK, turn, both_t, vt)
        if last:
            order[...] = join_order(heads)

    here = me_ref[0] * own + i * (rows // BLK)
    shut = []
    for by in bys:
        for j in range(CAP):
            row = [jnp.where(table_ref[by * CAP + j, here + a] > 0, 0.0, FLOOR) for a in range(rows // BLK)]
            shut.append(jnp.concatenate([jnp.full((1, BLK), closed, jnp.float32) for closed in row], axis=1))

    def fill(h, asked, scores, tops):
        found = mix(both_t[0, h], asked)
        for j in range(len(shut)):
            block = found[j * BLK : (j + 1) * BLK, :]
            tops[j : j + 1, :] = jnp.max(block, axis=0, keepdims=True)
            scores[j * BLK : (j + 1) * BLK, :] = block

    def use(h, before, stats, scores, tops):
        top, total, far_top, near_top = stats
        for j, closed in enumerate(shut):
            far_top = jnp.maximum(far_top, tops[j : j + 1, :] * SCALE + closed)
        weights, far_total = [], 0.0
        for j, closed in enumerate(shut):
            base = jnp.where(closed < 0.0, -FLOOR, far_top)
            w = jnp.exp2(scores[j * BLK : (j + 1) * BLK, :] * SCALE - base)
            far_total = far_total + jnp.sum(w, axis=0, keepdims=True)
            weights.append(w.astype(jnp.bfloat16))
        both = jnp.maximum(top, far_top)
        a = jnp.exp2(top - both)
        b = jnp.exp2(far_top - both)
        total = total * a + far_total * b
        part = before * a + mix(vt[h], jnp.concatenate(weights, axis=0)) * b
        return part, (both, total, far_top, near_top)

    def keep(h, part, stats):
        if last:
            done[h] = result(part, stats[1])
        else:
            for a in range(rows // BLK):
                acc_ref[a, h] = part[:, a * BLK : (a + 1) * BLK]
            for n, row in enumerate(stats):
                stat_ref[n, pl.ds(h, 1), :] = row

    fill(0, query(0), scores_a, tops_a)

    def next_heads(n, carry):
        base = STRIDE * n
        members = [base + m for m in range(STRIDE)]
        queries = [query(h) for h in members[1:]] + [query(jnp.minimum(base + STRIDE, heads - 1))]
        before = [jnp.concatenate([acc_in[a, h] for a in range(rows // BLK)], axis=1) for h in members]
        stats = [[stat_in[n, pl.ds(h, 1), :] for n in range(STATS)] for h in members]
        kept = []
        for m, h in enumerate(members):
            slots = (scores_a, tops_a, scores_b, tops_b) if m % 2 == 0 else (scores_b, tops_b, scores_a, tops_a)
            fill(jnp.minimum(h + 1, heads - 1), queries[m], *slots[2:])
            kept.append(use(h, before[m], stats[m], *slots[:2]))
        for h, found in zip(members, kept):
            keep(h, *found)
        return carry

    lax.fori_loop(0, heads // STRIDE, next_heads, 0)
    if last:
        finish(done, order[...], out_ref)


def far(bys, me, table, qt, halves, acc, stat, last):
    heads, width = qt.shape[1:3]
    tokens = qt.shape[0] * BLK
    rows = min(TILE, tokens)
    keys = len(bys) * CAP * BLK
    parts = pl.BlockSpec((rows // BLK, heads, width, BLK), lambda i, *_: (i, 0, 0, 0))
    stats = pl.BlockSpec((STATS, heads, rows), lambda i, *_: (0, 0, i))
    whole = pl.BlockSpec(halves[0].shape, lambda i, *_: (0, 0))
    scratch = [
        pltpu.VMEM((2, heads, keys, width), jnp.bfloat16),
        pltpu.VMEM((heads, width, keys), jnp.bfloat16),
        pltpu.VMEM((keys, rows), jnp.float32),
        pltpu.VMEM((keys, rows), jnp.float32),
        pltpu.VMEM((keys // BLK, rows), jnp.float32),
        pltpu.VMEM((keys // BLK, rows), jnp.float32),
    ]
    if last:
        out_specs = pl.BlockSpec((rows * heads, width), lambda i, *_: (i, 0))
        out_shape = jax.ShapeDtypeStruct((tokens * heads, width), jnp.bfloat16)
        aliases = {}
        scratch += [pltpu.VMEM((TILE, TILE), jnp.bfloat16), pltpu.VMEM((heads, rows, width), jnp.bfloat16)]
    else:
        out_specs = [parts, stats]
        out_shape = [
            jax.ShapeDtypeStruct(acc.shape, acc.dtype),
            jax.ShapeDtypeStruct(stat.shape, stat.dtype),
        ]
        aliases = {3 + len(halves): 0, 4 + len(halves): 1}
    grid_spec = pltpu.PrefetchScalarGridSpec(
        num_scalar_prefetch=2,
        grid=(tokens // rows,),
        in_specs=[parts] + [whole] * len(halves) + [parts, stats],
        out_specs=out_specs,
        scratch_shapes=scratch,
    )
    return pl.pallas_call(
        functools.partial(far_kernel, bys, tokens // BLK, last),
        grid_spec=grid_spec,
        out_shape=out_shape,
        input_output_aliases=aliases,
        compiler_params=pltpu.CompilerParams(vmem_limit_bytes=VMEM_BYTES),
        cost_estimate=SMALL,
        name="far",
    )(me, table, qt, *halves, acc, stat)


def rim_kernel(
    me_ref, q_ref, edge_mine, edge_other, tip_mine, tip_other, acc_in, stat_in, acc_ref, stat_ref, both_t, vt
):
    heads = q_ref.shape[1]
    c = pl.program_id(0)

    @pl.when(c == 0)
    def _():
        turn = split_order(heads)
        take_halves(me_ref, edge_mine, edge_other, 0, turn, both_t, vt)
        take_halves(me_ref, tip_mine, tip_other, BLK, turn, both_t, vt)

    for first_block in range(WB - 1):

        @pl.when(c == first_block)
        def _(first_block=first_block):
            blocks = range(first_block, WB - 1)
            shut = [jnp.where(me_ref[0] > 0, 0.0, FLOOR)] * len(blocks)
            span = slice(first_block * BLK, RIM)
            kept = []
            for h in range(heads):
                found = mix(both_t[0, h, span, :], q_ref[0, h])
                near = [found[n * BLK : (n + 1) * BLK, :] for n in range(len(blocks))]
                near_top, w, near_total = softmax_blocks(near, shut, stat_in[3, h : h + 1, :])
                top = stat_in[0, h : h + 1, :]
                both = jnp.maximum(top, near_top)
                a = jnp.exp2(top - both)
                b = jnp.exp2(near_top - both)
                total = stat_in[1, h : h + 1, :] * a + near_total * b
                part = acc_in[0, h] * a + mix(vt[h, :, span], w) * b
                kept.append((part, both, total, stat_in[2, h : h + 1, :], near_top))
            for h, (part, *rows) in enumerate(kept):
                acc_ref[0, h] = part
                for n, row in enumerate(rows):
                    stat_ref[n, h : h + 1, :] = row


def rim(me, qt, halves, acc, stat):
    heads, width = qt.shape[1:3]
    parts = pl.BlockSpec((1, heads, width, BLK), lambda i, *_: (i, 0, 0, 0))
    stats = pl.BlockSpec((STATS, heads, BLK), lambda i, *_: (0, 0, i))
    grid_spec = pltpu.PrefetchScalarGridSpec(
        num_scalar_prefetch=1,
        grid=(WB - 1,),
        in_specs=[parts]
        + [pl.BlockSpec(half.shape, lambda i, *_: (0, 0)) for half in halves]
        + [parts, stats],
        out_specs=[parts, stats],
        scratch_shapes=[
            pltpu.VMEM((2, heads, RIM, width), jnp.bfloat16),
            pltpu.VMEM((heads, width, RIM), jnp.bfloat16),
        ],
    )
    return pl.pallas_call(
        rim_kernel,
        grid_spec=grid_spec,
        out_shape=[
            jax.ShapeDtypeStruct(acc.shape, acc.dtype),
            jax.ShapeDtypeStruct(stat.shape, stat.dtype),
        ],
        input_output_aliases={2 + len(halves): 0, 3 + len(halves): 1},
        compiler_params=pltpu.CompilerParams(vmem_limit_bytes=VMEM_BYTES),
        cost_estimate=SMALL,
        name="rim",
    )(me, qt, *halves, acc, stat)


def other_core(x):
    return lax.ppermute(x, "rep", [(0, 1), (1, 0)])


def ahead(x, by):
    count = lax.axis_size("ctx")
    return lax.ppermute(x, "ctx", [(i, i + by) for i in range(count - by)])


def local(queries, keys_values, far_list, far_count):
    tokens, heads, _, width = queries.shape
    spans = lax.axis_size("ctx")
    me = jnp.stack([lax.axis_index("ctx"), lax.axis_index("rep")]).astype(jnp.int32)
    q = queries.reshape(tokens * heads, width)
    kv = keys_values.reshape(tokens * heads, width)
    tip = kv[(tokens - (WB - 2) * BLK) * heads :]
    far_count, tip = lax.optimization_barrier((far_count, tip))
    tip = ahead(tip, 1)
    other = other_core(kv)
    table, *pools, edge = route(me, far_list, far_count, kv, spans)
    pieces = {by: ahead(pool, by) for by, pool in enumerate(pools, 1)}
    edge = ahead(edge, 1)
    qt, acc, stat = first(me, table, q, kv, other, heads, spans)
    late = min(2, spans - 1)
    bys = [by for by in pieces if by != late]
    tip, stat = lax.optimization_barrier((tip, stat))
    *early, edge, stat = lax.optimization_barrier((*[pieces[by] for by in bys], edge, stat))
    acc, stat = rim(me, qt, [edge, other_core(edge), tip, other_core(tip)], acc, stat)
    others = [other_core(piece) for piece in early]
    for n in range(0, len(bys), GROUP):
        halves = [half for pair in zip(early[n : n + GROUP], others[n : n + GROUP]) for half in pair]
        acc, stat = far(bys[n : n + GROUP], me, table, qt, halves, acc, stat, False)
    piece, stat = lax.optimization_barrier((pieces[late], stat))
    done = far([late], me, table, qt, [piece, other_core(piece)], acc, stat, True)
    return done.reshape(queries.shape)


def solution(mesh):
    in_specs = (
        P(("groups", "ctx"), "head", "rep", None),
        P("rep", ("groups", "ctx"), "head", None),
        P("groups", None),
        P("groups"),
    )
    out_specs = P(("groups", "ctx"), "head", "rep", None)
    return jax.shard_map(local, mesh=mesh, in_specs=in_specs, out_specs=out_specs, check_vma=False)
```

```python
import functools
import math

import jax
import jax.numpy as jnp
from jax import lax
from jax.experimental import pallas as pl
from jax.experimental.pallas import tpu as pltpu
from jax.sharding import PartitionSpec as P

BLK = 128
WB = 4
CAP = 2
RIM = (WB - 1) * BLK
TILE = 256
GROUP = 3
STATS = 4
STRIDE = 4

FLOOR = -1.0e30
SCALE = math.log2(math.e) / 12.0
NONE = 1.0e6
VMEM_BYTES = 48 * 1024 * 1024
SMALL = pl.CostEstimate(flops=1024, bytes_accessed=1024, transcendentals=0)


def contract_last(a, b):
    return lax.dot_general(a, b, (((1,), (1,)), ((), ())), preferred_element_type=jnp.float32)


def mix(a, b):
    return jnp.dot(a, b, preferred_element_type=jnp.float32)


def unit(n):
    row = lax.broadcasted_iota(jnp.int32, (n, n), 0)
    col = lax.broadcasted_iota(jnp.int32, (n, n), 1)
    return (row == col).astype(jnp.float32).astype(jnp.bfloat16)


def causal_bias():
    key = lax.broadcasted_iota(jnp.int32, (BLK, BLK), 0)
    query = lax.broadcasted_iota(jnp.int32, (BLK, BLK), 1)
    return jnp.where(key <= query, 0.0, FLOOR)


def softmax_blocks(scores, shut, top=None):
    for block, closed in zip(scores, shut):
        block_top = jnp.max(block, axis=0, keepdims=True) * SCALE
        block_top = block_top if closed is None else block_top + closed
        top = block_top if top is None else jnp.maximum(top, block_top)
    weights, total = [], 0.0
    for block, closed in zip(scores, shut):
        base = top if closed is None else jnp.where(closed < 0.0, -FLOOR, top)
        w = jnp.exp2(block * SCALE - base)
        total = total + jnp.sum(w, axis=0, keepdims=True)
        weights.append(w.astype(jnp.bfloat16))
    return top, jnp.concatenate(weights, axis=0), total


def near_scores(scores, causal):
    blocks = [scores[b * BLK : (b + 1) * BLK, :] for b in range(scores.shape[0] // BLK)]
    return blocks[:-1] + [blocks[-1] + causal]


def split_order(heads):
    step = TILE // heads
    row = lax.broadcasted_iota(jnp.int32, (TILE, TILE), 0)
    col = lax.broadcasted_iota(jnp.int32, (TILE, TILE), 1)
    source = (row & (step - 1)) * heads + (row >> (step.bit_length() - 1))
    return (col == source).astype(jnp.float32).astype(jnp.bfloat16)


def join_order(heads):
    step = TILE // heads
    row = lax.broadcasted_iota(jnp.int32, (TILE, TILE), 0)
    col = lax.broadcasted_iota(jnp.int32, (TILE, TILE), 1)
    source = (row & (heads - 1)) * step + (row >> (heads.bit_length() - 1))
    return (col == source).astype(jnp.float32).astype(jnp.bfloat16)


def chunk_pairs(rows, order):
    turned = []
    for i in range(0, rows.shape[0], 2 * TILE):
        two = jnp.concatenate([rows[i : i + TILE, :], rows[i + TILE : i + 2 * TILE, :]], axis=1)
        two = mix(order, two).astype(jnp.bfloat16)
        turned += [two[:, : rows.shape[1]], two[:, rows.shape[1] :]]
    return turned


def put_heads(turned, dst, base):
    heads = dst.shape[0]
    step = TILE // heads
    for i, rows in enumerate(turned):
        dst[:, pl.ds(base + i * step, step), :] = rows.reshape(heads, step, rows.shape[-1])


def route_kernel(me_ref, list_ref, count_ref, kv_ref, table_ref, *rest):
    spans = table_ref.shape[0] // (2 * CAP)
    pools, rim_out, sem = rest[:-2], rest[-2], rest[-1]
    edge = pltpu.make_async_copy(
        kv_ref.at[pl.ds(kv_ref.shape[0] - rim_out.shape[0] * (WB - 1), rim_out.shape[0]), :],
        rim_out,
        sem.at[sem.shape[0] - 1],
    )
    edge.start()
    me = me_ref[0]
    listed = list_ref[...]
    entries, total = listed.shape
    own = total // spans
    slot = lax.broadcasted_iota(jnp.int32, (entries, total), 0)
    lane = lax.broadcasted_iota(jnp.int32, (entries, total), 1)
    counted = slot < count_ref[...]
    named = jnp.where(counted, listed.astype(jnp.float32), 2.0 * NONE)

    def pick(user, source):
        low = (source * own).astype(jnp.float32)
        mine = (lane >= user * own) & (lane < (user + 1) * own)
        left = jnp.where(mine & (named >= low) & (named < low + own), named, NONE)
        picked = []
        for _ in range(CAP):
            least = jnp.min(jnp.min(left, axis=0, keepdims=True), axis=1, keepdims=True)
            picked.append(least)
            left = jnp.where(left == least, NONE, left)
        return picked

    row_len = kv_ref.shape[0] // own
    sent = [block for by in range(1, spans) for block in pick(me + by, me)]
    copies = []
    for n, block in enumerate(sent):
        local = block - (me * own).astype(jnp.float32)
        local = jnp.max(jnp.where(local < own, local, 0.0)).astype(jnp.int32)
        start = pl.multiple_of(local * row_len, row_len)
        copy = pltpu.make_async_copy(
            kv_ref.at[pl.ds(start, row_len), :],
            pools[n // CAP].at[pl.ds(n % CAP * row_len, row_len), :],
            sem.at[n],
        )
        copies.append(copy)
    for copy in copies:
        copy.start()
    for by in range(spans):
        source = me - by
        for j, block in enumerate(pick(me, source)):
            used = jnp.max((named == block).astype(jnp.float32), axis=0, keepdims=True)
            local = block - (source * own).astype(jnp.float32)
            local = jnp.where(local < own, local, 0.0)
            row = by * CAP + j
            table_ref[row : row + 1, :] = used.astype(jnp.int32)
            ids = jnp.zeros((1, total), jnp.float32) + local
            table_ref[spans * CAP + row : spans * CAP + row + 1, :] = ids.astype(jnp.int32)
    for copy in copies:
        copy.wait()
    edge.wait()


def route(me, far_list, far_count, kv, spans):
    total = far_list.shape[0]
    rows = kv.shape[0] // (total // spans) * CAP
    pool = jax.ShapeDtypeStruct((rows, kv.shape[1]), kv.dtype)
    edge = jax.ShapeDtypeStruct((rows // CAP, kv.shape[1]), kv.dtype)
    grid_spec = pltpu.PrefetchScalarGridSpec(
        num_scalar_prefetch=1,
        grid=(1,),
        in_specs=[
            pl.BlockSpec(far_list.shape[::-1], lambda i, *_: (0, 0)),
            pl.BlockSpec((1, total), lambda i, *_: (0, 0)),
            pl.BlockSpec(memory_space=pltpu.HBM),
        ],
        out_specs=[pl.BlockSpec((2 * CAP * spans, total), lambda i, *_: (0, 0))]
        + [pl.BlockSpec(pool.shape, lambda i, *_: (0, 0))] * (spans - 1)
        + [pl.BlockSpec(edge.shape, lambda i, *_: (0, 0))],
        scratch_shapes=[pltpu.SemaphoreType.DMA(((spans - 1) * CAP + 1,))],
    )
    return pl.pallas_call(
        route_kernel,
        grid_spec=grid_spec,
        out_shape=[jax.ShapeDtypeStruct((2 * CAP * spans, total), jnp.int32)] + [pool] * (spans - 1) + [edge],
        cost_estimate=SMALL,
        name="route",
    )(me, far_list.T, far_count[None, :], kv)


def first_kernel(
    spans, me_ref, table_ref, q_ref, mine_ref, other_ref, qt_ref, acc_ref, stat_ref, both_t, vt, qs, qf, order, eye, diag
):
    heads = qt_ref.shape[1]
    own = pl.num_programs(0)
    c = pl.program_id(0)

    @pl.when(c == 0)
    def _():
        order[...] = split_order(heads)
        eye[...] = unit(eye.shape[0])
        diag[...] = causal_bias()

    base = pl.multiple_of(c * BLK, BLK)
    turn = order[...]
    turned = [chunk_pairs(ref[...], turn) for ref in (q_ref, mine_ref, other_ref)]
    put_heads(turned[0], qs, 0)
    put_heads(turned[1], both_t.at[me_ref[1]], base)
    put_heads(turned[2], both_t.at[1 - me_ref[1]], base)
    kt = both_t.at[0]
    flipped = [contract_last(eye[...], both_t[1, h, pl.ds(base, BLK), :]).astype(jnp.bfloat16) for h in range(heads)]
    asked = [contract_last(eye[...], qs[h]).astype(jnp.bfloat16) for h in range(heads)]
    for h in range(heads):
        vt[h, :, pl.ds(base, BLK)] = flipped[h]
        qf[h] = asked[h]
        qt_ref[0, h] = asked[h]

    causal = diag[...]

    def attend(blocks, with_far):
        start = pl.multiple_of((c - (blocks - 1)) * BLK, BLK)
        here = me_ref[0] * own + c
        shut = [jnp.where(table_ref[j, here] > 0, 0.0, FLOOR) for j in range(CAP)]
        far_at = [pl.multiple_of(jnp.minimum(table_ref[spans * CAP + j, here], c) * BLK, BLK) for j in range(CAP)]
        for group in range(0, heads, STRIDE):
            found = []
            for h in range(group, group + STRIDE):
                q = qf[h]
                near = near_scores(mix(kt[h, pl.ds(start, blocks * BLK), :], q), causal)
                top, w, total = softmax_blocks(near, [None] * blocks)
                part = mix(vt[h, :, pl.ds(start, blocks * BLK)], w)
                if not with_far:
                    found.append((part, top, total, jnp.full_like(top, FLOOR), top))
                    continue
                far = [mix(kt[h, pl.ds(at, BLK), :], q) for at in far_at]
                far_top, far_w, far_total = softmax_blocks(far, shut)
                far_v = jnp.concatenate([vt[h, :, pl.ds(at, BLK)] for at in far_at], axis=1)
                far_part = mix(far_v, far_w)
                both = jnp.maximum(top, far_top)
                a = jnp.exp2(top - both)
                b = jnp.exp2(far_top - both)
                found.append((part * a + far_part * b, both, total * a + far_total * b, far_top, top))
            for h, (part, *rows) in enumerate(found, group):
                acc_ref[0, h] = part
                for n, row in enumerate(rows):
                    stat_ref[n, h : h + 1, :] = row

    for at in range(WB):
        pl.when(c == at)(functools.partial(attend, at + 1, False))
    pl.when(c >= WB)(functools.partial(attend, WB, True))


def first(me, table, q, mine, other, heads, spans):
    tokens = q.shape[0] // heads
    width = q.shape[1]
    own = tokens // BLK
    raw = pl.BlockSpec((BLK * heads, width), lambda c, *_: (c, 0))
    grid_spec = pltpu.PrefetchScalarGridSpec(
        num_scalar_prefetch=2,
        grid=(own,),
        in_specs=[raw, raw, raw],
        out_specs=[
            pl.BlockSpec((1, heads, width, BLK), lambda c, *_: (c, 0, 0, 0)),
            pl.BlockSpec((1, heads, width, BLK), lambda c, *_: (c, 0, 0, 0)),
            pl.BlockSpec((STATS, heads, BLK), lambda c, *_: (0, 0, c)),
        ],
        scratch_shapes=[
            pltpu.VMEM((2, heads, tokens, width), jnp.bfloat16),
            pltpu.VMEM((heads, width, tokens), jnp.bfloat16),
            pltpu.VMEM((heads, BLK, width), jnp.bfloat16),
            pltpu.VMEM((heads, width, BLK), jnp.bfloat16),
            pltpu.VMEM((TILE, TILE), jnp.bfloat16),
            pltpu.VMEM((width, width), jnp.bfloat16),
            pltpu.VMEM((BLK, BLK), jnp.float32),
        ],
    )
    return pl.pallas_call(
        functools.partial(first_kernel, spans),
        grid_spec=grid_spec,
        out_shape=[
            jax.ShapeDtypeStruct((own, heads, width, BLK), jnp.bfloat16),
            jax.ShapeDtypeStruct((own, heads, width, BLK), jnp.float32),
            jax.ShapeDtypeStruct((STATS, heads, tokens), jnp.float32),
        ],
        compiler_params=pltpu.CompilerParams(vmem_limit_bytes=VMEM_BYTES),
        cost_estimate=SMALL,
        name="first",
    )(me, table, q, mine, other)


def take_halves(me_ref, mine_ref, other_ref, base, turn, both_t, vt):
    heads, width = vt.shape[:2]
    turned = [chunk_pairs(ref[...], turn) for ref in (mine_ref, other_ref)]
    put_heads(turned[0], both_t.at[me_ref[1]], base)
    put_heads(turned[1], both_t.at[1 - me_ref[1]], base)
    eye = unit(width)
    span = slice(base, base + mine_ref.shape[0] // heads)
    flipped = [contract_last(eye, both_t[1, h, span, :]).astype(jnp.bfloat16) for h in range(heads)]
    for h in range(heads):
        vt[h, :, span] = flipped[h]


def finish(done, order, out_ref):
    heads, rows, _ = done.shape
    step = TILE // heads
    ordered = jnp.concatenate([done[h, i : i + step, :] for i in range(0, rows, step) for h in range(heads)], axis=0)
    for i, chunk in enumerate(chunk_pairs(ordered, order)):
        out_ref[i * TILE : (i + 1) * TILE, :] = chunk


def result(part, total):
    return jnp.transpose(part * (1.0 / total)).astype(jnp.bfloat16)


def far_kernel(bys, own, last, me_ref, table_ref, q_ref, *rest):
    halves, rest = rest[: 2 * len(bys)], rest[2 * len(bys) :]
    acc_in, stat_in, *rest = rest
    if last:
        out_ref, *rest = rest
    acc_ref, stat_ref, *rest = rest
    both_t, vt, scores_a, scores_b, tops_a, tops_b, *rest = rest
    if last:
        order, done = rest
    heads, rows = q_ref.shape[1], q_ref.shape[0] * BLK

    def query(h):
        return jnp.concatenate([q_ref[a, h] for a in range(rows // BLK)], axis=1)

    i = pl.program_id(0)

    @pl.when(i == 0)
    def _():
        turn = split_order(heads)
        for n in range(len(bys)):
            take_halves(me_ref, halves[2 * n], halves[2 * n + 1], n * CAP * BLK, turn, both_t, vt)
        if last:
            order[...] = join_order(heads)

    here = me_ref[0] * own + i * (rows // BLK)
    shut = []
    for by in bys:
        for j in range(CAP):
            row = [jnp.where(table_ref[by * CAP + j, here + a] > 0, 0.0, FLOOR) for a in range(rows // BLK)]
            shut.append(jnp.concatenate([jnp.full((1, BLK), closed, jnp.float32) for closed in row], axis=1))

    def fill(h, asked, scores, tops):
        found = mix(both_t[0, h], asked)
        for j in range(len(shut)):
            block = found[j * BLK : (j + 1) * BLK, :]
            tops[j : j + 1, :] = jnp.max(block, axis=0, keepdims=True)
            scores[j * BLK : (j + 1) * BLK, :] = block

    def use(h, before, stats, scores, tops):
        top, total, far_top, near_top = stats
        for j, closed in enumerate(shut):
            far_top = jnp.maximum(far_top, tops[j : j + 1, :] * SCALE + closed)
        weights, far_total = [], 0.0
        for j, closed in enumerate(shut):
            base = jnp.where(closed < 0.0, -FLOOR, far_top)
            w = jnp.exp2(scores[j * BLK : (j + 1) * BLK, :] * SCALE - base)
            far_total = far_total + jnp.sum(w, axis=0, keepdims=True)
            weights.append(w.astype(jnp.bfloat16))
        both = jnp.maximum(top, far_top)
        a = jnp.exp2(top - both)
        b = jnp.exp2(far_top - both)
        total = total * a + far_total * b
        part = before * a + mix(vt[h], jnp.concatenate(weights, axis=0)) * b
        return part, (both, total, far_top, near_top)

    def keep(h, part, stats):
        if last:
            done[h] = result(part, stats[1])

            @pl.when(i == 0)
            def _():
                acc_ref[0, h] = part[:, :BLK]
                for n, row in enumerate(stats):
                    stat_ref[n, pl.ds(h, 1), :] = row[:, :BLK]

        else:
            for a in range(rows // BLK):
                acc_ref[a, h] = part[:, a * BLK : (a + 1) * BLK]
            for n, row in enumerate(stats):
                stat_ref[n, pl.ds(h, 1), :] = row

    fill(0, query(0), scores_a, tops_a)

    def next_heads(n, carry):
        base = STRIDE * n
        members = [base + m for m in range(STRIDE)]
        queries = [query(h) for h in members[1:]] + [query(jnp.minimum(base + STRIDE, heads - 1))]
        before = [jnp.concatenate([acc_in[a, h] for a in range(rows // BLK)], axis=1) for h in members]
        stats = [[stat_in[n, pl.ds(h, 1), :] for n in range(STATS)] for h in members]
        kept = []
        for m, h in enumerate(members):
            slots = (scores_a, tops_a, scores_b, tops_b) if m % 2 == 0 else (scores_b, tops_b, scores_a, tops_a)
            fill(jnp.minimum(h + 1, heads - 1), queries[m], *slots[2:])
            kept.append(use(h, before[m], stats[m], *slots[:2]))
        for h, found in zip(members, kept):
            keep(h, *found)
        return carry

    lax.fori_loop(0, heads // STRIDE, next_heads, 0)
    if last:
        finish(done, order[...], out_ref)


def far(bys, me, table, qt, halves, acc, stat, last):
    heads, width = qt.shape[1:3]
    tokens = qt.shape[0] * BLK
    rows = min(TILE, tokens)
    keys = len(bys) * CAP * BLK
    parts = pl.BlockSpec((rows // BLK, heads, width, BLK), lambda i, *_: (i, 0, 0, 0))
    stats = pl.BlockSpec((STATS, heads, rows), lambda i, *_: (0, 0, i))
    whole = pl.BlockSpec(halves[0].shape, lambda i, *_: (0, 0))
    scratch = [
        pltpu.VMEM((2, heads, keys, width), jnp.bfloat16),
        pltpu.VMEM((heads, width, keys), jnp.bfloat16),
        pltpu.VMEM((keys, rows), jnp.float32),
        pltpu.VMEM((keys, rows), jnp.float32),
        pltpu.VMEM((keys // BLK, rows), jnp.float32),
        pltpu.VMEM((keys // BLK, rows), jnp.float32),
    ]
    if last:
        out_specs = [
            pl.BlockSpec((rows * heads, width), lambda i, *_: (i, 0)),
            pl.BlockSpec((1, heads, width, BLK), lambda i, *_: (0, 0, 0, 0)),
            pl.BlockSpec((STATS, heads, BLK), lambda i, *_: (0, 0, 0)),
        ]
        out_shape = [
            jax.ShapeDtypeStruct((tokens * heads, width), jnp.bfloat16),
            jax.ShapeDtypeStruct((1, heads, width, BLK), jnp.float32),
            jax.ShapeDtypeStruct((STATS, heads, BLK), jnp.float32),
        ]
        aliases = {}
        scratch += [pltpu.VMEM((TILE, TILE), jnp.bfloat16), pltpu.VMEM((heads, rows, width), jnp.bfloat16)]
    else:
        out_specs = [parts, stats]
        out_shape = [
            jax.ShapeDtypeStruct(acc.shape, acc.dtype),
            jax.ShapeDtypeStruct(stat.shape, stat.dtype),
        ]
        aliases = {3 + len(halves): 0, 4 + len(halves): 1}
    grid_spec = pltpu.PrefetchScalarGridSpec(
        num_scalar_prefetch=2,
        grid=(tokens // rows,),
        in_specs=[parts] + [whole] * len(halves) + [parts, stats],
        out_specs=out_specs,
        scratch_shapes=scratch,
    )
    return pl.pallas_call(
        functools.partial(far_kernel, bys, tokens // BLK, last),
        grid_spec=grid_spec,
        out_shape=out_shape,
        input_output_aliases=aliases,
        compiler_params=pltpu.CompilerParams(vmem_limit_bytes=VMEM_BYTES),
        cost_estimate=SMALL,
        name="far",
    )(me, table, qt, *halves, acc, stat)


def add_rim(h, found, values, shut, acc_in, stat_in):
    near = [found[n * BLK : (n + 1) * BLK, :] for n in range(found.shape[0] // BLK)]
    near_top, w, near_total = softmax_blocks(near, [shut] * len(near), stat_in[3, h : h + 1, :])
    top = stat_in[0, h : h + 1, :]
    both = jnp.maximum(top, near_top)
    a = jnp.exp2(top - both)
    b = jnp.exp2(near_top - both)
    total = stat_in[1, h : h + 1, :] * a + near_total * b
    part = acc_in[0, h] * a + mix(values, w) * b
    return part, both, total, stat_in[2, h : h + 1, :], near_top


def rim_kernel(me_ref, q_ref, mine_ref, other_ref, acc_in, stat_in, acc_ref, stat_ref, both_t, vt):
    heads = q_ref.shape[1]
    c = pl.program_id(0)

    @pl.when(c == 0)
    def _():
        take_halves(me_ref, mine_ref, other_ref, 0, split_order(heads), both_t, vt)

    def attend(first_block):
        shut = jnp.where(me_ref[0] > 0, 0.0, FLOOR)
        span = slice(first_block * BLK, both_t.shape[2])
        kept = []
        for h in range(heads):
            found = mix(both_t[0, h, span, :], q_ref[0, h])
            kept.append(add_rim(h, found, vt[h, :, span], shut, acc_in, stat_in))
        for h, (part, *rows) in enumerate(kept):
            acc_ref[0, h] = part
            for n, row in enumerate(rows):
                stat_ref[n, h : h + 1, :] = row

    for at in range(WB - 1):
        pl.when(c == at)(functools.partial(attend, max(at - 1, 0)))


def rim(me, qt, halves, acc, stat):
    heads, width = qt.shape[1:3]
    parts = pl.BlockSpec((1, heads, width, BLK), lambda i, *_: (i, 0, 0, 0))
    stats = pl.BlockSpec((STATS, heads, BLK), lambda i, *_: (0, 0, i))
    keys = (WB - 2) * BLK
    grid_spec = pltpu.PrefetchScalarGridSpec(
        num_scalar_prefetch=1,
        grid=(WB - 1,),
        in_specs=[parts] + [pl.BlockSpec(half.shape, lambda i, *_: (0, 0)) for half in halves] + [parts, stats],
        out_specs=[parts, stats],
        scratch_shapes=[
            pltpu.VMEM((2, heads, keys, width), jnp.bfloat16),
            pltpu.VMEM((heads, width, keys), jnp.bfloat16),
        ],
    )
    return pl.pallas_call(
        rim_kernel,
        grid_spec=grid_spec,
        out_shape=[
            jax.ShapeDtypeStruct(acc.shape, acc.dtype),
            jax.ShapeDtypeStruct(stat.shape, stat.dtype),
        ],
        input_output_aliases={2 + len(halves): 0, 3 + len(halves): 1},
        compiler_params=pltpu.CompilerParams(vmem_limit_bytes=VMEM_BYTES),
        cost_estimate=SMALL,
        name="rim",
    )(me, qt, *halves, acc, stat)


def edge_kernel(me_ref, q_ref, mine_ref, other_ref, acc_in, stat_in, out_in, out_ref, both_t, vt, done):
    heads = q_ref.shape[1]
    take_halves(me_ref, mine_ref, other_ref, 0, split_order(heads), both_t, vt)
    shut = jnp.where(me_ref[0] > 0, 0.0, FLOOR)
    kept = [add_rim(h, mix(both_t[0, h], q_ref[0, h]), vt[h], shut, acc_in, stat_in) for h in range(heads)]
    for h, (part, _, total, *_) in enumerate(kept):
        done[h] = result(part, total)
    finish(done, join_order(heads), out_ref)


def edge_last(me, qt, halves, acc, stat, out):
    heads, width = qt.shape[1:3]
    parts = pl.BlockSpec((1, heads, width, BLK), lambda i, *_: (0, 0, 0, 0))
    grid_spec = pltpu.PrefetchScalarGridSpec(
        num_scalar_prefetch=1,
        grid=(1,),
        in_specs=[parts]
        + [pl.BlockSpec(half.shape, lambda i, *_: (0, 0)) for half in halves]
        + [parts, pl.BlockSpec(stat.shape, lambda i, *_: (0, 0, 0)), pl.BlockSpec(memory_space=pl.ANY)],
        out_specs=pl.BlockSpec((BLK * heads, width), lambda i, *_: (0, 0)),
        scratch_shapes=[
            pltpu.VMEM((2, heads, BLK, width), jnp.bfloat16),
            pltpu.VMEM((heads, width, BLK), jnp.bfloat16),
            pltpu.VMEM((heads, BLK, width), jnp.bfloat16),
        ],
    )
    return pl.pallas_call(
        edge_kernel,
        grid_spec=grid_spec,
        out_shape=jax.ShapeDtypeStruct(out.shape, out.dtype),
        input_output_aliases={4 + len(halves): 0},
        compiler_params=pltpu.CompilerParams(vmem_limit_bytes=VMEM_BYTES),
        cost_estimate=SMALL,
        name="edge",
    )(me, qt, *halves, acc, stat, out)


def other_core(x):
    return lax.ppermute(x, "rep", [(0, 1), (1, 0)])


def ahead(x, by):
    count = lax.axis_size("ctx")
    return lax.ppermute(x, "ctx", [(i, i + by) for i in range(count - by)])


def local(queries, keys_values, far_list, far_count):
    tokens, heads, _, width = queries.shape
    spans = lax.axis_size("ctx")
    me = jnp.stack([lax.axis_index("ctx"), lax.axis_index("rep")]).astype(jnp.int32)
    q = queries.reshape(tokens * heads, width)
    kv = keys_values.reshape(tokens * heads, width)
    tip = kv[(tokens - (WB - 2) * BLK) * heads :]
    far_count, tip = lax.optimization_barrier((far_count, tip))
    tip = ahead(tip, 1)
    other = other_core(kv)
    table, *pools, edge = route(me, far_list, far_count, kv, spans)
    pieces = {by: ahead(pool, by) for by, pool in enumerate(pools, 1)}
    edge = ahead(edge, 1)
    qt, acc, stat = first(me, table, q, kv, other, heads, spans)
    late = min(2, spans - 1)
    bys = [by for by in pieces if by != late]
    tip, stat = lax.optimization_barrier((tip, stat))
    *early, stat = lax.optimization_barrier((*[pieces[by] for by in bys], stat))
    acc, stat = rim(me, qt, [tip, other_core(tip)], acc, stat)
    others = [other_core(piece) for piece in early]
    for n in range(0, len(bys), GROUP):
        halves = [half for pair in zip(early[n : n + GROUP], others[n : n + GROUP]) for half in pair]
        acc, stat = far(bys[n : n + GROUP], me, table, qt, halves, acc, stat, False)
    piece, stat = lax.optimization_barrier((pieces[late], stat))
    done, acc, stat = far([late], me, table, qt, [piece, other_core(piece)], acc, stat, True)
    edge, stat = lax.optimization_barrier((edge, stat))
    done = edge_last(me, qt, [edge, other_core(edge)], acc, stat, done)
    return done.reshape(queries.shape)


def solution(mesh):
    in_specs = (
        P(("groups", "ctx"), "head", "rep", None),
        P("rep", ("groups", "ctx"), "head", None),
        P("groups", None),
        P("groups"),
    )
    out_specs = P(("groups", "ctx"), "head", "rep", None)
    return jax.shard_map(local, mesh=mesh, in_specs=in_specs, out_specs=out_specs, check_vma=False)
```

```python
import functools
import math

import jax
import jax.numpy as jnp
from jax import lax
from jax.experimental import pallas as pl
from jax.experimental.pallas import tpu as pltpu
from jax.sharding import PartitionSpec as P

BLK = 128
WB = 4
CAP = 2
RIM = (WB - 1) * BLK
TILE = 256
GROUP = 3
STATS = 4
STRIDE = 4

FLOOR = -1.0e30
SCALE = math.log2(math.e) / 12.0
NONE = 1.0e6
VMEM_BYTES = 48 * 1024 * 1024
SMALL = pl.CostEstimate(flops=1024, bytes_accessed=1024, transcendentals=0)


def contract_last(a, b):
    return lax.dot_general(a, b, (((1,), (1,)), ((), ())), preferred_element_type=jnp.float32)


def mix(a, b):
    return jnp.dot(a, b, preferred_element_type=jnp.float32)


def unit(n):
    row = lax.broadcasted_iota(jnp.int32, (n, n), 0)
    col = lax.broadcasted_iota(jnp.int32, (n, n), 1)
    return (row == col).astype(jnp.float32).astype(jnp.bfloat16)


def causal_bias():
    key = lax.broadcasted_iota(jnp.int32, (BLK, BLK), 0)
    query = lax.broadcasted_iota(jnp.int32, (BLK, BLK), 1)
    return jnp.where(key <= query, 0.0, FLOOR)


def softmax_blocks(scores, shut, top=None):
    for block, closed in zip(scores, shut):
        block_top = jnp.max(block, axis=0, keepdims=True) * SCALE
        block_top = block_top if closed is None else block_top + closed
        top = block_top if top is None else jnp.maximum(top, block_top)
    weights, total = [], 0.0
    for block, closed in zip(scores, shut):
        base = top if closed is None else jnp.where(closed < 0.0, -FLOOR, top)
        w = jnp.exp2(block * SCALE - base)
        total = total + jnp.sum(w, axis=0, keepdims=True)
        weights.append(w.astype(jnp.bfloat16))
    return top, jnp.concatenate(weights, axis=0), total


def near_scores(scores, causal):
    blocks = [scores[b * BLK : (b + 1) * BLK, :] for b in range(scores.shape[0] // BLK)]
    return blocks[:-1] + [blocks[-1] + causal]


def split_order(heads):
    step = TILE // heads
    row = lax.broadcasted_iota(jnp.int32, (TILE, TILE), 0)
    col = lax.broadcasted_iota(jnp.int32, (TILE, TILE), 1)
    source = (row & (step - 1)) * heads + (row >> (step.bit_length() - 1))
    return (col == source).astype(jnp.float32).astype(jnp.bfloat16)


def chunk_pairs(rows, order):
    turned = []
    for i in range(0, rows.shape[0], 2 * TILE):
        two = jnp.concatenate([rows[i : i + TILE, :], rows[i + TILE : i + 2 * TILE, :]], axis=1)
        two = mix(order, two).astype(jnp.bfloat16)
        turned += [two[:, : rows.shape[1]], two[:, rows.shape[1] :]]
    return turned


def put_heads(turned, dst, base):
    heads = dst.shape[0]
    step = TILE // heads
    for i, rows in enumerate(turned):
        dst[:, pl.ds(base + i * step, step), :] = rows.reshape(heads, step, rows.shape[-1])


def route_kernel(me_ref, list_ref, count_ref, kv_ref, table_ref, *rest):
    spans = table_ref.shape[0] // (2 * CAP)
    pools, rim_out, sem = rest[:-2], rest[-2], rest[-1]
    edge = pltpu.make_async_copy(
        kv_ref.at[pl.ds(kv_ref.shape[0] - rim_out.shape[0] * (WB - 1), rim_out.shape[0]), :],
        rim_out,
        sem.at[sem.shape[0] - 1],
    )
    edge.start()
    me = me_ref[0]
    listed = list_ref[...]
    entries, total = listed.shape
    own = total // spans
    slot = lax.broadcasted_iota(jnp.int32, (entries, total), 0)
    lane = lax.broadcasted_iota(jnp.int32, (entries, total), 1)
    counted = slot < count_ref[...]
    named = jnp.where(counted, listed.astype(jnp.float32), 2.0 * NONE)

    def pick(user, source):
        low = (source * own).astype(jnp.float32)
        mine = (lane >= user * own) & (lane < (user + 1) * own)
        left = jnp.where(mine & (named >= low) & (named < low + own), named, NONE)
        picked = []
        for _ in range(CAP):
            least = jnp.min(jnp.min(left, axis=0, keepdims=True), axis=1, keepdims=True)
            picked.append(least)
            left = jnp.where(left == least, NONE, left)
        return picked

    row_len = kv_ref.shape[0] // own
    sent = [block for by in range(1, spans) for block in pick(me + by, me)]
    copies = []
    for n, block in enumerate(sent):
        local = block - (me * own).astype(jnp.float32)
        local = jnp.max(jnp.where(local < own, local, 0.0)).astype(jnp.int32)
        start = pl.multiple_of(local * row_len, row_len)
        copy = pltpu.make_async_copy(
            kv_ref.at[pl.ds(start, row_len), :],
            pools[n // CAP].at[pl.ds(n % CAP * row_len, row_len), :],
            sem.at[n],
        )
        copies.append(copy)
    for copy in copies:
        copy.start()
    for by in range(spans):
        source = me - by
        for j, block in enumerate(pick(me, source)):
            used = jnp.max((named == block).astype(jnp.float32), axis=0, keepdims=True)
            local = block - (source * own).astype(jnp.float32)
            local = jnp.where(local < own, local, 0.0)
            row = by * CAP + j
            table_ref[row : row + 1, :] = used.astype(jnp.int32)
            ids = jnp.zeros((1, total), jnp.float32) + local
            table_ref[spans * CAP + row : spans * CAP + row + 1, :] = ids.astype(jnp.int32)
    for copy in copies:
        copy.wait()
    edge.wait()


def route(me, far_list, far_count, kv, spans):
    total = far_list.shape[0]
    rows = kv.shape[0] // (total // spans) * CAP
    pool = jax.ShapeDtypeStruct((rows, kv.shape[1]), kv.dtype)
    edge = jax.ShapeDtypeStruct((rows // CAP, kv.shape[1]), kv.dtype)
    grid_spec = pltpu.PrefetchScalarGridSpec(
        num_scalar_prefetch=1,
        grid=(1,),
        in_specs=[
            pl.BlockSpec(far_list.shape[::-1], lambda i, *_: (0, 0)),
            pl.BlockSpec((1, total), lambda i, *_: (0, 0)),
            pl.BlockSpec(memory_space=pltpu.HBM),
        ],
        out_specs=[pl.BlockSpec((2 * CAP * spans, total), lambda i, *_: (0, 0))]
        + [pl.BlockSpec(pool.shape, lambda i, *_: (0, 0))] * (spans - 1)
        + [pl.BlockSpec(edge.shape, lambda i, *_: (0, 0))],
        scratch_shapes=[pltpu.SemaphoreType.DMA(((spans - 1) * CAP + 1,))],
    )
    return pl.pallas_call(
        route_kernel,
        grid_spec=grid_spec,
        out_shape=[jax.ShapeDtypeStruct((2 * CAP * spans, total), jnp.int32)] + [pool] * (spans - 1) + [edge],
        cost_estimate=SMALL,
        name="route",
    )(me, far_list.T, far_count[None, :], kv)


def first_kernel(
    spans, me_ref, table_ref, q_ref, mine_ref, other_ref, qt_ref, acc_ref, stat_ref, both_t, vt, qs, qf, order, eye, diag
):
    heads = qt_ref.shape[1]
    own = pl.num_programs(0)
    c = pl.program_id(0)

    @pl.when(c == 0)
    def _():
        order[...] = split_order(heads)
        eye[...] = unit(eye.shape[0])
        diag[...] = causal_bias()

    base = pl.multiple_of(c * BLK, BLK)
    turn = order[...]
    turned = [chunk_pairs(ref[...], turn) for ref in (q_ref, mine_ref, other_ref)]
    put_heads(turned[0], qs, 0)
    put_heads(turned[1], both_t.at[me_ref[1]], base)
    put_heads(turned[2], both_t.at[1 - me_ref[1]], base)
    kt = both_t.at[0]
    flipped = [contract_last(eye[...], both_t[1, h, pl.ds(base, BLK), :]).astype(jnp.bfloat16) for h in range(heads)]
    asked = [contract_last(eye[...], qs[h]).astype(jnp.bfloat16) for h in range(heads)]
    for h in range(heads):
        vt[h, :, pl.ds(base, BLK)] = flipped[h]
        qf[h] = asked[h]
        qt_ref[0, h] = asked[h]

    causal = diag[...]

    def attend(blocks, with_far):
        start = pl.multiple_of((c - (blocks - 1)) * BLK, BLK)
        here = me_ref[0] * own + c
        shut = [jnp.where(table_ref[j, here] > 0, 0.0, FLOOR) for j in range(CAP)]
        far_at = [pl.multiple_of(jnp.minimum(table_ref[spans * CAP + j, here], c) * BLK, BLK) for j in range(CAP)]
        for group in range(0, heads, STRIDE):
            found = []
            for h in range(group, group + STRIDE):
                q = qf[h]
                near = near_scores(mix(kt[h, pl.ds(start, blocks * BLK), :], q), causal)
                top, w, total = softmax_blocks(near, [None] * blocks)
                part = mix(vt[h, :, pl.ds(start, blocks * BLK)], w)
                if not with_far:
                    found.append((part, top, total, jnp.full_like(top, FLOOR), top))
                    continue
                far = [mix(kt[h, pl.ds(at, BLK), :], q) for at in far_at]
                far_top, far_w, far_total = softmax_blocks(far, shut)
                far_v = jnp.concatenate([vt[h, :, pl.ds(at, BLK)] for at in far_at], axis=1)
                far_part = mix(far_v, far_w)
                both = jnp.maximum(top, far_top)
                a = jnp.exp2(top - both)
                b = jnp.exp2(far_top - both)
                found.append((part * a + far_part * b, both, total * a + far_total * b, far_top, top))
            for h, (part, *rows) in enumerate(found, group):
                acc_ref[0, h] = part
                for n, row in enumerate(rows):
                    stat_ref[n, h : h + 1, :] = row

    for at in range(WB):
        pl.when(c == at)(functools.partial(attend, at + 1, False))
    pl.when(c >= WB)(functools.partial(attend, WB, True))


def first(me, table, q, mine, other, heads, spans):
    tokens = q.shape[0] // heads
    width = q.shape[1]
    own = tokens // BLK
    raw = pl.BlockSpec((BLK * heads, width), lambda c, *_: (c, 0))
    grid_spec = pltpu.PrefetchScalarGridSpec(
        num_scalar_prefetch=2,
        grid=(own,),
        in_specs=[raw, raw, raw],
        out_specs=[
            pl.BlockSpec((1, heads, width, BLK), lambda c, *_: (c, 0, 0, 0)),
            pl.BlockSpec((1, heads, width, BLK), lambda c, *_: (c, 0, 0, 0)),
            pl.BlockSpec((STATS, heads, BLK), lambda c, *_: (0, 0, c)),
        ],
        scratch_shapes=[
            pltpu.VMEM((2, heads, tokens, width), jnp.bfloat16),
            pltpu.VMEM((heads, width, tokens), jnp.bfloat16),
            pltpu.VMEM((heads, BLK, width), jnp.bfloat16),
            pltpu.VMEM((heads, width, BLK), jnp.bfloat16),
            pltpu.VMEM((TILE, TILE), jnp.bfloat16),
            pltpu.VMEM((width, width), jnp.bfloat16),
            pltpu.VMEM((BLK, BLK), jnp.float32),
        ],
    )
    return pl.pallas_call(
        functools.partial(first_kernel, spans),
        grid_spec=grid_spec,
        out_shape=[
            jax.ShapeDtypeStruct((own, heads, width, BLK), jnp.bfloat16),
            jax.ShapeDtypeStruct((own, heads, width, BLK), jnp.float32),
            jax.ShapeDtypeStruct((STATS, heads, tokens), jnp.float32),
        ],
        compiler_params=pltpu.CompilerParams(vmem_limit_bytes=VMEM_BYTES),
        cost_estimate=SMALL,
        name="first",
    )(me, table, q, mine, other)


def take_halves(me_ref, mine_ref, other_ref, base, wide, both_t, vt):
    heads, width = vt.shape[:2]
    rows = mine_ref.shape[0]
    span = slice(base, base + rows // heads)
    for half, ref in ((me_ref[1], mine_ref), (1 - me_ref[1], other_ref)):
        wide[:rows, :] = ref[...].astype(jnp.float32)
        split = [wide[pl.ds(h, rows // heads, stride=heads), :].astype(jnp.bfloat16) for h in range(heads)]
        for h in range(heads):
            both_t[half, h, span, :] = split[h]
    eye = unit(width)
    flipped = [contract_last(eye, both_t[1, h, span, :]).astype(jnp.bfloat16) for h in range(heads)]
    for h in range(heads):
        vt[h, :, span] = flipped[h]


def far_kernel(bys, own, last, me_ref, table_ref, q_ref, *rest):
    halves, rest = rest[: 2 * len(bys)], rest[2 * len(bys) :]
    acc_in, stat_in, *rest = rest
    if last:
        out_ref, *rest = rest
    else:
        acc_ref, stat_ref, *rest = rest
    both_t, vt, scores_a, scores_b, tops_a, tops_b, wide = rest
    heads, rows = q_ref.shape[1], q_ref.shape[0] * BLK

    def query(h):
        return jnp.concatenate([q_ref[a, h] for a in range(rows // BLK)], axis=1)

    i = pl.program_id(0)

    @pl.when(i == 0)
    def _():
        for n in range(len(bys)):
            take_halves(me_ref, halves[2 * n], halves[2 * n + 1], n * CAP * BLK, wide, both_t, vt)

    here = me_ref[0] * own + i * (rows // BLK)
    shut = []
    for by in bys:
        for j in range(CAP):
            row = [jnp.where(table_ref[by * CAP + j, here + a] > 0, 0.0, FLOOR) for a in range(rows // BLK)]
            shut.append(jnp.concatenate([jnp.full((1, BLK), closed, jnp.float32) for closed in row], axis=1))

    def fill(h, asked, scores, tops):
        found = mix(both_t[0, h], asked)
        for j in range(len(shut)):
            block = found[j * BLK : (j + 1) * BLK, :]
            tops[j : j + 1, :] = jnp.max(block, axis=0, keepdims=True)
            scores[j * BLK : (j + 1) * BLK, :] = block

    def use(h, before, stats, scores, tops):
        top, total, far_top, near_top = stats
        for j, closed in enumerate(shut):
            far_top = jnp.maximum(far_top, tops[j : j + 1, :] * SCALE + closed)
        weights, far_total = [], 0.0
        for j, closed in enumerate(shut):
            base = jnp.where(closed < 0.0, -FLOOR, far_top)
            w = jnp.exp2(scores[j * BLK : (j + 1) * BLK, :] * SCALE - base)
            far_total = far_total + jnp.sum(w, axis=0, keepdims=True)
            weights.append(w.astype(jnp.bfloat16))
        both = jnp.maximum(top, far_top)
        a = jnp.exp2(top - both)
        b = jnp.exp2(far_top - both)
        total = total * a + far_total * b
        part = before * a + mix(vt[h], jnp.concatenate(weights, axis=0)) * b
        return part, (both, total, far_top, near_top)

    def keep(h, part, stats):
        if last:
            wide[pl.ds(h, rows, stride=heads), :] = jnp.transpose(part * (1.0 / stats[1]))
        else:
            for a in range(rows // BLK):
                acc_ref[a, h] = part[:, a * BLK : (a + 1) * BLK]
            for n, row in enumerate(stats):
                stat_ref[n, pl.ds(h, 1), :] = row

    fill(0, query(0), scores_a, tops_a)

    def next_heads(n, carry):
        base = STRIDE * n
        members = [base + m for m in range(STRIDE)]
        queries = [query(h) for h in members[1:]] + [query(jnp.minimum(base + STRIDE, heads - 1))]
        before = [jnp.concatenate([acc_in[a, h] for a in range(rows // BLK)], axis=1) for h in members]
        stats = [[stat_in[n, pl.ds(h, 1), :] for n in range(STATS)] for h in members]
        kept = []
        for m, h in enumerate(members):
            slots = (scores_a, tops_a, scores_b, tops_b) if m % 2 == 0 else (scores_b, tops_b, scores_a, tops_a)
            fill(jnp.minimum(h + 1, heads - 1), queries[m], *slots[2:])
            kept.append(use(h, before[m], stats[m], *slots[:2]))
        for h, found in zip(members, kept):
            keep(h, *found)
        return carry

    lax.fori_loop(0, heads // STRIDE, next_heads, 0)
    if last:
        out_ref[...] = wide[: rows * heads, :].astype(jnp.bfloat16)


def far(bys, me, table, qt, halves, acc, stat, last):
    heads, width = qt.shape[1:3]
    tokens = qt.shape[0] * BLK
    rows = min(TILE, tokens)
    keys = len(bys) * CAP * BLK
    parts = pl.BlockSpec((rows // BLK, heads, width, BLK), lambda i, *_: (i, 0, 0, 0))
    stats = pl.BlockSpec((STATS, heads, rows), lambda i, *_: (0, 0, i))
    whole = pl.BlockSpec(halves[0].shape, lambda i, *_: (0, 0))
    scratch = [
        pltpu.VMEM((2, heads, keys, width), jnp.bfloat16),
        pltpu.VMEM((heads, width, keys), jnp.bfloat16),
        pltpu.VMEM((keys, rows), jnp.float32),
        pltpu.VMEM((keys, rows), jnp.float32),
        pltpu.VMEM((keys // BLK, rows), jnp.float32),
        pltpu.VMEM((keys // BLK, rows), jnp.float32),
        pltpu.VMEM((max(CAP * BLK, rows) * heads, width), jnp.float32),
    ]
    if last:
        out_specs = pl.BlockSpec((rows * heads, width), lambda i, *_: (i, 0))
        out_shape = jax.ShapeDtypeStruct((tokens * heads, width), jnp.bfloat16)
        aliases = {}
    else:
        out_specs = [parts, stats]
        out_shape = [
            jax.ShapeDtypeStruct(acc.shape, acc.dtype),
            jax.ShapeDtypeStruct(stat.shape, stat.dtype),
        ]
        aliases = {3 + len(halves): 0, 4 + len(halves): 1}
    grid_spec = pltpu.PrefetchScalarGridSpec(
        num_scalar_prefetch=2,
        grid=(tokens // rows,),
        in_specs=[parts] + [whole] * len(halves) + [parts, stats],
        out_specs=out_specs,
        scratch_shapes=scratch,
    )
    return pl.pallas_call(
        functools.partial(far_kernel, bys, tokens // BLK, last),
        grid_spec=grid_spec,
        out_shape=out_shape,
        input_output_aliases=aliases,
        compiler_params=pltpu.CompilerParams(vmem_limit_bytes=VMEM_BYTES),
        cost_estimate=SMALL,
        name="far",
    )(me, table, qt, *halves, acc, stat)


def rim_kernel(
    me_ref, q_ref, edge_mine, edge_other, tip_mine, tip_other, acc_in, stat_in, acc_ref, stat_ref, both_t, vt, wide
):
    heads = q_ref.shape[1]
    c = pl.program_id(0)

    @pl.when(c == 0)
    def _():
        take_halves(me_ref, edge_mine, edge_other, 0, wide, both_t, vt)
        take_halves(me_ref, tip_mine, tip_other, BLK, wide, both_t, vt)

    for first_block in range(WB - 1):

        @pl.when(c == first_block)
        def _(first_block=first_block):
            blocks = range(first_block, WB - 1)
            shut = [jnp.where(me_ref[0] > 0, 0.0, FLOOR)] * len(blocks)
            span = slice(first_block * BLK, RIM)
            kept = []
            for h in range(heads):
                found = mix(both_t[0, h, span, :], q_ref[0, h])
                near = [found[n * BLK : (n + 1) * BLK, :] for n in range(len(blocks))]
                near_top, w, near_total = softmax_blocks(near, shut, stat_in[3, h : h + 1, :])
                top = stat_in[0, h : h + 1, :]
                both = jnp.maximum(top, near_top)
                a = jnp.exp2(top - both)
                b = jnp.exp2(near_top - both)
                total = stat_in[1, h : h + 1, :] * a + near_total * b
                part = acc_in[0, h] * a + mix(vt[h, :, span], w) * b
                kept.append((part, both, total, stat_in[2, h : h + 1, :], near_top))
            for h, (part, *rows) in enumerate(kept):
                acc_ref[0, h] = part
                for n, row in enumerate(rows):
                    stat_ref[n, h : h + 1, :] = row


def rim(me, qt, halves, acc, stat):
    heads, width = qt.shape[1:3]
    parts = pl.BlockSpec((1, heads, width, BLK), lambda i, *_: (i, 0, 0, 0))
    stats = pl.BlockSpec((STATS, heads, BLK), lambda i, *_: (0, 0, i))
    grid_spec = pltpu.PrefetchScalarGridSpec(
        num_scalar_prefetch=1,
        grid=(WB - 1,),
        in_specs=[parts]
        + [pl.BlockSpec(half.shape, lambda i, *_: (0, 0)) for half in halves]
        + [parts, stats],
        out_specs=[parts, stats],
        scratch_shapes=[
            pltpu.VMEM((2, heads, RIM, width), jnp.bfloat16),
            pltpu.VMEM((heads, width, RIM), jnp.bfloat16),
            pltpu.VMEM(((WB - 2) * BLK * heads, width), jnp.float32),
        ],
    )
    return pl.pallas_call(
        rim_kernel,
        grid_spec=grid_spec,
        out_shape=[
            jax.ShapeDtypeStruct(acc.shape, acc.dtype),
            jax.ShapeDtypeStruct(stat.shape, stat.dtype),
        ],
        input_output_aliases={2 + len(halves): 0, 3 + len(halves): 1},
        compiler_params=pltpu.CompilerParams(vmem_limit_bytes=VMEM_BYTES),
        cost_estimate=SMALL,
        name="rim",
    )(me, qt, *halves, acc, stat)


def other_core(x):
    return lax.ppermute(x, "rep", [(0, 1), (1, 0)])


def ahead(x, by):
    count = lax.axis_size("ctx")
    return lax.ppermute(x, "ctx", [(i, i + by) for i in range(count - by)])


def local(queries, keys_values, far_list, far_count):
    tokens, heads, _, width = queries.shape
    spans = lax.axis_size("ctx")
    me = jnp.stack([lax.axis_index("ctx"), lax.axis_index("rep")]).astype(jnp.int32)
    q = queries.reshape(tokens * heads, width)
    kv = keys_values.reshape(tokens * heads, width)
    tip = kv[(tokens - (WB - 2) * BLK) * heads :]
    far_count, tip = lax.optimization_barrier((far_count, tip))
    tip = ahead(tip, 1)
    other = other_core(kv)
    table, *pools, edge = route(me, far_list, far_count, kv, spans)
    pieces = {by: ahead(pool, by) for by, pool in enumerate(pools, 1)}
    edge = ahead(edge, 1)
    qt, acc, stat = first(me, table, q, kv, other, heads, spans)
    late = min(2, spans - 1)
    bys = [by for by in pieces if by != late]
    tip, stat = lax.optimization_barrier((tip, stat))
    *early, edge, stat = lax.optimization_barrier((*[pieces[by] for by in bys], edge, stat))
    acc, stat = rim(me, qt, [edge, other_core(edge), tip, other_core(tip)], acc, stat)
    others = [other_core(piece) for piece in early]
    for n in range(0, len(bys), GROUP):
        halves = [half for pair in zip(early[n : n + GROUP], others[n : n + GROUP]) for half in pair]
        acc, stat = far(bys[n : n + GROUP], me, table, qt, halves, acc, stat, False)
    piece, stat = lax.optimization_barrier((pieces[late], stat))
    done = far([late], me, table, qt, [piece, other_core(piece)], acc, stat, True)
    return done.reshape(queries.shape)


def solution(mesh):
    in_specs = (
        P(("groups", "ctx"), "head", "rep", None),
        P("rep", ("groups", "ctx"), "head", None),
        P("groups", None),
        P("groups"),
    )
    out_specs = P(("groups", "ctx"), "head", "rep", None)
    return jax.shard_map(local, mesh=mesh, in_specs=in_specs, out_specs=out_specs, check_vma=False)
```

```python
import functools
import math

import jax
import jax.numpy as jnp
from jax import lax
from jax.experimental import pallas as pl
from jax.experimental.pallas import tpu as pltpu
from jax.sharding import PartitionSpec as P

BLK = 128
WB = 4
CAP = 2
RIM = (WB - 1) * BLK
TILE = 256
GROUP = 3
STATS = 4
STRIDE = 4

FLOOR = -1.0e30
SCALE = math.log2(math.e) / 12.0
NONE = 1.0e6
VMEM_BYTES = 48 * 1024 * 1024
SMALL = pl.CostEstimate(flops=1024, bytes_accessed=1024, transcendentals=0)


def contract_last(a, b):
    return lax.dot_general(a, b, (((1,), (1,)), ((), ())), preferred_element_type=jnp.float32)


def mix(a, b):
    return jnp.dot(a, b, preferred_element_type=jnp.float32)


def unit(n):
    row = lax.broadcasted_iota(jnp.int32, (n, n), 0)
    col = lax.broadcasted_iota(jnp.int32, (n, n), 1)
    return (row == col).astype(jnp.float32).astype(jnp.bfloat16)


def causal_bias():
    key = lax.broadcasted_iota(jnp.int32, (BLK, BLK), 0)
    query = lax.broadcasted_iota(jnp.int32, (BLK, BLK), 1)
    return jnp.where(key <= query, 0.0, FLOOR)


def softmax_blocks(scores, shut, top=None):
    for block, closed in zip(scores, shut):
        block_top = jnp.max(block, axis=0, keepdims=True) * SCALE
        block_top = block_top if closed is None else block_top + closed
        top = block_top if top is None else jnp.maximum(top, block_top)
    weights, total = [], 0.0
    for block, closed in zip(scores, shut):
        base = top if closed is None else jnp.where(closed < 0.0, -FLOOR, top)
        w = jnp.exp2(block * SCALE - base)
        total = total + jnp.sum(w, axis=0, keepdims=True)
        weights.append(w.astype(jnp.bfloat16))
    return top, jnp.concatenate(weights, axis=0), total


def near_scores(scores, causal):
    blocks = [scores[b * BLK : (b + 1) * BLK, :] for b in range(scores.shape[0] // BLK)]
    return blocks[:-1] + [blocks[-1] + causal]


def split_order(heads):
    step = TILE // heads
    row = lax.broadcasted_iota(jnp.int32, (TILE, TILE), 0)
    col = lax.broadcasted_iota(jnp.int32, (TILE, TILE), 1)
    source = (row & (step - 1)) * heads + (row >> (step.bit_length() - 1))
    return (col == source).astype(jnp.float32).astype(jnp.bfloat16)


def chunk_pairs(rows, order):
    turned = []
    for i in range(0, rows.shape[0], 2 * TILE):
        two = jnp.concatenate([rows[i : i + TILE, :], rows[i + TILE : i + 2 * TILE, :]], axis=1)
        two = mix(order, two).astype(jnp.bfloat16)
        turned += [two[:, : rows.shape[1]], two[:, rows.shape[1] :]]
    return turned


def put_heads(turned, dst, base):
    heads = dst.shape[0]
    step = TILE // heads
    for i, rows in enumerate(turned):
        dst[:, pl.ds(base + i * step, step), :] = rows.reshape(heads, step, rows.shape[-1])


def route_kernel(me_ref, list_ref, count_ref, kv_ref, table_ref, *rest):
    spans = table_ref.shape[0] // (2 * CAP)
    pools, rim_out, sem = rest[:-2], rest[-2], rest[-1]
    edge = pltpu.make_async_copy(
        kv_ref.at[pl.ds(kv_ref.shape[0] - rim_out.shape[0] * (WB - 1), rim_out.shape[0]), :],
        rim_out,
        sem.at[sem.shape[0] - 1],
    )
    edge.start()
    me = me_ref[0]
    listed = list_ref[...]
    entries, total = listed.shape
    own = total // spans
    slot = lax.broadcasted_iota(jnp.int32, (entries, total), 0)
    lane = lax.broadcasted_iota(jnp.int32, (entries, total), 1)
    counted = slot < count_ref[...]
    named = jnp.where(counted, listed.astype(jnp.float32), 2.0 * NONE)

    def pick(user, source):
        low = (source * own).astype(jnp.float32)
        mine = (lane >= user * own) & (lane < (user + 1) * own)
        left = jnp.where(mine & (named >= low) & (named < low + own), named, NONE)
        picked = []
        for _ in range(CAP):
            least = jnp.min(jnp.min(left, axis=0, keepdims=True), axis=1, keepdims=True)
            picked.append(least)
            left = jnp.where(left == least, NONE, left)
        return picked

    row_len = kv_ref.shape[0] // own
    sent = [block for by in range(1, spans) for block in pick(me + by, me)]
    copies = []
    for n, block in enumerate(sent):
        local = block - (me * own).astype(jnp.float32)
        local = jnp.max(jnp.where(local < own, local, 0.0)).astype(jnp.int32)
        start = pl.multiple_of(local * row_len, row_len)
        copy = pltpu.make_async_copy(
            kv_ref.at[pl.ds(start, row_len), :],
            pools[n // CAP].at[pl.ds(n % CAP * row_len, row_len), :],
            sem.at[n],
        )
        copies.append(copy)
    for copy in copies:
        copy.start()
    for by in range(spans):
        source = me - by
        for j, block in enumerate(pick(me, source)):
            used = jnp.max((named == block).astype(jnp.float32), axis=0, keepdims=True)
            local = block - (source * own).astype(jnp.float32)
            local = jnp.where(local < own, local, 0.0)
            row = by * CAP + j
            table_ref[row : row + 1, :] = used.astype(jnp.int32)
            ids = jnp.zeros((1, total), jnp.float32) + local
            table_ref[spans * CAP + row : spans * CAP + row + 1, :] = ids.astype(jnp.int32)
    for copy in copies:
        copy.wait()
    edge.wait()


def route(me, far_list, far_count, kv, spans):
    total = far_list.shape[0]
    rows = kv.shape[0] // (total // spans) * CAP
    pool = jax.ShapeDtypeStruct((rows, kv.shape[1]), kv.dtype)
    edge = jax.ShapeDtypeStruct((rows // CAP, kv.shape[1]), kv.dtype)
    grid_spec = pltpu.PrefetchScalarGridSpec(
        num_scalar_prefetch=1,
        grid=(1,),
        in_specs=[
            pl.BlockSpec(far_list.shape[::-1], lambda i, *_: (0, 0)),
            pl.BlockSpec((1, total), lambda i, *_: (0, 0)),
            pl.BlockSpec(memory_space=pltpu.HBM),
        ],
        out_specs=[pl.BlockSpec((2 * CAP * spans, total), lambda i, *_: (0, 0))]
        + [pl.BlockSpec(pool.shape, lambda i, *_: (0, 0))] * (spans - 1)
        + [pl.BlockSpec(edge.shape, lambda i, *_: (0, 0))],
        scratch_shapes=[pltpu.SemaphoreType.DMA(((spans - 1) * CAP + 1,))],
    )
    return pl.pallas_call(
        route_kernel,
        grid_spec=grid_spec,
        out_shape=[jax.ShapeDtypeStruct((2 * CAP * spans, total), jnp.int32)] + [pool] * (spans - 1) + [edge],
        cost_estimate=SMALL,
        name="route",
    )(me, far_list.T, far_count[None, :], kv)


def first_kernel(
    spans, me_ref, table_ref, q_ref, mine_ref, other_ref, qt_ref, acc_ref, stat_ref, both_t, vt, qs, qf, order, eye, diag
):
    heads = qt_ref.shape[1]
    own = pl.num_programs(0)
    c = pl.program_id(0)

    @pl.when(c == 0)
    def _():
        order[...] = split_order(heads)
        eye[...] = unit(eye.shape[0])
        diag[...] = causal_bias()

    base = pl.multiple_of(c * BLK, BLK)
    turn = order[...]
    turned = [chunk_pairs(ref[...], turn) for ref in (q_ref, mine_ref, other_ref)]
    put_heads(turned[0], qs, 0)
    put_heads(turned[1], both_t.at[me_ref[1]], base)
    put_heads(turned[2], both_t.at[1 - me_ref[1]], base)
    kt = both_t.at[0]
    flipped = [contract_last(eye[...], both_t[1, h, pl.ds(base, BLK), :]).astype(jnp.bfloat16) for h in range(heads)]
    asked = [contract_last(eye[...], qs[h]).astype(jnp.bfloat16) for h in range(heads)]
    for h in range(heads):
        vt[h, :, pl.ds(base, BLK)] = flipped[h]
        qf[h] = asked[h]
        qt_ref[0, h] = asked[h]

    causal = diag[...]

    def attend(blocks, with_far):
        start = pl.multiple_of((c - (blocks - 1)) * BLK, BLK)
        here = me_ref[0] * own + c
        shut = [jnp.where(table_ref[j, here] > 0, 0.0, FLOOR) for j in range(CAP)]
        far_at = [pl.multiple_of(jnp.minimum(table_ref[spans * CAP + j, here], c) * BLK, BLK) for j in range(CAP)]
        for group in range(0, heads, STRIDE):
            found = []
            for h in range(group, group + STRIDE):
                q = qf[h]
                near = near_scores(mix(kt[h, pl.ds(start, blocks * BLK), :], q), causal)
                top, w, total = softmax_blocks(near, [None] * blocks)
                part = mix(vt[h, :, pl.ds(start, blocks * BLK)], w)
                if not with_far:
                    found.append((part, top, total, jnp.full_like(top, FLOOR), top))
                    continue
                far = [mix(kt[h, pl.ds(at, BLK), :], q) for at in far_at]
                far_top, far_w, far_total = softmax_blocks(far, shut)
                far_v = jnp.concatenate([vt[h, :, pl.ds(at, BLK)] for at in far_at], axis=1)
                far_part = mix(far_v, far_w)
                both = jnp.maximum(top, far_top)
                a = jnp.exp2(top - both)
                b = jnp.exp2(far_top - both)
                found.append((part * a + far_part * b, both, total * a + far_total * b, far_top, top))
            for h, (part, *rows) in enumerate(found, group):
                acc_ref[0, h] = part
                for n, row in enumerate(rows):
                    stat_ref[n, h : h + 1, :] = row

    for at in range(WB):
        pl.when(c == at)(functools.partial(attend, at + 1, False))
    pl.when(c >= WB)(functools.partial(attend, WB, True))


def first(me, table, q, mine, other, heads, spans):
    tokens = q.shape[0] // heads
    width = q.shape[1]
    own = tokens // BLK
    raw = pl.BlockSpec((BLK * heads, width), lambda c, *_: (c, 0))
    grid_spec = pltpu.PrefetchScalarGridSpec(
        num_scalar_prefetch=2,
        grid=(own,),
        in_specs=[raw, raw, raw],
        out_specs=[
            pl.BlockSpec((1, heads, width, BLK), lambda c, *_: (c, 0, 0, 0)),
            pl.BlockSpec((1, heads, width, BLK), lambda c, *_: (c, 0, 0, 0)),
            pl.BlockSpec((STATS, heads, BLK), lambda c, *_: (0, 0, c)),
        ],
        scratch_shapes=[
            pltpu.VMEM((2, heads, tokens, width), jnp.bfloat16),
            pltpu.VMEM((heads, width, tokens), jnp.bfloat16),
            pltpu.VMEM((heads, BLK, width), jnp.bfloat16),
            pltpu.VMEM((heads, width, BLK), jnp.bfloat16),
            pltpu.VMEM((TILE, TILE), jnp.bfloat16),
            pltpu.VMEM((width, width), jnp.bfloat16),
            pltpu.VMEM((BLK, BLK), jnp.float32),
        ],
    )
    return pl.pallas_call(
        functools.partial(first_kernel, spans),
        grid_spec=grid_spec,
        out_shape=[
            jax.ShapeDtypeStruct((own, heads, width, BLK), jnp.bfloat16),
            jax.ShapeDtypeStruct((own, heads, width, BLK), jnp.float32),
            jax.ShapeDtypeStruct((STATS, heads, tokens), jnp.float32),
        ],
        compiler_params=pltpu.CompilerParams(vmem_limit_bytes=VMEM_BYTES),
        cost_estimate=SMALL,
        name="first",
    )(me, table, q, mine, other)


def take_halves(me_ref, mine_ref, other_ref, base, wide, both_t, vt):
    heads, width = vt.shape[:2]
    rows = mine_ref.shape[0]
    span = slice(base, base + rows // heads)
    for half, ref in ((me_ref[1], mine_ref), (1 - me_ref[1], other_ref)):
        wide[:rows, :] = ref[...].astype(jnp.float32)
        split = [wide[pl.ds(h, rows // heads, stride=heads), :].astype(jnp.bfloat16) for h in range(heads)]
        for h in range(heads):
            both_t[half, h, span, :] = split[h]
    eye = unit(width)
    flipped = [contract_last(eye, both_t[1, h, span, :]).astype(jnp.bfloat16) for h in range(heads)]
    for h in range(heads):
        vt[h, :, span] = flipped[h]


def far_kernel(bys, own, last, me_ref, table_ref, q_ref, *rest):
    halves, rest = rest[: 2 * len(bys)], rest[2 * len(bys) :]
    acc_in, stat_in, *rest = rest
    if last:
        out_ref, *rest = rest
    else:
        acc_ref, stat_ref, *rest = rest
    both_t, vt, scores_a, scores_b, tops_a, tops_b, wide = rest
    heads, rows = q_ref.shape[1], q_ref.shape[0] * BLK

    def query(h):
        return jnp.concatenate([q_ref[a, h] for a in range(rows // BLK)], axis=1)

    i = pl.program_id(0)

    @pl.when(i == 0)
    def _():
        for n in range(len(bys)):
            take_halves(me_ref, halves[2 * n], halves[2 * n + 1], n * CAP * BLK, wide, both_t, vt)

    here = me_ref[0] * own + i * (rows // BLK)
    shut = []
    for by in bys:
        for j in range(CAP):
            row = [jnp.where(table_ref[by * CAP + j, here + a] > 0, 0.0, FLOOR) for a in range(rows // BLK)]
            shut.append(jnp.concatenate([jnp.full((1, BLK), closed, jnp.float32) for closed in row], axis=1))

    def fill(h, asked, scores, tops):
        found = mix(both_t[0, h], asked)
        for j in range(len(shut)):
            block = found[j * BLK : (j + 1) * BLK, :]
            tops[j : j + 1, :] = jnp.max(block, axis=0, keepdims=True)
            scores[j * BLK : (j + 1) * BLK, :] = block

    def use(h, before, stats, scores, tops):
        top, total, far_top, near_top = stats
        for j, closed in enumerate(shut):
            far_top = jnp.maximum(far_top, tops[j : j + 1, :] * SCALE + closed)
        weights, far_total = [], 0.0
        for j, closed in enumerate(shut):
            base = jnp.where(closed < 0.0, -FLOOR, far_top)
            w = jnp.exp2(scores[j * BLK : (j + 1) * BLK, :] * SCALE - base)
            far_total = far_total + jnp.sum(w, axis=0, keepdims=True)
            weights.append(w.astype(jnp.bfloat16))
        both = jnp.maximum(top, far_top)
        a = jnp.exp2(top - both)
        b = jnp.exp2(far_top - both)
        total = total * a + far_total * b
        part = before * a + mix(vt[h], jnp.concatenate(weights, axis=0)) * b
        return part, (both, total, far_top, near_top)

    def keep(h, part, stats):
        if last:
            wide[pl.ds(h, rows, stride=heads), :] = jnp.transpose(part * (1.0 / stats[1]))
        else:
            for a in range(rows // BLK):
                acc_ref[a, h] = part[:, a * BLK : (a + 1) * BLK]
            for n, row in enumerate(stats):
                stat_ref[n, pl.ds(h, 1), :] = row

    members = range(heads)
    queries = [query(h) for h in members]
    before = [jnp.concatenate([acc_in[a, h] for a in range(rows // BLK)], axis=1) for h in members]
    stats = [[stat_in[n, h : h + 1, :] for n in range(STATS)] for h in members]
    slots = (scores_a, tops_a), (scores_b, tops_b)
    fill(0, queries[0], *slots[0])
    kept = []
    for h in members:
        if h + 1 < heads:
            fill(h + 1, queries[h + 1], *slots[(h + 1) % 2])
        kept.append(use(h, before[h], stats[h], *slots[h % 2]))
    for h, found in zip(members, kept):
        keep(h, *found)
    if last:
        out_ref[...] = wide[: rows * heads, :].astype(jnp.bfloat16)


def far(bys, me, table, qt, halves, acc, stat, last):
    heads, width = qt.shape[1:3]
    tokens = qt.shape[0] * BLK
    rows = min(TILE, tokens)
    keys = len(bys) * CAP * BLK
    parts = pl.BlockSpec((rows // BLK, heads, width, BLK), lambda i, *_: (i, 0, 0, 0))
    stats = pl.BlockSpec((STATS, heads, rows), lambda i, *_: (0, 0, i))
    whole = pl.BlockSpec(halves[0].shape, lambda i, *_: (0, 0))
    scratch = [
        pltpu.VMEM((2, heads, keys, width), jnp.bfloat16),
        pltpu.VMEM((heads, width, keys), jnp.bfloat16),
        pltpu.VMEM((keys, rows), jnp.float32),
        pltpu.VMEM((keys, rows), jnp.float32),
        pltpu.VMEM((keys // BLK, rows), jnp.float32),
        pltpu.VMEM((keys // BLK, rows), jnp.float32),
        pltpu.VMEM((max(CAP * BLK, rows) * heads, width), jnp.float32),
    ]
    if last:
        out_specs = pl.BlockSpec((rows * heads, width), lambda i, *_: (i, 0))
        out_shape = jax.ShapeDtypeStruct((tokens * heads, width), jnp.bfloat16)
        aliases = {}
    else:
        out_specs = [parts, stats]
        out_shape = [
            jax.ShapeDtypeStruct(acc.shape, acc.dtype),
            jax.ShapeDtypeStruct(stat.shape, stat.dtype),
        ]
        aliases = {3 + len(halves): 0, 4 + len(halves): 1}
    grid_spec = pltpu.PrefetchScalarGridSpec(
        num_scalar_prefetch=2,
        grid=(tokens // rows,),
        in_specs=[parts] + [whole] * len(halves) + [parts, stats],
        out_specs=out_specs,
        scratch_shapes=scratch,
    )
    return pl.pallas_call(
        functools.partial(far_kernel, bys, tokens // BLK, last),
        grid_spec=grid_spec,
        out_shape=out_shape,
        input_output_aliases=aliases,
        compiler_params=pltpu.CompilerParams(vmem_limit_bytes=VMEM_BYTES),
        cost_estimate=SMALL,
        name="far",
    )(me, table, qt, *halves, acc, stat)


def rim_kernel(
    me_ref, q_ref, edge_mine, edge_other, tip_mine, tip_other, acc_in, stat_in, acc_ref, stat_ref, both_t, vt, wide
):
    heads = q_ref.shape[1]
    c = pl.program_id(0)

    @pl.when(c == 0)
    def _():
        take_halves(me_ref, edge_mine, edge_other, 0, wide, both_t, vt)
        take_halves(me_ref, tip_mine, tip_other, BLK, wide, both_t, vt)

    for first_block in range(WB - 1):

        @pl.when(c == first_block)
        def _(first_block=first_block):
            blocks = range(first_block, WB - 1)
            shut = [jnp.where(me_ref[0] > 0, 0.0, FLOOR)] * len(blocks)
            span = slice(first_block * BLK, RIM)
            kept = []
            for h in range(heads):
                found = mix(both_t[0, h, span, :], q_ref[0, h])
                near = [found[n * BLK : (n + 1) * BLK, :] for n in range(len(blocks))]
                near_top, w, near_total = softmax_blocks(near, shut, stat_in[3, h : h + 1, :])
                top = stat_in[0, h : h + 1, :]
                both = jnp.maximum(top, near_top)
                a = jnp.exp2(top - both)
                b = jnp.exp2(near_top - both)
                total = stat_in[1, h : h + 1, :] * a + near_total * b
                part = acc_in[0, h] * a + mix(vt[h, :, span], w) * b
                kept.append((part, both, total, stat_in[2, h : h + 1, :], near_top))
            for h, (part, *rows) in enumerate(kept):
                acc_ref[0, h] = part
                for n, row in enumerate(rows):
                    stat_ref[n, h : h + 1, :] = row


def rim(me, qt, halves, acc, stat):
    heads, width = qt.shape[1:3]
    parts = pl.BlockSpec((1, heads, width, BLK), lambda i, *_: (i, 0, 0, 0))
    stats = pl.BlockSpec((STATS, heads, BLK), lambda i, *_: (0, 0, i))
    grid_spec = pltpu.PrefetchScalarGridSpec(
        num_scalar_prefetch=1,
        grid=(WB - 1,),
        in_specs=[parts]
        + [pl.BlockSpec(half.shape, lambda i, *_: (0, 0)) for half in halves]
        + [parts, stats],
        out_specs=[parts, stats],
        scratch_shapes=[
            pltpu.VMEM((2, heads, RIM, width), jnp.bfloat16),
            pltpu.VMEM((heads, width, RIM), jnp.bfloat16),
            pltpu.VMEM(((WB - 2) * BLK * heads, width), jnp.float32),
        ],
    )
    return pl.pallas_call(
        rim_kernel,
        grid_spec=grid_spec,
        out_shape=[
            jax.ShapeDtypeStruct(acc.shape, acc.dtype),
            jax.ShapeDtypeStruct(stat.shape, stat.dtype),
        ],
        input_output_aliases={2 + len(halves): 0, 3 + len(halves): 1},
        compiler_params=pltpu.CompilerParams(vmem_limit_bytes=VMEM_BYTES),
        cost_estimate=SMALL,
        name="rim",
    )(me, qt, *halves, acc, stat)


def other_core(x):
    return lax.ppermute(x, "rep", [(0, 1), (1, 0)])


def ahead(x, by):
    count = lax.axis_size("ctx")
    return lax.ppermute(x, "ctx", [(i, i + by) for i in range(count - by)])


def local(queries, keys_values, far_list, far_count):
    tokens, heads, _, width = queries.shape
    spans = lax.axis_size("ctx")
    me = jnp.stack([lax.axis_index("ctx"), lax.axis_index("rep")]).astype(jnp.int32)
    q = queries.reshape(tokens * heads, width)
    kv = keys_values.reshape(tokens * heads, width)
    tip = kv[(tokens - (WB - 2) * BLK) * heads :]
    far_count, tip = lax.optimization_barrier((far_count, tip))
    tip = ahead(tip, 1)
    other = other_core(kv)
    table, *pools, edge = route(me, far_list, far_count, kv, spans)
    pieces = {by: ahead(pool, by) for by, pool in enumerate(pools, 1)}
    edge = ahead(edge, 1)
    qt, acc, stat = first(me, table, q, kv, other, heads, spans)
    late = min(2, spans - 1)
    bys = [by for by in pieces if by != late]
    tip, stat = lax.optimization_barrier((tip, stat))
    *early, edge, stat = lax.optimization_barrier((*[pieces[by] for by in bys], edge, stat))
    acc, stat = rim(me, qt, [edge, other_core(edge), tip, other_core(tip)], acc, stat)
    others = [other_core(piece) for piece in early]
    for n in range(0, len(bys), GROUP):
        halves = [half for pair in zip(early[n : n + GROUP], others[n : n + GROUP]) for half in pair]
        acc, stat = far(bys[n : n + GROUP], me, table, qt, halves, acc, stat, False)
    piece, stat = lax.optimization_barrier((pieces[late], stat))
    done = far([late], me, table, qt, [piece, other_core(piece)], acc, stat, True)
    return done.reshape(queries.shape)


def solution(mesh):
    in_specs = (
        P(("groups", "ctx"), "head", "rep", None),
        P("rep", ("groups", "ctx"), "head", None),
        P("groups", None),
        P("groups"),
    )
    out_specs = P(("groups", "ctx"), "head", "rep", None)
    return jax.shard_map(local, mesh=mesh, in_specs=in_specs, out_specs=out_specs, check_vma=False)
```
